32 devices in a mesh: dp: 8 (over z, core), seq: 4 (over y, x).
Axes of the slice: x: 2, y: 2, z: 4, core: 2. Of those that a mesh axis runs over, the one named last changes fastest.
Arguments:
- inputs: bfloat16 [8, 1024, 4096], P('dp', 'seq'), may hold values from -10 to 10
- weights: bfloat16 [4096, 768], P('dp'), may hold values from -0.09375 to 0.09375
- cotangent: bfloat16 [8, 1024, 512], P('dp', 'seq'), may hold values from -6 to 6
- doc_lengths: int32 [8, 8], P('dp'), may hold values from 1 to 512, 1024 in all within a row
- kept_flags: int32 [8, 8], P('dp'), may hold values 0 or 1
Outputs:
- attention: bfloat16 [8, 1024, 512], P('dp', 'seq')
- inputs_grad: bfloat16 [8, 1024, 4096], P('dp', 'seq')
- weights_grad: float32 [4096, 768], P(('dp', 'seq'))
The draws below stay inside these ranges and needn't reach their ends.
All inputs are finite; a program needn't handle non-finite values. No bound on the sum of `kept_flags` on one device may be relied on, other than what follows from the above.
Results may differ from the reference program's by a relative error of at most 0.013.
Values may be sent and summed in bfloat16 or wider, within the bound.
No kernel may reach another device: no remote copies, remote signals or barrier semaphores. Data moves between devices by JAX's collectives and lax.ppermute only.
A program may use at most 128 MiB of HBM per device.

```python
import math
import jax
import jax.numpy as jnp
import numpy as np
from jax import lax

D = 4096
HEAD_DIM = 128
NDOC = 8
HEADS = 4
COLS = 768
SEQ = 1024
PACKS = 8


def draw_inputs(key, part):
    values = jax.random.normal(key, (PACKS, SEQ, D), jnp.float32)
    values = jnp.clip(values, -5.0, 5.0)
    return values.astype(jnp.bfloat16)


def plant(entries, stream_key, smallest, top_value):
    shape = entries.shape
    spot = [jax.random.randint(jax.random.fold_in(stream_key, axis), (), 0, shape[axis]) for axis in range(len(shape))]
    entries = entries.at[tuple(spot)].set(smallest)
    longest = shape.index(max(shape))
    spot[longest] = (spot[longest] + 1) % shape[longest]
    return entries.at[tuple(spot)].set(top_value)


def steps_of(own_key, extent, pieces, least, largest):
    gain = 1.0
    for position, parts in pieces:
        steps = jax.random.uniform(jax.random.fold_in(jax.random.fold_in(own_key, 6), position), (parts,), jnp.float32, least / len(pieces), largest / len(pieces))
        gain = gain * jnp.repeat(jnp.exp(steps), extent[position] // parts).reshape((-1,) + (1,) * (len(extent) - 1 - position))
    return gain


def length_profile(count, total, most, slope):
    weights = [(1 << 20) // math.isqrt(standing ** slope) + 1 for standing in range(2, count + 1)]
    rest, counts = total - most - (count - 1), [1] * (count - 1)
    while rest > 0:
        candidates = [i for i in range(count - 1) if counts[i] < most]
        pool, left = sum([weights[i] for i in candidates]), rest
        for i in candidates:
            extra = min(most - counts[i], max(1, left * weights[i] // pool), rest)
            counts[i] = counts[i] + extra
            rest = rest - extra
    return np.array([most] + counts)


def ragged_sizes(own_key, count, total, bound, lean):
    if count == 2:
        one = jax.random.randint(own_key, (), max(1, total - bound), min(bound, total - 1) + 1)
        return jnp.stack([one, total - one])
    sizes = jnp.asarray(length_profile(count, total, bound, lean), jnp.int32)
    couples = (count - 1) // 2
    giver, sink = sizes[1:1 + 2 * couples:2], sizes[2:2 + 2 * couples:2]
    room = jnp.minimum(giver - 1, bound - sink)
    moved = jax.random.randint(jax.random.fold_in(own_key, 1), (couples,), 0, 1 << 20) % (room + 1)
    sizes = sizes.at[1:1 + 2 * couples:2].set(giver - moved).at[2:2 + 2 * couples:2].set(sink + moved)
    return sizes[jax.random.permutation(jax.random.fold_in(own_key, 2), count)]


def scatter_about(own_key, shape, deviation, limit, cuts=(), kind=jnp.bfloat16):
    drawn = deviation * jax.random.normal(own_key, shape, jnp.float32)
    if cuts:
        drawn = drawn * steps_of(own_key, shape, cuts, -0.22, 0.18)
    return jnp.clip(drawn, -limit, limit).astype(kind)


def setup_inputs(seed: int = 0) -> dict:
    key_of = jax.random.split(jax.random.key(seed), 6)
    return {
        "inputs": draw_inputs(jax.random.fold_in(key_of[5], 71), 0),
        "weights": scatter_about(key_of[1], (D, COLS), D ** -0.5, 0.09375, ((0, 8),)),
        "cotangent": scatter_about(key_of[2], (PACKS, SEQ, HEADS * HEAD_DIM), 1.0, 6.0, ((0, 8), (1, 4))),
        "doc_lengths": jax.vmap(lambda own: ragged_sizes(own, NDOC, SEQ, SEQ // 2, 2))(jax.random.split(key_of[3], PACKS)).reshape((PACKS, NDOC)).astype(jnp.int32),
        "kept_flags": plant((jax.random.randint(key_of[4], (PACKS, NDOC), 0, 4) < 3).astype(jnp.int32), jax.random.fold_in(key_of[4], 1), 0, 1),
    }


def doc_tables(doc_row, flag_row, positions):
    doc_ends = jnp.cumsum(doc_row).astype(jnp.int32)
    doc_starts = (doc_ends - doc_row).astype(jnp.int32)
    inside = (positions[:, None] >= doc_starts[None, :]) & (positions[:, None] < doc_ends[None, :])
    start_of = lax.optimization_barrier(jnp.sum(jnp.where(inside, doc_starts[None, :], 0), axis=1)).astype(jnp.int32)
    keep_of = lax.optimization_barrier(jnp.sum(jnp.where(inside, flag_row[None, :], 0), axis=1)).astype(jnp.int32)
    return (start_of, keep_of)

def reference(inputs, weights, cotangent, doc_lengths, kept_flags):
    qwidth = HEADS * HEAD_DIM
    softmax_scale = 1.0 / math.sqrt(HEAD_DIM)
    positions = jnp.arange(SEQ, dtype=jnp.int32)

    def one_pack(grad_total, packed):
        tokens, cot_rows, doc_row, flag_row = packed
        start_of, keep_of = doc_tables(doc_row, flag_row, positions)
        projected = jnp.dot(tokens, weights, preferred_element_type=jnp.float32).astype(jnp.bfloat16)
        queries = projected[:, :qwidth].reshape(SEQ, HEADS, HEAD_DIM).transpose(1, 0, 2)
        keys = projected[:, qwidth:qwidth + HEAD_DIM]
        values = projected[:, qwidth + HEAD_DIM:]
        cot_kept = jnp.where(keep_of[:, None] > 0, cot_rows, jnp.zeros_like(cot_rows))
        cot_heads = cot_kept.reshape(SEQ, HEADS, HEAD_DIM).transpose(1, 0, 2)
        allowed = (positions[None, :] >= start_of[:, None]) & (positions[None, :] <= positions[:, None])

        def one_head(pair):
            query_rows, cot_head = pair
            logits = lax.dot_general(query_rows, keys, (((1,), (1,)), ((), ())), preferred_element_type=jnp.float32) * softmax_scale
            logits = jnp.where(allowed, logits, -jnp.inf)
            attn_weights = jax.nn.softmax(logits, axis=1)
            weights_half = attn_weights.astype(jnp.bfloat16)
            out_head = jnp.dot(weights_half, values, preferred_element_type=jnp.float32).astype(jnp.bfloat16)
            weight_grads = lax.dot_general(cot_head, values, (((1,), (1,)), ((), ())), preferred_element_type=jnp.float32)
            row_delta = lax.optimization_barrier(jnp.sum(cot_head.astype(jnp.float32) * out_head.astype(jnp.float32), axis=1))
            score_grads = (attn_weights * (weight_grads - row_delta[:, None])).astype(jnp.bfloat16)
            query_grad = (jnp.dot(score_grads, keys, preferred_element_type=jnp.float32) * softmax_scale).astype(jnp.bfloat16)
            key_grad = lax.dot_general(score_grads, query_rows, (((0,), (0,)), ((), ())), preferred_element_type=jnp.float32) * softmax_scale
            value_grad = lax.dot_general(weights_half, cot_head, (((0,), (0,)), ((), ())), preferred_element_type=jnp.float32)
            return (out_head, query_grad, key_grad, value_grad)
        out_heads, query_grads, key_grads, value_grads = lax.map(one_head, (queries, cot_heads))
        attention = out_heads.transpose(1, 0, 2).reshape(SEQ, qwidth)
        query_part = query_grads.transpose(1, 0, 2).reshape(SEQ, qwidth)
        key_part = lax.optimization_barrier(jnp.sum(key_grads, axis=0)).astype(jnp.bfloat16)
        value_part = lax.optimization_barrier(jnp.sum(value_grads, axis=0)).astype(jnp.bfloat16)
        dprojected = jnp.concatenate([query_part, key_part, value_part], axis=1)
        inputs_grad = lax.dot_general(dprojected, weights, (((1,), (1,)), ((), ())), preferred_element_type=jnp.float32).astype(jnp.bfloat16)
        grad_total = grad_total + lax.dot_general(tokens, dprojected, (((0,), (0,)), ((), ())), preferred_element_type=jnp.float32)
        return (grad_total, (attention, inputs_grad))
    start_grad = jnp.zeros((D, COLS), jnp.float32)
    weights_grad, outputs = lax.scan(one_pack, start_grad, (inputs, cotangent, doc_lengths, kept_flags))
    return (outputs[0], outputs[1], weights_grad)
```

```python
import functools
import math

import jax
import jax.numpy as jnp
from jax import lax
from jax.experimental import pallas as pl
from jax.experimental.pallas import tpu as pltpu
from jax.sharding import PartitionSpec as P

HEAD_DIM = 128
PAIR = 2
CORES = 2
BF16 = jnp.bfloat16
F32 = jnp.float32
NT = (((1,), (1,)), ((), ()))
TN = (((0,), (0,)), ((), ()))
VMEM = pl.BlockSpec(memory_space=pltpu.VMEM)
SMEM = pl.BlockSpec(memory_space=pltpu.SMEM)


def dot(a, b, dims=(((1,), (0,)), ((), ()))):
    return lax.dot_general(a, b, dims, preferred_element_type=F32)


def swap_x(array):
    count = lax.axis_size("seq")
    return lax.ppermute(array, "seq", [(i, i ^ 1) for i in range(count)])


def shift_rest(array, step):
    count = lax.axis_size("seq")
    rest = count // PAIR
    pairs = [(i, PAIR * ((i // PAIR + step) % rest) + i % PAIR) for i in range(count)]
    return lax.ppermute(array, "seq", pairs)


def swap_core(array):
    count = lax.axis_size("dp")
    return lax.ppermute(array, "dp", [(i, i ^ 1) for i in range(count)])


def shift_chip(array, step):
    count = lax.axis_size("dp")
    chips = count // CORES
    pairs = [(i, CORES * ((i // CORES + step) % chips) + i % CORES) for i in range(count)]
    return lax.ppermute(array, "dp", pairs)


def shift_seq(array, step):
    count = lax.axis_size("seq")
    pairs = [(i, i + step) for i in range(count) if 0 <= i + step < count]
    return lax.ppermute(array, "seq", pairs)


def block_order(chips, rest, x):
    dp_index = lax.axis_index("dp")
    chip, core = dp_index // CORES, dp_index % CORES
    place = lax.axis_index("seq") // PAIR
    order = []
    for k in range(chips):
        for c in range(CORES):
            for j in range(rest):
                shard = CORES * ((chip - k + chips) % chips) + (core ^ c)
                order.append(shard * (PAIR * rest) + PAIR * ((place - j + rest) % rest) + x)
    return jnp.stack(order).astype(jnp.int32)


def copy_block(order_ref, in_ref, out_ref):
    out_ref[...] = in_ref[...]


def pick_blocks(tokens, order, width):
    rows, total = tokens.shape
    count = order.shape[0]
    if width % 128:
        blocks = tokens.reshape(rows, total // width, width)
        return jnp.take(blocks, order, axis=1).reshape(rows, count * width)
    return pl.pallas_call(
        copy_block,
        grid_spec=pltpu.PrefetchScalarGridSpec(
            num_scalar_prefetch=1,
            grid=(count,),
            in_specs=[pl.BlockSpec((rows, width), lambda i, order: (0, order[i]))],
            out_specs=pl.BlockSpec((rows, width), lambda i, order: (0, i)),
        ),
        out_shape=jax.ShapeDtypeStruct((rows, count * width), tokens.dtype),
        name="pick_blocks",
    )(order, tokens)


def place_block(half, where_ref, mine_ref, other_ref, out_ref):
    source = where_ref[pl.program_id(0)]

    @pl.when(source < half)
    def _():
        out_ref[...] = mine_ref[...]

    @pl.when(source >= half)
    def _():
        out_ref[...] = other_ref[...]


def place_blocks(mine, other, where, width):
    rows, total = mine.shape
    half = total // width
    if width % 128:
        blocks = jnp.concatenate([mine, other], axis=1).reshape(rows, 2 * half, width)
        return jnp.take(blocks, where, axis=1).reshape(rows, 2 * total)
    return pl.pallas_call(
        functools.partial(place_block, half),
        grid_spec=pltpu.PrefetchScalarGridSpec(
            num_scalar_prefetch=1,
            grid=(2 * half,),
            in_specs=[
                pl.BlockSpec((rows, width), lambda i, where: (0, jnp.minimum(where[i], half - 1))),
                pl.BlockSpec((rows, width), lambda i, where: (0, jnp.maximum(where[i] - half, 0))),
            ],
            out_specs=pl.BlockSpec((rows, width), lambda i, where: (0, i)),
        ),
        out_shape=jax.ShapeDtypeStruct((rows, 2 * total), mine.dtype),
        name="place_blocks",
    )(where, mine, other)


def attend_kernel(
    heads, back, place_ref, docs_ref, q_ref, cot_ref, *refs
):
    pair_refs, (out_ref, dq_ref, dpair_ref, dback_ref) = refs[: back + 1], refs[back + 1 :]
    rows = q_ref.shape[0]
    hd = HEAD_DIM
    scale = 1.0 / math.sqrt(hd)
    first = place_ref[0] * rows
    base = first - back * rows
    total = (back + 1) * rows

    row_pos = first + lax.broadcasted_iota(jnp.int32, (1, rows), 1)
    start_of = jnp.zeros((1, rows), jnp.int32)
    start = jnp.int32(0)
    for d in range(docs_ref.shape[0]):
        end = start + docs_ref[d]
        start_of = jnp.where((row_pos >= start) & (row_pos < end), start, start_of)
        start = end
    key_pos = base + lax.broadcasted_iota(jnp.int32, (total, rows), 0)
    allowed = (key_pos >= start_of) & (key_pos <= row_pos)

    pairs = [r[...] for r in pair_refs]
    keys = jnp.concatenate([p[:, :hd] for p in pairs], axis=0)
    values = jnp.concatenate([p[:, hd:] for p in pairs], axis=0)
    keys_t, values_t = keys.T, values.T
    dk = jnp.zeros((total, hd), F32)
    dv = jnp.zeros((total, hd), F32)
    for h in range(heads):
        cols = slice(h * hd, (h + 1) * hd)
        q, cot = q_ref[:, cols], cot_ref[:, cols]
        logits = jnp.where(allowed, dot(keys, q, NT) * scale, -1e30)
        top = jnp.max(logits, axis=0, keepdims=True)
        raised = jnp.exp(logits - top)
        probs = raised * (1.0 / jnp.sum(raised, axis=0, keepdims=True))
        probs_half = probs.astype(BF16)
        out_t = dot(values_t, probs_half).astype(BF16)
        cot_t = cot.T
        delta = jnp.sum(cot_t.astype(F32) * out_t.astype(F32), axis=0, keepdims=True)
        dscores = (probs * (dot(values, cot, NT) - delta)).astype(BF16)
        out_ref[:, cols] = out_t.T
        dq_ref[:, cols] = (dot(keys_t, dscores) * scale).astype(BF16).T
        dk += dot(dscores, q)
        dv += dot(probs_half, cot)
    both = jnp.concatenate([dk * scale, dv], axis=1)
    dpair_ref[...] = both[back * rows :]
    dback_ref[...] = both[: back * rows].astype(BF16)


def attend(place, docs, q, cot, pairs):
    rows, width = q.shape
    back = len(pairs) - 1
    two = 2 * HEAD_DIM
    return pl.pallas_call(
        functools.partial(attend_kernel, width // HEAD_DIM, back),
        in_specs=[SMEM, SMEM] + [VMEM] * (back + 3),
        out_specs=[VMEM] * 4,
        out_shape=[
            jax.ShapeDtypeStruct((rows, width), BF16),
            jax.ShapeDtypeStruct((rows, width), BF16),
            jax.ShapeDtypeStruct((rows, two), F32),
            jax.ShapeDtypeStruct((back * rows, two), BF16),
        ],
        compiler_params=pltpu.CompilerParams(vmem_limit_bytes=48 * 2**20),
        name="attend",
    )(place, docs, q, cot, *pairs)


def kept_rows(doc_row, flag_row, positions):
    ends = jnp.cumsum(doc_row)
    starts = ends - doc_row
    inside = (positions[:, None] >= starts[None, :]) & (positions[:, None] < ends[None, :])
    return jnp.sum(jnp.where(inside, flag_row[None, :], 0), axis=1)


def shards(inputs, weights, cotangent, doc_lengths, kept_flags):
    seq_count = lax.axis_size("seq")
    chips = lax.axis_size("dp") // CORES
    rest = seq_count // PAIR
    place = lax.axis_index("seq")
    x = place % PAIR
    tokens = inputs[0]
    local = tokens.shape[0]
    qwidth = cotangent.shape[2]
    shard_rows, cols = weights.shape
    width = shard_rows // seq_count
    back = -(-(local * seq_count // 2 - 1) // local)

    order_mine = block_order(chips, rest, x)
    order_other = block_order(chips, rest, 1 - x)
    tokens_other = swap_x(pick_blocks(tokens, order_other, width))
    tokens_mine = pick_blocks(tokens, order_mine, width)

    blocks = weights.reshape(seq_count, width, cols)

    def own_block(step):
        index = PAIR * ((place // PAIR - step + rest) % rest) + x
        return lax.dynamic_index_in_dim(blocks, index, 0, keepdims=False)

    groups = []
    for k in range(chips):
        if k == 0:
            here = [own_block(j) for j in range(rest)]
        else:
            first = shift_chip(own_block(0), k)
            here = [first] + [shift_rest(first, j) for j in range(1, rest)]
        here = jnp.concatenate(here, axis=0)
        groups += [here, swap_core(here)]
    weights_half = jnp.concatenate(groups, axis=0)

    partial_other = dot(tokens_other, weights_half).astype(BF16)
    pair_from = swap_x(partial_other[:, qwidth:])
    query_from = swap_x(partial_other[:, :qwidth])
    partial_mine = dot(tokens_mine, weights_half)
    pair = (partial_mine[:, qwidth:] + pair_from.astype(F32)).astype(BF16)
    query = (partial_mine[:, :qwidth] + query_from.astype(F32)).astype(BF16)

    doc_row, flag_row = doc_lengths[0], kept_flags[0]
    positions = place * local + lax.iota(jnp.int32, local)
    kept = kept_rows(doc_row, flag_row, positions)
    cot = jnp.where(kept[:, None] > 0, cotangent[0], jnp.zeros_like(cotangent[0]))

    pairs = [shift_seq(pair, j) for j in range(back, 0, -1)] + [pair]
    attention, dquery, dpair, dback = attend(place[None], doc_row, query, cot, pairs)

    dquery_other = swap_x(dquery)
    for j in range(1, back + 1):
        sent = dback[(back - j) * local : (back - j + 1) * local]
        dpair = dpair + shift_seq(sent, -j).astype(F32)
    dpair = dpair.astype(BF16)
    dpair_other = swap_x(dpair)

    dmine = jnp.concatenate([dquery, dpair], axis=1)
    dother = jnp.concatenate([dquery_other, dpair_other], axis=1)

    grad_from = swap_x(dot(dother, weights_half, NT).astype(BF16))
    grad_mine = dot(dmine, weights_half, NT).astype(BF16)
    order_all = jnp.concatenate([order_mine, order_other])
    where = jnp.zeros_like(order_all).at[order_all].set(lax.iota(jnp.int32, order_all.shape[0]))
    inputs_grad = place_blocks(grad_mine, grad_from, where, width)

    total = dot(tokens_mine, dmine, TN) + dot(tokens_other, dother, TN)
    total = total.reshape(chips, CORES, rest, width, cols)
    result = None
    for step in range(chips):
        k = (step + 1) % chips
        group = total[k, 0] + swap_core(total[k, 1].astype(BF16)).astype(F32)
        part = group[0]
        for j in range(1, rest):
            part = part + shift_rest(group[j].astype(BF16), -j).astype(F32)
        if k:
            part = shift_chip(part.astype(BF16), -k).astype(F32)
        result = part if result is None else result + part
    return (attention[None], inputs_grad[None], result)


def solution(mesh):
    in_specs = (
        P("dp", "seq", None),
        P("dp", None),
        P("dp", "seq", None),
        P("dp", None),
        P("dp", None),
    )
    out_specs = (P("dp", "seq", None), P("dp", "seq", None), P(("dp", "seq"), None))
    return jax.shard_map(shards, mesh=mesh, in_specs=in_specs, out_specs=out_specs, check_vma=False)
```

```python
import functools
import math

import jax
import jax.numpy as jnp
from jax import lax
from jax.experimental import pallas as pl
from jax.experimental.pallas import tpu as pltpu
from jax.sharding import PartitionSpec as P

HEAD_DIM = 128
PAIR = 2
CORES = 2
BF16 = jnp.bfloat16
F32 = jnp.float32
NT = (((1,), (1,)), ((), ()))
TN = (((0,), (0,)), ((), ()))
VMEM = pl.BlockSpec(memory_space=pltpu.VMEM)
SMEM = pl.BlockSpec(memory_space=pltpu.SMEM)


def dot(a, b, dims=(((1,), (0,)), ((), ()))):
    return lax.dot_general(a, b, dims, preferred_element_type=F32)


def swap_x(array):
    count = lax.axis_size("seq")
    return lax.ppermute(array, "seq", [(i, i ^ 1) for i in range(count)])


def shift_rest(array, step):
    count = lax.axis_size("seq")
    rest = count // PAIR
    pairs = [(i, PAIR * ((i // PAIR + step) % rest) + i % PAIR) for i in range(count)]
    return lax.ppermute(array, "seq", pairs)


def swap_core(array):
    count = lax.axis_size("dp")
    return lax.ppermute(array, "dp", [(i, i ^ 1) for i in range(count)])


def shift_chip(array, step):
    count = lax.axis_size("dp")
    chips = count // CORES
    pairs = [(i, CORES * ((i // CORES + step) % chips) + i % CORES) for i in range(count)]
    return lax.ppermute(array, "dp", pairs)


def shift_seq(array, step):
    count = lax.axis_size("seq")
    pairs = [(i, i + step) for i in range(count) if 0 <= i + step < count]
    return lax.ppermute(array, "seq", pairs)


def block_order(chips, rest, x):
    dp_index = lax.axis_index("dp")
    chip, core = dp_index // CORES, dp_index % CORES
    place = lax.axis_index("seq") // PAIR
    order = []
    for k in range(chips):
        for c in range(CORES):
            for j in range(rest):
                shard = CORES * ((chip - k + chips) % chips) + (core ^ c)
                order.append(shard * (PAIR * rest) + PAIR * ((place - j + rest) % rest) + x)
    return jnp.stack(order).astype(jnp.int32)


def lanes(index, width):
    return pl.ds(pl.multiple_of(index * width, width), width)


def split_kernel(width, mine_order, other_order, in_ref, mine_ref, other_ref):
    for i in range(mine_order.shape[0]):
        out = slice(i * width, (i + 1) * width)
        other_ref[:, out] = in_ref[:, lanes(other_order[i], width)]
        mine_ref[:, out] = in_ref[:, lanes(mine_order[i], width)]


def split_tokens(tokens, mine_order, other_order, width):
    rows, total = tokens.shape
    half = total // 2
    if width % 128:
        blocks = tokens.reshape(rows, total // width, width)
        take = lambda order: jnp.take(blocks, order, axis=1).reshape(rows, half)
        return take(mine_order), take(other_order)
    tile = min(rows, 64)
    return pl.pallas_call(
        functools.partial(split_kernel, width),
        grid_spec=pltpu.PrefetchScalarGridSpec(
            num_scalar_prefetch=2,
            grid=(rows // tile,),
            in_specs=[pl.BlockSpec((tile, total), lambda i, *_: (i, 0))],
            out_specs=[pl.BlockSpec((tile, half), lambda i, *_: (i, 0))] * 2,
        ),
        out_shape=[jax.ShapeDtypeStruct((rows, half), tokens.dtype)] * 2,
        name="split_tokens",
    )(mine_order, other_order, tokens)


def place_kernel(width, order, half_ref, base_ref, out_ref, sems):
    copies = []
    for i in range(order.shape[0]):
        source = half_ref.at[:, pl.ds(i * width, width)]
        copies.append(pltpu.make_async_copy(source, out_ref.at[:, lanes(order[i], width)], sems.at[i]))
    for copy in copies:
        copy.start()
    for copy in copies:
        copy.wait()


def place_half(base, half, order, width):
    anywhere = pl.BlockSpec(memory_space=pl.ANY)
    return pl.pallas_call(
        functools.partial(place_kernel, width),
        in_specs=[SMEM, anywhere, anywhere],
        out_specs=anywhere,
        out_shape=jax.ShapeDtypeStruct(base.shape, base.dtype),
        scratch_shapes=[pltpu.SemaphoreType.DMA((order.shape[0],))],
        input_output_aliases={2: 0},
        name="place_half",
    )(order, half, base)


def group_rows(width, rest, own_ref, piece_refs, own_order, k):
    if k == 0:
        here = [own_ref[pl.ds(pl.multiple_of(own_order[j] * width, width), width), :] for j in range(rest)]
        return jnp.concatenate(here + [piece_refs[0][...]], axis=0)
    return jnp.concatenate([r[...] for r in piece_refs[1 + (k - 1) * (rest + 1) : 1 + k * (rest + 1)]], axis=0)


def project_kernel(chips, rest, width, qwidth, own_order, tokens_ref, own_ref, *refs):
    pieces, (query_ref, pair_ref) = refs[:-2], refs[-2:]
    span = CORES * rest * width
    total = None
    for k in range(chips):
        rows = group_rows(width, rest, own_ref, pieces, own_order, k)
        term = dot(tokens_ref[:, k * span : (k + 1) * span], rows)
        total = term if total is None else total + term
    query_ref[...] = total[:, :qwidth].astype(query_ref.dtype)
    pair_ref[...] = total[:, qwidth:].astype(pair_ref.dtype)


def project(tokens, own_order, own, pieces, chips, rest, width, qwidth, kind):
    rows, cols = tokens.shape[0], own.shape[1]
    return pl.pallas_call(
        functools.partial(project_kernel, chips, rest, width, qwidth),
        in_specs=[SMEM] + [VMEM] * (2 + len(pieces)),
        out_specs=[VMEM] * 2,
        out_shape=[
            jax.ShapeDtypeStruct((rows, qwidth), kind),
            jax.ShapeDtypeStruct((rows, cols - qwidth), kind),
        ],
        compiler_params=pltpu.CompilerParams(vmem_limit_bytes=48 * 2**20),
        name="project",
    )(own_order, tokens, own, *pieces)


def grad_kernel(chips, rest, width, scatter, own_order, order, dquery_ref, dpair_ref, own_ref, *refs):
    pieces, out_ref = refs[:-1], refs[-1]
    span = CORES * rest * width
    grads = jnp.concatenate([dquery_ref[...], dpair_ref[...]], axis=1)
    for k in range(chips):
        rows = group_rows(width, rest, own_ref, pieces, own_order, k)
        term = dot(grads, rows, NT).astype(BF16)
        if scatter:
            for i in range(CORES * rest):
                place = lanes(order[k * CORES * rest + i], width)
                out_ref[:, place] = term[:, i * width : (i + 1) * width]
        else:
            out_ref[:, k * span : (k + 1) * span] = term


def width_grad(dquery, dpair, own_order, order, own, pieces, chips, rest, width, scatter):
    rows = dquery.shape[0]
    total = chips * CORES * rest * width * (PAIR if scatter else 1)
    return pl.pallas_call(
        functools.partial(grad_kernel, chips, rest, width, scatter),
        in_specs=[SMEM, SMEM] + [VMEM] * (3 + len(pieces)),
        out_specs=VMEM,
        out_shape=jax.ShapeDtypeStruct((rows, total), BF16),
        compiler_params=pltpu.CompilerParams(vmem_limit_bytes=48 * 2**20),
        name="width_grad",
    )(own_order, order, dquery, dpair, own, *pieces)


def weight_kernel(span, tokens_ref, other_ref, dq_ref, dp_ref, dq_other_ref, dp_other_ref, keep_ref, send_ref):
    mine = jnp.concatenate([dq_ref[...], dp_ref[...]], axis=1)
    other = jnp.concatenate([dq_other_ref[...], dp_other_ref[...]], axis=1)
    both = jnp.concatenate([mine, other], axis=0)
    left = jnp.concatenate([tokens_ref[...], other_ref[...]], axis=0)
    total = dot(left.T, both)
    keep_ref[...] = total[: span // 2]
    send_ref[...] = total[span // 2 :].astype(BF16)


def weight_terms(tokens, other, k, span, grads):
    rows = tokens.shape[0]
    cols = grads[0].shape[1] + grads[1].shape[1]
    column = pl.BlockSpec((rows, span), lambda i: (0, k))
    whole = [pl.BlockSpec(g.shape, lambda i: (0, 0)) for g in grads]
    return pl.pallas_call(
        functools.partial(weight_kernel, span),
        grid=(1,),
        in_specs=[column, column] + whole,
        out_specs=[pl.BlockSpec((span // 2, cols), lambda i: (0, 0))] * 2,
        out_shape=[
            jax.ShapeDtypeStruct((span // 2, cols), F32),
            jax.ShapeDtypeStruct((span // 2, cols), BF16),
        ],
        compiler_params=pltpu.CompilerParams(vmem_limit_bytes=48 * 2**20),
        name="weight_terms",
    )(tokens, other, *grads)


def core_sum_kernel(width, keep_ref, from_ref, mine_ref, *send_refs):
    total = keep_ref[...] + from_ref[...].astype(F32)
    mine_ref[...] = total[:width]
    for j, ref in enumerate(send_refs, 1):
        ref[...] = total[j * width : (j + 1) * width].astype(BF16)


def core_sum(keep, received, rest, width):
    cols = keep.shape[1]
    return pl.pallas_call(
        functools.partial(core_sum_kernel, width),
        in_specs=[VMEM] * 2,
        out_specs=[VMEM] * rest,
        out_shape=[jax.ShapeDtypeStruct((width, cols), F32)]
        + [jax.ShapeDtypeStruct((width, cols), BF16)] * (rest - 1),
        name="core_sum",
    )(keep, received)


def attend_kernel(
    heads, back, place_ref, docs_ref, q_ref, q_from_ref, cot_ref, *refs
):
    pair_refs, (out_ref, dq_ref, dpair_ref, dback_ref) = refs[: back + 1], refs[back + 1 :]
    rows = q_ref.shape[0]
    hd = HEAD_DIM
    scale = 1.0 / math.sqrt(hd)
    first = place_ref[0] * rows
    base = first - back * rows
    total = (back + 1) * rows

    row_pos = first + lax.broadcasted_iota(jnp.int32, (1, rows), 1)
    start_of = jnp.zeros((1, rows), jnp.int32)
    start = jnp.int32(0)
    for d in range(docs_ref.shape[0]):
        end = start + docs_ref[d]
        start_of = jnp.where((row_pos >= start) & (row_pos < end), start, start_of)
        start = end
    key_pos = base + lax.broadcasted_iota(jnp.int32, (total, rows), 0)
    allowed = (key_pos >= start_of) & (key_pos <= row_pos)

    pairs = [r[...] for r in pair_refs]
    keys = jnp.concatenate([p[:, :hd] for p in pairs], axis=0)
    values = jnp.concatenate([p[:, hd:] for p in pairs], axis=0)
    keys_t, values_t = keys.T, values.T
    dk = jnp.zeros((total, hd), F32)
    dv = jnp.zeros((total, hd), F32)
    for h in range(heads):
        cols = slice(h * hd, (h + 1) * hd)
        q = (q_ref[:, cols] + q_from_ref[:, cols].astype(F32)).astype(BF16)
        cot = cot_ref[:, cols]
        logits = jnp.where(allowed, dot(keys, q, NT) * scale, -1e30)
        top = jnp.max(logits, axis=0, keepdims=True)
        raised = jnp.exp(logits - top)
        probs = raised * (1.0 / jnp.sum(raised, axis=0, keepdims=True))
        probs_half = probs.astype(BF16)
        out_t = dot(values_t, probs_half).astype(BF16)
        cot_t = cot.T
        delta = jnp.sum(cot_t.astype(F32) * out_t.astype(F32), axis=0, keepdims=True)
        dscores = (probs * (dot(values, cot, NT) - delta)).astype(BF16)
        out_ref[:, cols] = out_t.T
        dq_ref[:, cols] = (dot(keys_t, dscores) * scale).astype(BF16).T
        dk += dot(dscores, q)
        dv += dot(probs_half, cot)
    both = jnp.concatenate([dk * scale, dv], axis=1)
    dpair_ref[...] = both[back * rows :]
    dback_ref[...] = both[: back * rows].astype(BF16)


def attend(place, docs, q, q_from, cot, pairs):
    rows, width = q.shape
    back = len(pairs) - 1
    two = 2 * HEAD_DIM
    return pl.pallas_call(
        functools.partial(attend_kernel, width // HEAD_DIM, back),
        in_specs=[SMEM, SMEM] + [VMEM] * (back + 4),
        out_specs=[VMEM] * 4,
        out_shape=[
            jax.ShapeDtypeStruct((rows, width), BF16),
            jax.ShapeDtypeStruct((rows, width), BF16),
            jax.ShapeDtypeStruct((rows, two), F32),
            jax.ShapeDtypeStruct((back * rows, two), BF16),
        ],
        compiler_params=pltpu.CompilerParams(vmem_limit_bytes=48 * 2**20),
        name="attend",
    )(place, docs, q, q_from, cot, *pairs)


def kept_rows(doc_row, flag_row, positions):
    ends = jnp.cumsum(doc_row)
    starts = ends - doc_row
    inside = (positions[:, None] >= starts[None, :]) & (positions[:, None] < ends[None, :])
    return jnp.sum(jnp.where(inside, flag_row[None, :], 0), axis=1)


def shards(inputs, weights, cotangent, doc_lengths, kept_flags):
    seq_count = lax.axis_size("seq")
    chips = lax.axis_size("dp") // CORES
    rest = seq_count // PAIR
    place = lax.axis_index("seq")
    x = place % PAIR
    tokens = inputs[0]
    local = tokens.shape[0]
    qwidth = cotangent.shape[2]
    shard_rows, cols = weights.shape
    width = shard_rows // seq_count
    back = -(-(local * seq_count // 2 - 1) // local)

    order_mine = block_order(chips, rest, x)
    order_other = block_order(chips, rest, 1 - x)
    tokens_mine, tokens_sent = split_tokens(tokens, order_mine, order_other, width)
    tokens_other = swap_x(tokens_sent)

    blocks = weights.reshape(seq_count, width, cols)
    own_order = jnp.stack([PAIR * ((place // PAIR - j + rest) % rest) + x for j in range(rest)])
    own_blocks = [lax.dynamic_index_in_dim(blocks, own_order[j], 0, keepdims=False) for j in range(rest)]
    pieces = [swap_core(jnp.concatenate(own_blocks, axis=0))]
    for k in range(1, chips):
        first = shift_chip(own_blocks[0], k)
        here = [first] + [shift_rest(first, j) for j in range(1, rest)]
        pieces += here + [swap_core(jnp.concatenate(here, axis=0))]
    weight_args = (weights, pieces, chips, rest, width)

    query_sent, pair_sent = project(tokens_other, own_order, *weight_args, qwidth, BF16)
    pair_from, query_from = swap_x(pair_sent), swap_x(query_sent)
    query, pair = project(tokens_mine, own_order, *weight_args, qwidth, F32)
    pair = (pair + pair_from.astype(F32)).astype(BF16)

    doc_row, flag_row = doc_lengths[0], kept_flags[0]
    positions = place * local + lax.iota(jnp.int32, local)
    kept = kept_rows(doc_row, flag_row, positions)
    cot = jnp.where(kept[:, None] > 0, cotangent[0], jnp.zeros_like(cotangent[0]))

    pairs = [shift_seq(pair, j) for j in range(back, 0, -1)] + [pair]
    attention, dquery, dpair, dback = attend(place[None], doc_row, query, query_from, cot, pairs)

    dquery_other = swap_x(dquery)
    for j in range(1, back + 1):
        sent = dback[(back - j) * local : (back - j + 1) * local]
        dpair = dpair + shift_seq(sent, -j).astype(F32)
    dpair = dpair.astype(BF16)
    dpair_other = swap_x(dpair)

    span = CORES * rest * width
    grads = (dquery, dpair, dquery_other, dpair_other)
    result = None
    for step in range(chips):
        k = (step + 1) % chips
        keep, sent = weight_terms(tokens_mine, tokens_other, k, span, grads)
        part, *sent = core_sum(keep, swap_core(sent), rest, width)
        for j in range(1, rest):
            part = part + shift_rest(sent[j - 1], -j).astype(F32)
        if k:
            part = shift_chip(part.astype(BF16), -k).astype(F32)
        result = part if result is None else result + part

    grad_args = (own_order, order_mine, *weight_args)
    grad_from = swap_x(width_grad(dquery_other, dpair_other, *grad_args, False))
    if width % 128:
        grad_mine = width_grad(dquery, dpair, *grad_args, False)
        order_all = jnp.concatenate([order_mine, order_other])
        where = jnp.zeros_like(order_all).at[order_all].set(lax.iota(jnp.int32, order_all.shape[0]))
        both = jnp.concatenate([grad_mine, grad_from], axis=1).reshape(local, -1, width)
        inputs_grad = jnp.take(both, where, axis=1).reshape(tokens.shape)
    else:
        base = width_grad(dquery, dpair, *grad_args, True)
        inputs_grad = place_half(base, grad_from, order_other, width)
    return (attention[None], inputs_grad[None], result)


def solution(mesh):
    in_specs = (
        P("dp", "seq", None),
        P("dp", None),
        P("dp", "seq", None),
        P("dp", None),
        P("dp", None),
    )
    out_specs = (P("dp", "seq", None), P("dp", "seq", None), P(("dp", "seq"), None))
    return jax.shard_map(shards, mesh=mesh, in_specs=in_specs, out_specs=out_specs, check_vma=False)
```

```python
import functools
import math

import jax
import jax.numpy as jnp
from jax import lax
from jax.experimental import pallas as pl
from jax.experimental.pallas import tpu as pltpu
from jax.sharding import PartitionSpec as P

HEAD_DIM = 128
PAIR = 2
CORES = 2
BF16 = jnp.bfloat16
F32 = jnp.float32
NT = (((1,), (1,)), ((), ()))
TN = (((0,), (0,)), ((), ()))
VMEM = pl.BlockSpec(memory_space=pltpu.VMEM)
SMEM = pl.BlockSpec(memory_space=pltpu.SMEM)


def dot(a, b, dims=(((1,), (0,)), ((), ()))):
    return lax.dot_general(a, b, dims, preferred_element_type=F32)


def swap_x(array):
    count = lax.axis_size("seq")
    return lax.ppermute(array, "seq", [(i, i ^ 1) for i in range(count)])


def shift_rest(array, step):
    count = lax.axis_size("seq")
    rest = count // PAIR
    pairs = [(i, PAIR * ((i // PAIR + step) % rest) + i % PAIR) for i in range(count)]
    return lax.ppermute(array, "seq", pairs)


def swap_core(array):
    count = lax.axis_size("dp")
    return lax.ppermute(array, "dp", [(i, i ^ 1) for i in range(count)])


def shift_chip(array, step):
    count = lax.axis_size("dp")
    chips = count // CORES
    pairs = [(i, CORES * ((i // CORES + step) % chips) + i % CORES) for i in range(count)]
    return lax.ppermute(array, "dp", pairs)


def shift_seq(array, step):
    count = lax.axis_size("seq")
    pairs = [(i, i + step) for i in range(count) if 0 <= i + step < count]
    return lax.ppermute(array, "seq", pairs)


def block_order(chips, rest, flip):
    dp_index, place = lax.axis_index("dp"), lax.axis_index("seq")
    chip, core = dp_index // CORES, dp_index % CORES
    around, x = place // PAIR, (place + flip) % PAIR
    order = []
    for k in range(chips):
        for c in range(CORES):
            for j in range(rest):
                shard = CORES * ((chip - k + chips) % chips) + (core + c) % CORES
                order.append(shard * (PAIR * rest) + PAIR * ((around - j + rest) % rest) + x)
    return order


def lanes(index, width):
    return pl.ds(pl.multiple_of(index * width, width), width)


def split_kernel(chips, rest, width, in_ref, mine_ref, other_ref):
    mine, other = block_order(chips, rest, 0), block_order(chips, rest, 1)
    for i in range(len(mine)):
        out = slice(i * width, (i + 1) * width)
        other_ref[:, out] = in_ref[:, lanes(other[i], width)]
        mine_ref[:, out] = in_ref[:, lanes(mine[i], width)]


def split_tokens(tokens, chips, rest, width):
    rows, total = tokens.shape
    half = total // 2
    if width % 128:
        blocks = tokens.reshape(rows, total // width, width)
        orders = [jnp.stack(block_order(chips, rest, flip)) for flip in range(PAIR)]
        return [jnp.take(blocks, order, axis=1).reshape(rows, half) for order in orders]
    tile = min(rows, 128)
    return pl.pallas_call(
        functools.partial(split_kernel, chips, rest, width),
        grid=(rows // tile,),
        in_specs=[pl.BlockSpec((tile, total), lambda i: (i, 0))],
        out_specs=[pl.BlockSpec((tile, half), lambda i: (i, 0))] * 2,
        out_shape=[jax.ShapeDtypeStruct((rows, half), tokens.dtype)] * 2,
        name="split_tokens",
    )(tokens)


def merge_kernel(chips, rest, width, mine_ref, other_ref, out_ref):
    mine, other = block_order(chips, rest, 0), block_order(chips, rest, 1)
    for i in range(len(mine)):
        source = slice(i * width, (i + 1) * width)
        out_ref[:, lanes(mine[i], width)] = mine_ref[:, source]
        out_ref[:, lanes(other[i], width)] = other_ref[:, source]


def merge_halves(mine, other, chips, rest, width):
    rows, half = mine.shape
    if width % 128:
        order = jnp.stack(block_order(chips, rest, 0) + block_order(chips, rest, 1))
        where = jnp.zeros_like(order).at[order].set(lax.iota(order.dtype, order.shape[0]))
        blocks = jnp.concatenate([mine, other], axis=1).reshape(rows, order.shape[0], width)
        return jnp.take(blocks, where, axis=1).reshape(rows, 2 * half)
    tile = min(rows, 128)
    return pl.pallas_call(
        functools.partial(merge_kernel, chips, rest, width),
        grid=(rows // tile,),
        in_specs=[pl.BlockSpec((tile, half), lambda i: (i, 0))] * 2,
        out_specs=pl.BlockSpec((tile, 2 * half), lambda i: (i, 0)),
        out_shape=jax.ShapeDtypeStruct((rows, 2 * half), mine.dtype),
        name="merge_halves",
    )(mine, other)


def project_kernel(first, span, per, qwidth, has_sum, tokens_ref, *refs):
    if has_sum:
        sum_ref, refs = refs[0], refs[1:]
        total = sum_ref[...]
    else:
        total = None
    pieces = refs[:-2] if qwidth else refs[:-1]
    for g in range(len(pieces) // per):
        rows = jnp.concatenate([r[...] for r in pieces[g * per : (g + 1) * per]], axis=0)
        term = dot(tokens_ref[:, (first + g) * span : (first + g + 1) * span], rows)
        total = term if total is None else total + term
    if qwidth:
        query_ref, pair_ref = refs[-2:]
        query_ref[...] = total[:, :qwidth].astype(query_ref.dtype)
        pair_ref[...] = total[:, qwidth:].astype(pair_ref.dtype)
    else:
        refs[-1][...] = total


def project(tokens, groups, first, qwidth=0, kind=F32, so_far=None):
    rows = tokens.shape[0]
    cols = groups[0][0].shape[1]
    pieces = [piece for group in groups for piece in group]
    span = sum(piece.shape[0] for piece in groups[0])
    widths = [qwidth, cols - qwidth] if qwidth else [cols]
    sums = [] if so_far is None else [so_far]
    outs = pl.pallas_call(
        functools.partial(project_kernel, first, span, len(groups[0]), qwidth, len(sums)),
        in_specs=[VMEM] * (1 + len(sums) + len(pieces)),
        out_specs=[VMEM] * len(widths),
        out_shape=[jax.ShapeDtypeStruct((rows, w), kind) for w in widths],
        compiler_params=pltpu.CompilerParams(vmem_limit_bytes=48 * 2**20),
        name="project",
    )(tokens, *sums, *pieces)
    return outs if qwidth else outs[0]


def grad_kernel(span, per, dquery_ref, dpair_ref, *refs):
    pieces, out_ref = refs[:-1], refs[-1]
    grads = jnp.concatenate([dquery_ref[...], dpair_ref[...]], axis=1)
    for k in range(len(pieces) // per):
        rows = jnp.concatenate([r[...] for r in pieces[k * per : (k + 1) * per]], axis=0)
        out_ref[:, k * span : (k + 1) * span] = dot(grads, rows, NT).astype(BF16)


def width_grad(dquery, dpair, groups):
    rows = dquery.shape[0]
    pieces = [piece for group in groups for piece in group]
    span = sum(piece.shape[0] for piece in groups[0])
    return pl.pallas_call(
        functools.partial(grad_kernel, span, len(groups[0])),
        in_specs=[VMEM] * (2 + len(pieces)),
        out_specs=VMEM,
        out_shape=jax.ShapeDtypeStruct((rows, span * len(groups)), BF16),
        compiler_params=pltpu.CompilerParams(vmem_limit_bytes=48 * 2**20),
        name="width_grad",
    )(dquery, dpair, *pieces)


def weight_kernel(steps, span, tokens_ref, other_ref, dq_ref, dp_ref, dq_other_ref, dp_other_ref, keep_ref, send_ref):
    mine = jnp.concatenate([dq_ref[...], dp_ref[...]], axis=1)
    other = jnp.concatenate([dq_other_ref[...], dp_other_ref[...]], axis=1)
    both = jnp.concatenate([mine, other], axis=0)
    half = span // 2
    for i, k in enumerate(steps):
        cut = slice(k * span, (k + 1) * span)
        left = jnp.concatenate([tokens_ref[:, cut], other_ref[:, cut]], axis=0)
        total = dot(left.T, both).astype(BF16)
        keep_ref[i * half : (i + 1) * half, :] = total[:half]
        send_ref[i * half : (i + 1) * half, :] = total[half:]


def weight_terms(tokens, other, steps, span, grads):
    cols = grads[0].shape[1] + grads[1].shape[1]
    return pl.pallas_call(
        functools.partial(weight_kernel, steps, span),
        in_specs=[VMEM] * 6,
        out_specs=[VMEM] * 2,
        out_shape=[jax.ShapeDtypeStruct((len(steps) * span // 2, cols), BF16)] * 2,
        compiler_params=pltpu.CompilerParams(vmem_limit_bytes=48 * 2**20),
        name="weight_terms",
    )(tokens, other, *grads)


def core_sum_kernel(rest, width, keep_ref, from_ref, *out_refs):
    total = (keep_ref[...].astype(F32) + from_ref[...].astype(F32)).astype(BF16)
    for i in range(total.shape[0] // (rest * width)):
        for j in range(rest):
            source = (i * rest + j) * width
            out_refs[j][i * width : (i + 1) * width, :] = total[source : source + width]


def core_sum(keep, received, rest, width):
    rows, cols = keep.shape
    return pl.pallas_call(
        functools.partial(core_sum_kernel, rest, width),
        in_specs=[VMEM] * 2,
        out_specs=[VMEM] * rest,
        out_shape=[jax.ShapeDtypeStruct((rows // rest, cols), BF16)] * rest,
        name="core_sum",
    )(keep, received)


def sum_kernel(width, *refs):
    count = refs[0].shape[0] // width
    terms, outs = refs[:-count], refs[-count:]
    total = terms[0][...].astype(F32)
    for ref in terms[1:]:
        total = total + ref[...].astype(F32)
    for i, ref in enumerate(outs):
        ref[...] = total[i * width : (i + 1) * width].astype(ref.dtype)


def sum_terms(terms, width, kinds):
    cols = terms[0].shape[1]
    return pl.pallas_call(
        functools.partial(sum_kernel, width),
        in_specs=[VMEM] * len(terms),
        out_specs=[VMEM] * len(kinds),
        out_shape=[jax.ShapeDtypeStruct((width, cols), kind) for kind in kinds],
        name="sum_terms",
    )(*terms)


def attend_kernel(
    heads, back, docs_ref, q_ref, q_from_ref, cot_ref, *refs
):
    pair_refs, (out_ref, dq_ref, dpair_ref, dback_ref) = refs[: back + 1], refs[back + 1 :]
    rows = q_ref.shape[0]
    hd = HEAD_DIM
    scale = 1.0 / math.sqrt(hd)
    first = lax.axis_index("seq") * rows
    base = first - back * rows
    total = (back + 1) * rows

    row_pos = first + lax.broadcasted_iota(jnp.int32, (1, rows), 1)
    start_of = jnp.zeros((1, rows), jnp.int32)
    start = jnp.int32(0)
    for d in range(docs_ref.shape[0]):
        end = start + docs_ref[d]
        start_of = jnp.where((row_pos >= start) & (row_pos < end), start, start_of)
        start = end
    key_pos = base + lax.broadcasted_iota(jnp.int32, (total, rows), 0)
    allowed = (key_pos >= start_of) & (key_pos <= row_pos)

    pairs = [r[...] for r in pair_refs]
    keys = jnp.concatenate([p[:, :hd] for p in pairs], axis=0)
    values = jnp.concatenate([p[:, hd:] for p in pairs], axis=0)
    keys_t, values_t = keys.T, values.T
    dk = jnp.zeros((total, hd), F32)
    dv = jnp.zeros((total, hd), F32)
    for h in range(heads):
        cols = slice(h * hd, (h + 1) * hd)
        q = (q_ref[:, cols] + q_from_ref[:, cols].astype(F32)).astype(BF16)
        cot = cot_ref[:, cols]
        logits = jnp.where(allowed, dot(keys, q, NT) * scale, -1e30)
        top = jnp.max(logits, axis=0, keepdims=True)
        raised = jnp.exp(logits - top)
        probs = raised * (1.0 / jnp.sum(raised, axis=0, keepdims=True))
        probs_half = probs.astype(BF16)
        out_t = dot(values_t, probs_half).astype(BF16)
        cot_t = cot.T
        delta = jnp.sum(cot_t.astype(F32) * out_t.astype(F32), axis=0, keepdims=True)
        dscores = (probs * (dot(values, cot, NT) - delta)).astype(BF16)
        out_ref[:, cols] = out_t.T
        dq_ref[:, cols] = (dot(keys_t, dscores) * scale).astype(BF16).T
        dk += dot(dscores, q)
        dv += dot(probs_half, cot)
    both = jnp.concatenate([dk * scale, dv], axis=1)
    dpair_ref[...] = both[back * rows :]
    dback_ref[...] = both[: back * rows].astype(BF16)


def attend(docs, q, q_from, cot, pairs):
    rows, width = q.shape
    back = len(pairs) - 1
    two = 2 * HEAD_DIM
    return pl.pallas_call(
        functools.partial(attend_kernel, width // HEAD_DIM, back),
        in_specs=[SMEM] + [VMEM] * (back + 4),
        out_specs=[VMEM] * 4,
        out_shape=[
            jax.ShapeDtypeStruct((rows, width), BF16),
            jax.ShapeDtypeStruct((rows, width), BF16),
            jax.ShapeDtypeStruct((rows, two), F32),
            jax.ShapeDtypeStruct((back * rows, two), BF16),
        ],
        compiler_params=pltpu.CompilerParams(vmem_limit_bytes=48 * 2**20),
        name="attend",
    )(docs, q, q_from, cot, *pairs)


def kept_rows(doc_row, flag_row, positions):
    ends = jnp.cumsum(doc_row)
    starts = ends - doc_row
    inside = (positions[:, None] >= starts[None, :]) & (positions[:, None] < ends[None, :])
    return jnp.sum(jnp.where(inside, flag_row[None, :], 0), axis=1)


def shards(inputs, weights, cotangent, doc_lengths, kept_flags):
    seq_count = lax.axis_size("seq")
    chips = lax.axis_size("dp") // CORES
    rest = seq_count // PAIR
    place = lax.axis_index("seq")
    tokens = inputs[0]
    local = tokens.shape[0]
    qwidth = cotangent.shape[2]
    shard_rows, cols = weights.shape
    width = shard_rows // seq_count
    back = -(-(local * seq_count // 2 - 1) // local)

    tokens_mine, tokens_sent = split_tokens(tokens, chips, rest, width)
    tokens_other = swap_x(tokens_sent)

    blocks = weights.reshape(seq_count, width, cols)
    groups = []
    for k in range(chips):
        if k == 0:
            places = [PAIR * ((place // PAIR - j + rest) % rest) + place % PAIR for j in range(rest)]
            here = [lax.dynamic_index_in_dim(blocks, p, 0, keepdims=False) for p in places]
            own = here[0]
        else:
            first = shift_chip(own, k)
            here = [first] + [shift_rest(first, j) for j in range(1, rest)]
        groups.append(here + [swap_core(piece) for piece in here])

    early, late, last = groups[:-1], groups[-1:], chips - 1
    so_far = project(tokens_other, early, 0)
    query_sent, pair_sent = project(tokens_other, late, last, qwidth, BF16, so_far)
    pair_from, query_from = swap_x(pair_sent), swap_x(query_sent)
    so_far = project(tokens_mine, early, 0)
    query, pair = project(tokens_mine, late, last, qwidth, F32, so_far)
    pair = (pair + pair_from.astype(F32)).astype(BF16)

    doc_row, flag_row = doc_lengths[0], kept_flags[0]
    positions = place * local + lax.iota(jnp.int32, local)
    kept = kept_rows(doc_row, flag_row, positions)
    cot = jnp.where(kept[:, None] > 0, cotangent[0], jnp.zeros_like(cotangent[0]))

    pairs = [shift_seq(pair, j) for j in range(back, 0, -1)] + [pair]
    attention, dquery, dpair, dback = attend(doc_row, query, query_from, cot, pairs)

    dquery_other = swap_x(dquery)
    for j in range(1, back + 1):
        sent = dback[(back - j) * local : (back - j + 1) * local]
        dpair = dpair + shift_seq(sent, -j).astype(F32)
    dpair = dpair.astype(BF16)
    dpair_other = swap_x(dpair)

    span = CORES * rest * width
    grads = (dquery, dpair, dquery_other, dpair_other)
    order = sorted(range(chips), key=lambda k: (k == 0, -min(k, chips - k), k))
    finished = []
    for steps in (order[: chips // 2], order[chips // 2 :]):
        keep, sent = weight_terms(tokens_mine, tokens_other, steps, span, grads)
        kept_here, *sent = core_sum(keep, swap_core(sent), rest, width)
        terms = [kept_here] + [shift_rest(piece, -j) for j, piece in enumerate(sent, 1)]
        parts = sum_terms(terms, width, [BF16 if k else F32 for k in steps])
        finished += [shift_chip(part, -k) if k else part for k, part in zip(steps, parts)]
    (weights_grad,) = sum_terms(finished, width, [F32])

    grad_from = swap_x(width_grad(dquery_other, dpair_other, groups))
    inputs_grad = merge_halves(width_grad(dquery, dpair, groups), grad_from, chips, rest, width)
    return (attention[None], inputs_grad[None], weights_grad)


def solution(mesh):
    in_specs = (
        P("dp", "seq", None),
        P("dp", None),
        P("dp", "seq", None),
        P("dp", None),
        P("dp", None),
    )
    out_specs = (P("dp", "seq", None), P("dp", "seq", None), P(("dp", "seq"), None))
    return jax.shard_map(shards, mesh=mesh, in_specs=in_specs, out_specs=out_specs, check_vma=False)
```

```python
import functools
import math

import jax
import jax.numpy as jnp
from jax import lax
from jax.experimental import pallas as pl
from jax.experimental.pallas import tpu as pltpu
from jax.sharding import PartitionSpec as P

HEAD_DIM = 128
PAIR = 2
CORES = 2
BF16 = jnp.bfloat16
F32 = jnp.float32
NT = (((1,), (1,)), ((), ()))
TN = (((0,), (0,)), ((), ()))
VMEM = pl.BlockSpec(memory_space=pltpu.VMEM)
SMEM = pl.BlockSpec(memory_space=pltpu.SMEM)


def dot(a, b, dims=(((1,), (0,)), ((), ()))):
    return lax.dot_general(a, b, dims, preferred_element_type=F32)


def swap_x(array):
    count = lax.axis_size("seq")
    return lax.ppermute(array, "seq", [(i, i ^ 1) for i in range(count)])


def shift_rest(array, step):
    count = lax.axis_size("seq")
    rest = count // PAIR
    pairs = [(i, PAIR * ((i // PAIR + step) % rest) + i % PAIR) for i in range(count)]
    return lax.ppermute(array, "seq", pairs)


def swap_core(array):
    count = lax.axis_size("dp")
    return lax.ppermute(array, "dp", [(i, i ^ 1) for i in range(count)])


def shift_chip(array, step):
    count = lax.axis_size("dp")
    chips = count // CORES
    pairs = [(i, CORES * ((i // CORES + step) % chips) + i % CORES) for i in range(count)]
    return lax.ppermute(array, "dp", pairs)


def shift_seq(array, step):
    count = lax.axis_size("seq")
    pairs = [(i, i + step) for i in range(count) if 0 <= i + step < count]
    return lax.ppermute(array, "seq", pairs)


def block_order(chips, rest, flip):
    dp_index, place = lax.axis_index("dp"), lax.axis_index("seq")
    chip, core = dp_index // CORES, dp_index % CORES
    around, x = place // PAIR, (place + flip) % PAIR
    order = []
    for c in range(CORES):
        for k in range(chips):
            for j in range(rest):
                shard = CORES * ((chip - k + chips) % chips) + (core + c) % CORES
                order.append(shard * (PAIR * rest) + PAIR * ((around - j + rest) % rest) + x)
    return order


def lanes(index, width):
    return pl.ds(pl.multiple_of(index * width, width), width)


def split_kernel(chips, rest, width, in_ref, *out_refs):
    for flip in range(PAIR):
        order = block_order(chips, rest, flip)
        count = len(order) // CORES
        for i, block in enumerate(order):
            at = slice(i % count * width, (i % count + 1) * width)
            out_refs[flip * CORES + i // count][:, at] = in_ref[:, lanes(block, width)]


def split_tokens(tokens, chips, rest, width):
    rows, total = tokens.shape
    parts = PAIR * CORES
    if width % 128:
        blocks = tokens.reshape(rows, total // width, width)
        order = jnp.stack(block_order(chips, rest, 0) + block_order(chips, rest, 1))
        return jnp.split(jnp.take(blocks, order, axis=1).reshape(rows, total), parts, axis=1)
    tile = min(rows, 128)
    return pl.pallas_call(
        functools.partial(split_kernel, chips, rest, width),
        grid=(rows // tile,),
        in_specs=[pl.BlockSpec((tile, total), lambda i: (i, 0))],
        out_specs=[pl.BlockSpec((tile, total // parts), lambda i: (i, 0))] * parts,
        out_shape=[jax.ShapeDtypeStruct((rows, total // parts), tokens.dtype)] * parts,
        name="split_tokens",
    )(tokens)


def merge_kernel(chips, rest, width, mine_ref, other_ref, out_ref):
    mine, other = block_order(chips, rest, 0), block_order(chips, rest, 1)
    for i in range(len(mine)):
        source = slice(i * width, (i + 1) * width)
        out_ref[:, lanes(mine[i], width)] = mine_ref[:, source]
        out_ref[:, lanes(other[i], width)] = other_ref[:, source]


def merge_halves(mine, other, chips, rest, width):
    rows, half = mine.shape
    if width % 128:
        order = jnp.stack(block_order(chips, rest, 0) + block_order(chips, rest, 1))
        where = jnp.zeros_like(order).at[order].set(lax.iota(order.dtype, order.shape[0]))
        blocks = jnp.concatenate([mine, other], axis=1).reshape(rows, order.shape[0], width)
        return jnp.take(blocks, where, axis=1).reshape(rows, 2 * half)
    tile = min(rows, 128)
    return pl.pallas_call(
        functools.partial(merge_kernel, chips, rest, width),
        grid=(rows // tile,),
        in_specs=[pl.BlockSpec((tile, half), lambda i: (i, 0))] * 2,
        out_specs=pl.BlockSpec((tile, 2 * half), lambda i: (i, 0)),
        out_shape=jax.ShapeDtypeStruct((rows, 2 * half), mine.dtype),
        name="merge_halves",
    )(mine, other)


def project_kernel(span, per, qwidth, has_sum, tokens_ref, *refs):
    if has_sum:
        sum_ref, refs = refs[0], refs[1:]
        total = sum_ref[...]
    else:
        total = None
    pieces = refs[:-2] if qwidth else refs[:-1]
    for g in range(len(pieces) // per):
        rows = jnp.concatenate([r[...] for r in pieces[g * per : (g + 1) * per]], axis=0)
        term = dot(tokens_ref[:, g * span : (g + 1) * span], rows)
        total = term if total is None else total + term
    if qwidth:
        query_ref, pair_ref = refs[-2:]
        query_ref[...] = total[:, :qwidth].astype(query_ref.dtype)
        pair_ref[...] = total[:, qwidth:].astype(pair_ref.dtype)
    else:
        refs[-1][...] = total


def project(tokens, groups, qwidth=0, kind=F32, so_far=None):
    rows = tokens.shape[0]
    cols = groups[0][0].shape[1]
    pieces = [piece for group in groups for piece in group]
    span = sum(piece.shape[0] for piece in groups[0])
    widths = [qwidth, cols - qwidth] if qwidth else [cols]
    sums = [] if so_far is None else [so_far]
    outs = pl.pallas_call(
        functools.partial(project_kernel, span, len(groups[0]), qwidth, len(sums)),
        in_specs=[VMEM] * (1 + len(sums) + len(pieces)),
        out_specs=[VMEM] * len(widths),
        out_shape=[jax.ShapeDtypeStruct((rows, w), kind) for w in widths],
        compiler_params=pltpu.CompilerParams(vmem_limit_bytes=48 * 2**20),
        name="project",
    )(tokens, *sums, *pieces)
    return outs if qwidth else outs[0]


def grad_kernel(span, per, dquery_ref, dpair_ref, *refs):
    pieces, out_ref = refs[:-1], refs[-1]
    grads = jnp.concatenate([dquery_ref[...], dpair_ref[...]], axis=1)
    for k in range(len(pieces) // per):
        rows = jnp.concatenate([r[...] for r in pieces[k * per : (k + 1) * per]], axis=0)
        out_ref[:, k * span : (k + 1) * span] = dot(grads, rows, NT).astype(BF16)


def width_grad(dquery, dpair, groups):
    rows = dquery.shape[0]
    pieces = [piece for group in groups for piece in group]
    span = sum(piece.shape[0] for piece in groups[0])
    return pl.pallas_call(
        functools.partial(grad_kernel, span, len(groups[0])),
        in_specs=[VMEM] * (2 + len(pieces)),
        out_specs=VMEM,
        out_shape=jax.ShapeDtypeStruct((rows, span * len(groups)), BF16),
        compiler_params=pltpu.CompilerParams(vmem_limit_bytes=48 * 2**20),
        name="width_grad",
    )(dquery, dpair, *pieces)


def weight_kernel(steps, rest, width, count, *refs):
    tokens, dquery, dpair = refs[:count], refs[count : 2 * count], refs[2 * count : 3 * count]
    outs = refs[3 * count :]
    right = jnp.concatenate(
        [jnp.concatenate([q[...], p[...]], axis=1) for q, p in zip(dquery, dpair)], axis=0
    )
    span = rest * width
    for i, k in enumerate(steps):
        left = jnp.concatenate([t[:, k * span : (k + 1) * span] for t in tokens], axis=0)
        total = dot(left.T, right)
        for j in range(rest):
            out = outs[i * rest + j]
            out[...] = total[j * width : (j + 1) * width].astype(out.dtype)


def weight_terms(steps, rest, width, tokens, dquery, dpair):
    cols = dquery[0].shape[1] + dpair[0].shape[1]
    count = len(tokens)
    return pl.pallas_call(
        functools.partial(weight_kernel, steps, rest, width, count),
        in_specs=[VMEM] * (3 * count),
        out_specs=[VMEM] * (len(steps) * rest),
        out_shape=[jax.ShapeDtypeStruct((width, cols), BF16 if j else F32) for _ in steps for j in range(rest)],
        compiler_params=pltpu.CompilerParams(vmem_limit_bytes=48 * 2**20),
        name="weight_terms",
    )(*tokens, *dquery, *dpair)


def attend_kernel(
    heads, back, docs_ref, q_ref, q_from_ref, cot_ref, *refs
):
    pair_refs, (out_ref, dq_ref, dpair_ref, dback_ref) = refs[: back + 1], refs[back + 1 :]
    rows = q_ref.shape[0]
    hd = HEAD_DIM
    scale = 1.0 / math.sqrt(hd)
    first = lax.axis_index("seq") * rows
    base = first - back * rows
    total = (back + 1) * rows

    row_pos = first + lax.broadcasted_iota(jnp.int32, (1, rows), 1)
    start_of = jnp.zeros((1, rows), jnp.int32)
    start = jnp.int32(0)
    for d in range(docs_ref.shape[0]):
        end = start + docs_ref[d]
        start_of = jnp.where((row_pos >= start) & (row_pos < end), start, start_of)
        start = end
    key_pos = base + lax.broadcasted_iota(jnp.int32, (total, rows), 0)
    allowed = (key_pos >= start_of) & (key_pos <= row_pos)

    pairs = [r[...] for r in pair_refs]
    keys = jnp.concatenate([p[:, :hd] for p in pairs], axis=0)
    values = jnp.concatenate([p[:, hd:] for p in pairs], axis=0)
    keys_t, values_t = keys.T, values.T
    dk = jnp.zeros((total, hd), F32)
    dv = jnp.zeros((total, hd), F32)
    for h in range(heads):
        cols = slice(h * hd, (h + 1) * hd)
        q = (q_ref[:, cols] + q_from_ref[:, cols].astype(F32)).astype(BF16)
        cot = cot_ref[:, cols]
        logits = jnp.where(allowed, dot(keys, q, NT) * scale, -1e30)
        top = jnp.max(logits, axis=0, keepdims=True)
        raised = jnp.exp(logits - top)
        probs = raised * (1.0 / jnp.sum(raised, axis=0, keepdims=True))
        probs_half = probs.astype(BF16)
        out_t = dot(values_t, probs_half).astype(BF16)
        cot_t = cot.T
        delta = jnp.sum(cot_t.astype(F32) * out_t.astype(F32), axis=0, keepdims=True)
        dscores = (probs * (dot(values, cot, NT) - delta)).astype(BF16)
        out_ref[:, cols] = out_t.T
        dq_ref[:, cols] = (dot(keys_t, dscores) * scale).astype(BF16).T
        dk += dot(dscores, q)
        dv += dot(probs_half, cot)
    both = jnp.concatenate([dk * scale, dv], axis=1)
    dpair_ref[...] = both[back * rows :]
    dback_ref[...] = both[: back * rows].astype(BF16)


def attend(docs, q, q_from, cot, pairs):
    rows, width = q.shape
    back = len(pairs) - 1
    two = 2 * HEAD_DIM
    return pl.pallas_call(
        functools.partial(attend_kernel, width // HEAD_DIM, back),
        in_specs=[SMEM] + [VMEM] * (back + 4),
        out_specs=[VMEM] * 4,
        out_shape=[
            jax.ShapeDtypeStruct((rows, width), BF16),
            jax.ShapeDtypeStruct((rows, width), BF16),
            jax.ShapeDtypeStruct((rows, two), F32),
            jax.ShapeDtypeStruct((back * rows, two), BF16),
        ],
        compiler_params=pltpu.CompilerParams(vmem_limit_bytes=48 * 2**20),
        name="attend",
    )(docs, q, q_from, cot, *pairs)


def kept_rows(doc_row, flag_row, positions):
    ends = jnp.cumsum(doc_row)
    starts = ends - doc_row
    inside = (positions[:, None] >= starts[None, :]) & (positions[:, None] < ends[None, :])
    return jnp.sum(jnp.where(inside, flag_row[None, :], 0), axis=1)


def shards(inputs, weights, cotangent, doc_lengths, kept_flags):
    seq_count = lax.axis_size("seq")
    chips = lax.axis_size("dp") // CORES
    rest = seq_count // PAIR
    place = lax.axis_index("seq")
    tokens = inputs[0]
    local = tokens.shape[0]
    qwidth = cotangent.shape[2]
    shard_rows, cols = weights.shape
    width = shard_rows // seq_count
    back = -(-(local * seq_count // 2 - 1) // local)

    mine_own, mine_across, *sent = split_tokens(tokens, chips, rest, width)
    other_own, other_across = [swap_x(part) for part in sent]

    blocks = weights.reshape(seq_count, width, cols)
    places = [PAIR * ((place // PAIR - j + rest) % rest) + place % PAIR for j in range(rest)]
    groups_own = [[lax.dynamic_index_in_dim(blocks, p, 0, keepdims=False) for p in places]]
    for k in range(1, chips):
        first = shift_chip(groups_own[0][0], k)
        groups_own.append([first] + [shift_rest(first, j) for j in range(1, rest)])
    groups_across = [[swap_core(piece) for piece in group] for group in groups_own]

    so_far = project(other_own, groups_own)
    query_sent, pair_sent = project(other_across, groups_across, qwidth, BF16, so_far)
    pair_from, query_from = swap_x(pair_sent), swap_x(query_sent)
    so_far = project(mine_own, groups_own)
    query, pair = project(mine_across, groups_across, qwidth, F32, so_far)
    pair = (pair + pair_from.astype(F32)).astype(BF16)

    doc_row, flag_row = doc_lengths[0], kept_flags[0]
    positions = place * local + lax.iota(jnp.int32, local)
    kept = kept_rows(doc_row, flag_row, positions)
    cot = jnp.where(kept[:, None] > 0, cotangent[0], jnp.zeros_like(cotangent[0]))

    pairs = [shift_seq(pair, j) for j in range(back, 0, -1)] + [pair]
    attention, dquery, dpair, dback = attend(doc_row, query, query_from, cot, pairs)

    dquery_other = swap_x(dquery)
    for j in range(1, back + 1):
        sent = dback[(back - j) * local : (back - j + 1) * local]
        dpair = dpair + shift_seq(sent, -j).astype(F32)
    dpair = dpair.astype(BF16)
    dpair_other = swap_x(dpair)

    left = [mine_own, other_own, swap_core(mine_across), swap_core(other_across)]
    right = [[mine, other, swap_core(mine), swap_core(other)] for mine, other in ((dquery, dquery_other), (dpair, dpair_other))]
    order = sorted(range(chips), key=lambda k: (k == 0, -min(k, chips - k), k))
    weights_grad = None
    for steps in (order[: chips // 2], order[chips // 2 :]):
        terms = weight_terms(steps, rest, width, left, *right)
        for i, k in enumerate(steps):
            part, *sent = terms[i * rest : (i + 1) * rest]
            for j, piece in enumerate(sent, 1):
                part = part + shift_rest(piece, -j).astype(F32)
            if k:
                part = shift_chip(part.astype(BF16), -k).astype(F32)
            weights_grad = part if weights_grad is None else weights_grad + part

    groups = groups_own + groups_across
    grad_from = swap_x(width_grad(dquery_other, dpair_other, groups))
    inputs_grad = merge_halves(width_grad(dquery, dpair, groups), grad_from, chips, rest, width)
    return (attention[None], inputs_grad[None], weights_grad)


def solution(mesh):
    in_specs = (
        P("dp", "seq", None),
        P("dp", None),
        P("dp", "seq", None),
        P("dp", None),
        P("dp", None),
    )
    out_specs = (P("dp", "seq", None), P("dp", "seq", None), P(("dp", "seq"), None))
    return jax.shard_map(shards, mesh=mesh, in_specs=in_specs, out_specs=out_specs, check_vma=False)
```

```python
import functools
import math

import jax
import jax.numpy as jnp
from jax import lax
from jax.experimental import pallas as pl
from jax.experimental.pallas import tpu as pltpu
from jax.sharding import PartitionSpec as P

HEAD_DIM = 128
PAIR = 2
CORES = 2
BF16 = jnp.bfloat16
F32 = jnp.float32
NT = (((1,), (1,)), ((), ()))
TN = (((0,), (0,)), ((), ()))
VMEM = pl.BlockSpec(memory_space=pltpu.VMEM)
SMEM = pl.BlockSpec(memory_space=pltpu.SMEM)


def dot(a, b, dims=(((1,), (0,)), ((), ()))):
    return lax.dot_general(a, b, dims, preferred_element_type=F32)


def swap_x(array):
    count = lax.axis_size("seq")
    return lax.ppermute(array, "seq", [(i, i ^ 1) for i in range(count)])


def shift_rest(array, step):
    count = lax.axis_size("seq")
    rest = count // PAIR
    pairs = [(i, PAIR * ((i // PAIR + step) % rest) + i % PAIR) for i in range(count)]
    return lax.ppermute(array, "seq", pairs)


def swap_core(array):
    count = lax.axis_size("dp")
    return lax.ppermute(array, "dp", [(i, i ^ 1) for i in range(count)])


def shift_chip(array, step):
    count = lax.axis_size("dp")
    chips = count // CORES
    pairs = [(i, CORES * ((i // CORES + step) % chips) + i % CORES) for i in range(count)]
    return lax.ppermute(array, "dp", pairs)


def shift_seq(array, step):
    count = lax.axis_size("seq")
    pairs = [(i, i + step) for i in range(count) if 0 <= i + step < count]
    return lax.ppermute(array, "seq", pairs)


def block_order(chips, rest, flip):
    dp_index, place = lax.axis_index("dp"), lax.axis_index("seq")
    chip, core = dp_index // CORES, dp_index % CORES
    around, x = place // PAIR, (place + flip) % PAIR
    order = []
    for c in range(CORES):
        for k in range(chips):
            for j in range(rest):
                shard = CORES * ((chip - k + chips) % chips) + (core + c) % CORES
                order.append(shard * (PAIR * rest) + PAIR * ((around - j + rest) % rest) + x)
    return order


def lanes(index, width):
    return pl.ds(pl.multiple_of(index * width, width), width)


def split_kernel(chips, rest, width, in_ref, held_ref, *out_refs):
    for flip in range(PAIR):
        for i, block in enumerate(block_order(chips, rest, flip)):
            out_refs[flip][:, i * width : (i + 1) * width] = in_ref[:, lanes(block, width)]
    out_refs[PAIR][...] = held_ref[...]


def split_tokens(tokens, held, chips, rest, width):
    rows, total = tokens.shape
    if width % 128:
        blocks = tokens.reshape(rows, total // width, width)
        order = jnp.stack(block_order(chips, rest, 0) + block_order(chips, rest, 1))
        return *jnp.split(jnp.take(blocks, order, axis=1).reshape(rows, total), PAIR, axis=1), held
    tile = min(rows, 128)
    half = pl.BlockSpec((tile, total // PAIR), lambda i: (i, 0))
    whole = pl.BlockSpec(held.shape, lambda i: (0, 0))
    return pl.pallas_call(
        functools.partial(split_kernel, chips, rest, width),
        grid=(rows // tile,),
        in_specs=[pl.BlockSpec((tile, total), lambda i: (i, 0)), whole],
        out_specs=[half] * PAIR + [whole],
        out_shape=[jax.ShapeDtypeStruct((rows, total // PAIR), tokens.dtype)] * PAIR
        + [jax.ShapeDtypeStruct(held.shape, held.dtype)],
        name="split_tokens",
    )(tokens, held)


def merge_kernel(chips, rest, width, mine_ref, other_ref, out_ref, sems):
    copies = []
    for flip, ref in enumerate((mine_ref, other_ref)):
        for i, block in enumerate(block_order(chips, rest, flip)):
            source = ref.at[:, pl.ds(i * width, width)]
            target = out_ref.at[:, lanes(block, width)]
            copies.append(pltpu.make_async_copy(source, target, sems.at[len(copies)]))
    for copy in copies:
        copy.start()
    for copy in copies:
        copy.wait()


def merge_halves(mine, other, chips, rest, width):
    rows, half = mine.shape
    count = PAIR * half // width
    if width % 128:
        order = jnp.stack(block_order(chips, rest, 0) + block_order(chips, rest, 1))
        where = jnp.zeros_like(order).at[order].set(lax.iota(order.dtype, count))
        blocks = jnp.concatenate([mine, other], axis=1).reshape(rows, count, width)
        return jnp.take(blocks, where, axis=1).reshape(rows, PAIR * half)
    return pl.pallas_call(
        functools.partial(merge_kernel, chips, rest, width),
        in_specs=[VMEM] * 2,
        out_specs=pl.BlockSpec(memory_space=pl.ANY),
        out_shape=jax.ShapeDtypeStruct((rows, PAIR * half), mine.dtype),
        scratch_shapes=[pltpu.SemaphoreType.DMA((count,))],
        compiler_params=pltpu.CompilerParams(vmem_limit_bytes=48 * 2**20),
        name="merge_halves",
    )(mine, other)


def project_kernel(first, span, per, qwidth, has_sum, tokens_ref, *refs):
    if has_sum:
        sum_ref, refs = refs[0], refs[1:]
        total = sum_ref[...]
    else:
        total = None
    pieces = refs[:-2] if qwidth else refs[:-1]
    for g in range(len(pieces) // per):
        rows = jnp.concatenate([r[...] for r in pieces[g * per : (g + 1) * per]], axis=0)
        term = dot(tokens_ref[:, (first + g) * span : (first + g + 1) * span], rows)
        total = term if total is None else total + term
    if qwidth:
        query_ref, pair_ref = refs[-2:]
        query_ref[...] = total[:, :qwidth].astype(query_ref.dtype)
        pair_ref[...] = total[:, qwidth:].astype(pair_ref.dtype)
    else:
        refs[-1][...] = total


def project(tokens, groups, first=0, qwidth=0, kind=F32, so_far=None):
    rows = tokens.shape[0]
    cols = groups[0][0].shape[1]
    pieces = [piece for group in groups for piece in group]
    span = sum(piece.shape[0] for piece in groups[0])
    widths = [qwidth, cols - qwidth] if qwidth else [cols]
    sums = [] if so_far is None else [so_far]
    outs = pl.pallas_call(
        functools.partial(project_kernel, first, span, len(groups[0]), qwidth, len(sums)),
        in_specs=[VMEM] * (1 + len(sums) + len(pieces)),
        out_specs=[VMEM] * len(widths),
        out_shape=[jax.ShapeDtypeStruct((rows, w), kind) for w in widths],
        compiler_params=pltpu.CompilerParams(vmem_limit_bytes=48 * 2**20),
        name="project",
    )(tokens, *sums, *pieces)
    return outs if qwidth else outs[0]


def grad_kernel(span, per, dquery_ref, dpair_ref, *refs):
    pieces, out_ref = refs[:-1], refs[-1]
    grads = jnp.concatenate([dquery_ref[...], dpair_ref[...]], axis=1)
    for k in range(len(pieces) // per):
        rows = jnp.concatenate([r[...] for r in pieces[k * per : (k + 1) * per]], axis=0)
        out_ref[:, k * span : (k + 1) * span] = dot(grads, rows, NT).astype(BF16)


def width_grad(dquery, dpair, groups):
    rows = dquery.shape[0]
    pieces = [piece for group in groups for piece in group]
    span = sum(piece.shape[0] for piece in groups[0])
    return pl.pallas_call(
        functools.partial(grad_kernel, span, len(groups[0])),
        in_specs=[VMEM] * (2 + len(pieces)),
        out_specs=VMEM,
        out_shape=jax.ShapeDtypeStruct((rows, span * len(groups)), BF16),
        compiler_params=pltpu.CompilerParams(vmem_limit_bytes=48 * 2**20),
        name="width_grad",
    )(dquery, dpair, *pieces)


def weight_kernel(steps, rest, width, count, *refs):
    tokens, dquery, dpair = refs[:count], refs[count : 2 * count], refs[2 * count : 3 * count]
    outs = refs[3 * count + 1 :]
    right = jnp.concatenate(
        [jnp.concatenate([q[...], p[...]], axis=1) for q, p in zip(dquery, dpair)], axis=0
    )
    span = rest * width
    for i, k in enumerate(steps):
        left = jnp.concatenate([t[:, k * span : (k + 1) * span] for t in tokens], axis=0)
        total = dot(left.T, right)
        for j in range(rest):
            out = outs[i * rest + j]
            out[...] = total[j * width : (j + 1) * width].astype(out.dtype)


def weight_terms(steps, rest, width, tokens, dquery, dpair, after):
    cols = dquery[0].shape[1] + dpair[0].shape[1]
    count = len(tokens)
    return pl.pallas_call(
        functools.partial(weight_kernel, steps, rest, width, count),
        in_specs=[VMEM] * (3 * count) + [pl.BlockSpec(memory_space=pl.ANY)],
        out_specs=[VMEM] * (len(steps) * rest),
        out_shape=[jax.ShapeDtypeStruct((width, cols), BF16 if j else F32) for _ in steps for j in range(rest)],
        compiler_params=pltpu.CompilerParams(vmem_limit_bytes=48 * 2**20),
        name="weight_terms",
    )(*tokens, *dquery, *dpair, after)


def attend_kernel(
    heads, back, docs_ref, q_ref, q_from_ref, cot_ref, *refs
):
    pair_refs, (out_ref, dq_ref, dpair_ref, dback_ref) = refs[: back + 1], refs[back + 1 :]
    rows = q_ref.shape[0]
    hd = HEAD_DIM
    scale = 1.0 / math.sqrt(hd)
    first = lax.axis_index("seq") * rows
    base = first - back * rows
    total = (back + 1) * rows

    row_pos = first + lax.broadcasted_iota(jnp.int32, (1, rows), 1)
    start_of = jnp.zeros((1, rows), jnp.int32)
    start = jnp.int32(0)
    for d in range(docs_ref.shape[0]):
        end = start + docs_ref[d]
        start_of = jnp.where((row_pos >= start) & (row_pos < end), start, start_of)
        start = end
    key_pos = base + lax.broadcasted_iota(jnp.int32, (total, rows), 0)
    allowed = (key_pos >= start_of) & (key_pos <= row_pos)

    pairs = [r[...] for r in pair_refs]
    keys = jnp.concatenate([p[:, :hd] for p in pairs], axis=0)
    values = jnp.concatenate([p[:, hd:] for p in pairs], axis=0)
    keys_t, values_t = keys.T, values.T
    dk = jnp.zeros((total, hd), F32)
    dv = jnp.zeros((total, hd), F32)
    for h in range(heads):
        cols = slice(h * hd, (h + 1) * hd)
        q = (q_ref[:, cols] + q_from_ref[:, cols].astype(F32)).astype(BF16)
        cot = cot_ref[:, cols]
        logits = jnp.where(allowed, dot(keys, q, NT) * scale, -1e30)
        top = jnp.max(logits, axis=0, keepdims=True)
        raised = jnp.exp(logits - top)
        probs = raised * (1.0 / jnp.sum(raised, axis=0, keepdims=True))
        probs_half = probs.astype(BF16)
        out_t = dot(values_t, probs_half).astype(BF16)
        cot_t = cot.T
        delta = jnp.sum(cot_t.astype(F32) * out_t.astype(F32), axis=0, keepdims=True)
        dscores = (probs * (dot(values, cot, NT) - delta)).astype(BF16)
        out_ref[:, cols] = out_t.T
        dq_ref[:, cols] = (dot(keys_t, dscores) * scale).astype(BF16).T
        dk += dot(dscores, q)
        dv += dot(probs_half, cot)
    both = jnp.concatenate([dk * scale, dv], axis=1)
    dpair_ref[...] = both[back * rows :]
    dback_ref[...] = both[: back * rows].astype(BF16)


def attend(docs, q, q_from, cot, pairs):
    rows, width = q.shape
    back = len(pairs) - 1
    two = 2 * HEAD_DIM
    return pl.pallas_call(
        functools.partial(attend_kernel, width // HEAD_DIM, back),
        in_specs=[SMEM] + [VMEM] * (back + 4),
        out_specs=[VMEM] * 4,
        out_shape=[
            jax.ShapeDtypeStruct((rows, width), BF16),
            jax.ShapeDtypeStruct((rows, width), BF16),
            jax.ShapeDtypeStruct((rows, two), F32),
            jax.ShapeDtypeStruct((back * rows, two), BF16),
        ],
        compiler_params=pltpu.CompilerParams(vmem_limit_bytes=48 * 2**20),
        name="attend",
    )(docs, q, q_from, cot, *pairs)


def kept_rows(doc_row, flag_row, positions):
    ends = jnp.cumsum(doc_row)
    starts = ends - doc_row
    inside = (positions[:, None] >= starts[None, :]) & (positions[:, None] < ends[None, :])
    return jnp.sum(jnp.where(inside, flag_row[None, :], 0), axis=1)


def shards(inputs, weights, cotangent, doc_lengths, kept_flags):
    seq_count = lax.axis_size("seq")
    chips = lax.axis_size("dp") // CORES
    rest = seq_count // PAIR
    place = lax.axis_index("seq")
    tokens = inputs[0]
    local = tokens.shape[0]
    qwidth = cotangent.shape[2]
    shard_rows, cols = weights.shape
    width = shard_rows // seq_count
    back = -(-(local * seq_count // 2 - 1) // local)

    blocks = weights.reshape(seq_count, width, cols)
    places = [PAIR * ((place // PAIR - j + rest) % rest) + place % PAIR for j in range(rest)]
    groups_own = [[lax.dynamic_index_in_dim(blocks, p, 0, keepdims=False) for p in places]]
    own = groups_own[0][0]
    farthest = chips // 2
    arrived = {farthest: shift_chip(own, farthest)}

    tokens_mine, tokens_sent, own = split_tokens(tokens, own, chips, rest, width)
    tokens_other = swap_x(tokens_sent)

    for k in range(1, chips):
        first = arrived[k] if k in arrived else shift_chip(own, k)
        groups_own.append([first] + [shift_rest(first, j) for j in range(1, rest)])
    groups_across = [[swap_core(piece) for piece in group] for group in groups_own]

    so_far = project(tokens_other, groups_own)
    query_sent, pair_sent = project(tokens_other, groups_across, chips, qwidth, BF16, so_far)
    pair_from, query_from = swap_x(pair_sent), swap_x(query_sent)
    so_far = project(tokens_mine, groups_own)
    query, pair = project(tokens_mine, groups_across, chips, qwidth, F32, so_far)
    pair = (pair + pair_from.astype(F32)).astype(BF16)

    doc_row, flag_row = doc_lengths[0], kept_flags[0]
    positions = place * local + lax.iota(jnp.int32, local)
    kept = kept_rows(doc_row, flag_row, positions)
    cot = jnp.where(kept[:, None] > 0, cotangent[0], jnp.zeros_like(cotangent[0]))

    pairs = [shift_seq(pair, j) for j in range(back, 0, -1)] + [pair]
    attention, dquery, dpair, dback = attend(doc_row, query, query_from, cot, pairs)

    dquery_other = swap_x(dquery)
    for j in range(1, back + 1):
        sent = dback[(back - j) * local : (back - j + 1) * local]
        dpair = dpair + shift_seq(sent, -j).astype(F32)
    dpair = dpair.astype(BF16)
    dpair_other = swap_x(dpair)

    groups = groups_own + groups_across
    grad_sent = width_grad(dquery_other, dpair_other, groups)
    grad_from = swap_x(grad_sent)

    half = chips * rest * width
    left = [tokens_mine, tokens_other, swap_core(tokens_mine[:, half:]), swap_core(tokens_other[:, half:])]
    right = [[mine, other, swap_core(mine), swap_core(other)] for mine, other in ((dquery, dquery_other), (dpair, dpair_other))]
    order = sorted(range(chips), key=lambda k: (k == 0, -min(k, chips - k), k))
    weights_grad, after = None, grad_sent
    for steps in (order[: chips // 2], order[chips // 2 :]):
        terms = weight_terms(steps, rest, width, left, *right, after)
        after = terms[-1]
        for i, k in enumerate(steps):
            part, *sent = terms[i * rest : (i + 1) * rest]
            for j, piece in enumerate(sent, 1):
                part = part + shift_rest(piece, -j).astype(F32)
            if k:
                part = shift_chip(part.astype(BF16), -k).astype(F32)
            weights_grad = part if weights_grad is None else weights_grad + part

    inputs_grad = merge_halves(width_grad(dquery, dpair, groups), grad_from, chips, rest, width)
    return (attention[None], inputs_grad[None], weights_grad)


def solution(mesh):
    in_specs = (
        P("dp", "seq", None),
        P("dp", None),
        P("dp", "seq", None),
        P("dp", None),
        P("dp", None),
    )
    out_specs = (P("dp", "seq", None), P("dp", "seq", None), P(("dp", "seq"), None))
    return jax.shard_map(shards, mesh=mesh, in_specs=in_specs, out_specs=out_specs, check_vma=False)
```

```python
import functools
import math

import jax
import jax.numpy as jnp
from jax import lax
from jax.experimental import pallas as pl
from jax.experimental.pallas import tpu as pltpu
from jax.sharding import PartitionSpec as P

HEAD_DIM = 128
PAIR = 2
CORES = 2
BF16 = jnp.bfloat16
F32 = jnp.float32
NT = (((1,), (1,)), ((), ()))
TN = (((0,), (0,)), ((), ()))
VMEM = pl.BlockSpec(memory_space=pltpu.VMEM)
SMEM = pl.BlockSpec(memory_space=pltpu.SMEM)


def dot(a, b, dims=(((1,), (0,)), ((), ()))):
    return lax.dot_general(a, b, dims, preferred_element_type=F32)


def swap_x(array):
    count = lax.axis_size("seq")
    return lax.ppermute(array, "seq", [(i, i ^ 1) for i in range(count)])


def shift_rest(array, step):
    count = lax.axis_size("seq")
    rest = count // PAIR
    pairs = [(i, PAIR * ((i // PAIR + step) % rest) + i % PAIR) for i in range(count)]
    return lax.ppermute(array, "seq", pairs)


def swap_core(array):
    count = lax.axis_size("dp")
    return lax.ppermute(array, "dp", [(i, i ^ 1) for i in range(count)])


def shift_chip(array, step):
    count = lax.axis_size("dp")
    chips = count // CORES
    pairs = [(i, CORES * ((i // CORES + step) % chips) + i % CORES) for i in range(count)]
    return lax.ppermute(array, "dp", pairs)


def shift_seq(array, step):
    count = lax.axis_size("seq")
    pairs = [(i, i + step) for i in range(count) if 0 <= i + step < count]
    return lax.ppermute(array, "seq", pairs)


def block_order(chips, rest, flip):
    dp_index, place = lax.axis_index("dp"), lax.axis_index("seq")
    chip, core = dp_index // CORES, dp_index % CORES
    around, x = place // PAIR, (place + flip) % PAIR
    order = []
    for c in range(CORES):
        for k in range(chips):
            for j in range(rest):
                shard = CORES * ((chip - k + chips) % chips) + (core + c) % CORES
                order.append(shard * (PAIR * rest) + PAIR * ((around - j + rest) % rest) + x)
    return order


def lanes(index, width):
    return pl.ds(pl.multiple_of(index * width, width), width)


def split_kernel(chips, rest, width, in_ref, weights_ref, *out_refs):
    own_ref = out_refs[-1]
    order = block_order(chips, rest, 0) + block_order(chips, rest, 1)
    for ref in out_refs[:-1]:
        for i in range(ref.shape[1] // width):
            ref[:, i * width : (i + 1) * width] = in_ref[:, lanes(order.pop(0), width)]

    @pl.when(pl.program_id(0) == 0)
    def _():
        own_ref[...] = weights_ref[lanes(lax.axis_index("seq"), width), :]


def own_places(rest):
    place = lax.axis_index("seq")
    return [PAIR * ((place // PAIR - j + rest) % rest) + place % PAIR for j in range(rest)]


def split_inputs(tokens, weights, chips, rest):
    (rows, total), (shard, cols) = tokens.shape, weights.shape
    width = shard // (PAIR * rest)
    half = total // PAIR
    few = half // 8
    widths = [half // CORES] * CORES + [half - few, few]
    if width % 128:
        blocks = tokens.reshape(rows, total // width, width)
        order = jnp.stack(block_order(chips, rest, 0) + block_order(chips, rest, 1))
        taken = jnp.take(blocks, order, axis=1).reshape(rows, total)
        own = lax.dynamic_index_in_dim(weights.reshape(PAIR * rest, width, cols), lax.axis_index("seq"), 0, keepdims=False)
        return *jnp.split(taken, [half // CORES, half, total - few], axis=1), own
    tile = min(rows, 128)
    own = pl.BlockSpec((width, cols), lambda i: (0, 0))
    return pl.pallas_call(
        functools.partial(split_kernel, chips, rest, width),
        grid=(rows // tile,),
        in_specs=[
            pl.BlockSpec((tile, total), lambda i: (i, 0)),
            pl.BlockSpec((shard, cols), lambda i: (0, 0)),
        ],
        out_specs=[pl.BlockSpec((tile, w), lambda i: (i, 0)) for w in widths] + [own],
        out_shape=[jax.ShapeDtypeStruct((rows, w), tokens.dtype) for w in widths]
        + [jax.ShapeDtypeStruct((width, cols), weights.dtype)],
        name="split_inputs",
    )(tokens, weights)


def merge_kernel(chips, rest, width, mine_ref, other_ref, out_ref, sems):
    copies = []
    for flip, ref in enumerate((mine_ref, other_ref)):
        for i, block in enumerate(block_order(chips, rest, flip)):
            source = ref.at[:, pl.ds(i * width, width)]
            target = out_ref.at[:, lanes(block, width)]
            copies.append(pltpu.make_async_copy(source, target, sems.at[len(copies)]))
    for copy in copies:
        copy.start()
    for copy in copies:
        copy.wait()


def merge_halves(mine, other, chips, rest, width):
    rows, half = mine.shape
    count = PAIR * half // width
    if width % 128:
        order = jnp.stack(block_order(chips, rest, 0) + block_order(chips, rest, 1))
        where = jnp.zeros_like(order).at[order].set(lax.iota(order.dtype, count))
        blocks = jnp.concatenate([mine, other], axis=1).reshape(rows, count, width)
        return jnp.take(blocks, where, axis=1).reshape(rows, PAIR * half)
    return pl.pallas_call(
        functools.partial(merge_kernel, chips, rest, width),
        in_specs=[VMEM] * 2,
        out_specs=pl.BlockSpec(memory_space=pl.ANY),
        out_shape=jax.ShapeDtypeStruct((rows, PAIR * half), mine.dtype),
        scratch_shapes=[pltpu.SemaphoreType.DMA((count,))],
        compiler_params=pltpu.CompilerParams(vmem_limit_bytes=20 * 2**20),
        name="merge_halves",
    )(mine, other)


def cut(parts, first, step):
    for part in parts:
        if first < part.shape[1]:
            return part[:, first : first + step]
        first -= part.shape[1]


def project_kernel(span, per, qwidth, count, *refs):
    tokens, pieces, (query_ref, pair_ref) = refs[:count], refs[count:-2], refs[-2:]
    total = None
    for g in range(len(pieces) // per):
        rows = jnp.concatenate([r[...] for r in pieces[g * per : (g + 1) * per]], axis=0)
        term = dot(cut(tokens, g * span, span), rows)
        total = term if total is None else total + term
    query_ref[...] = total[:, :qwidth].astype(query_ref.dtype)
    pair_ref[...] = total[:, qwidth:].astype(pair_ref.dtype)


def project(tokens, groups, qwidth, kind):
    rows = tokens[0].shape[0]
    cols = groups[0][0].shape[1]
    pieces = [piece for group in groups for piece in group]
    span = sum(piece.shape[0] for piece in groups[0])
    return pl.pallas_call(
        functools.partial(project_kernel, span, len(groups[0]), qwidth, len(tokens)),
        in_specs=[VMEM] * (len(tokens) + len(pieces)),
        out_specs=[VMEM] * 2,
        out_shape=[jax.ShapeDtypeStruct((rows, w), kind) for w in (qwidth, cols - qwidth)],
        compiler_params=pltpu.CompilerParams(vmem_limit_bytes=20 * 2**20),
        name="project",
    )(*tokens, *pieces)


def grad_kernel(span, per, dquery_ref, dpair_ref, *refs):
    pieces, (out_ref, mark_ref) = refs[:-2], refs[-2:]
    grads = jnp.concatenate([dquery_ref[...], dpair_ref[...]], axis=1)
    for k in range(len(pieces) // per):
        rows = jnp.concatenate([r[...] for r in pieces[k * per : (k + 1) * per]], axis=0)
        out_ref[:, k * span : (k + 1) * span] = dot(grads, rows, NT).astype(BF16)
    mark_ref[...] = grads[:16, :128]


def width_grad(dquery, dpair, groups):
    rows = dquery.shape[0]
    pieces = [piece for group in groups for piece in group]
    span = sum(piece.shape[0] for piece in groups[0])
    return pl.pallas_call(
        functools.partial(grad_kernel, span, len(groups[0])),
        in_specs=[VMEM] * (2 + len(pieces)),
        out_specs=[VMEM] * 2,
        out_shape=[jax.ShapeDtypeStruct((rows, span * len(groups)), BF16), jax.ShapeDtypeStruct((16, 128), BF16)],
        compiler_params=pltpu.CompilerParams(vmem_limit_bytes=20 * 2**20),
        name="width_grad",
    )(dquery, dpair, *pieces)


def weight_kernel(steps, rest, width, sources, grads, *refs):
    tokens = []
    for count, _ in sources:
        tokens.append(refs[:count])
        refs = refs[count:]
    right = [jnp.concatenate([r[...] for r in refs[i : i + grads]], axis=1) for i in range(0, grads * len(sources), grads)]
    right = jnp.concatenate(right, axis=0)
    outs = refs[grads * len(sources) + 1 :]
    span = rest * width
    for i, k in enumerate(steps):
        left = jnp.concatenate([cut(t, first + k * span, span) for t, (_, first) in zip(tokens, sources)], axis=0)
        total = dot(left.T, right)
        for j in range(rest):
            out = outs[i * rest + j]
            out[...] = total[j * width : (j + 1) * width].astype(out.dtype)


def weight_terms(steps, rest, width, tokens, grads, after):
    cols = sum(g.shape[1] for g in grads[0])
    sources = [(len(parts), first) for parts, first in tokens]
    parts = [part for group, _ in tokens for part in group]
    given = [g for group in grads for g in group]
    return pl.pallas_call(
        functools.partial(weight_kernel, steps, rest, width, sources, len(grads[0])),
        in_specs=[VMEM] * (len(parts) + len(given) + 1),
        out_specs=[VMEM] * (len(steps) * rest),
        out_shape=[jax.ShapeDtypeStruct((width, cols), BF16 if j else F32) for _ in steps for j in range(rest)],
        compiler_params=pltpu.CompilerParams(vmem_limit_bytes=20 * 2**20),
        name="weight_terms",
    )(*parts, *given, after)


def attend_kernel(
    heads, back, docs_ref, q_ref, q_from_ref, cot_ref, *refs
):
    pair_refs, (out_ref, dq_ref, dpair_ref, dback_ref) = refs[: back + 1], refs[back + 1 :]
    rows = q_ref.shape[0]
    hd = HEAD_DIM
    scale = 1.0 / math.sqrt(hd)
    first = lax.axis_index("seq") * rows
    base = first - back * rows
    total = (back + 1) * rows

    row_pos = first + lax.broadcasted_iota(jnp.int32, (1, rows), 1)
    start_of = jnp.zeros((1, rows), jnp.int32)
    start = jnp.int32(0)
    for d in range(docs_ref.shape[0]):
        end = start + docs_ref[d]
        start_of = jnp.where((row_pos >= start) & (row_pos < end), start, start_of)
        start = end
    key_pos = base + lax.broadcasted_iota(jnp.int32, (total, rows), 0)
    allowed = (key_pos >= start_of) & (key_pos <= row_pos)

    pairs = [r[...] for r in pair_refs]
    keys = jnp.concatenate([p[:, :hd] for p in pairs], axis=0)
    values = jnp.concatenate([p[:, hd:] for p in pairs], axis=0)
    keys_t, values_t = keys.T, values.T
    dk = jnp.zeros((total, hd), F32)
    dv = jnp.zeros((total, hd), F32)
    for h in range(heads):
        cols = slice(h * hd, (h + 1) * hd)
        q = (q_ref[:, cols] + q_from_ref[:, cols].astype(F32)).astype(BF16)
        cot = cot_ref[:, cols]
        logits = jnp.where(allowed, dot(keys, q, NT) * scale, -1e30)
        top = jnp.max(logits, axis=0, keepdims=True)
        raised = jnp.exp(logits - top)
        probs = raised * (1.0 / jnp.sum(raised, axis=0, keepdims=True))
        probs_half = probs.astype(BF16)
        out_t = dot(values_t, probs_half).astype(BF16)
        cot_t = cot.T
        delta = jnp.sum(cot_t.astype(F32) * out_t.astype(F32), axis=0, keepdims=True)
        dscores = (probs * (dot(values, cot, NT) - delta)).astype(BF16)
        out_ref[:, cols] = out_t.T
        dq_ref[:, cols] = (dot(keys_t, dscores) * scale).astype(BF16).T
        dk += dot(dscores, q)
        dv += dot(probs_half, cot)
    both = jnp.concatenate([dk * scale, dv], axis=1)
    dpair_ref[...] = both[back * rows :]
    dback_ref[...] = both[: back * rows].astype(BF16)


def attend(docs, q, q_from, cot, pairs):
    rows, width = q.shape
    back = len(pairs) - 1
    two = 2 * HEAD_DIM
    return pl.pallas_call(
        functools.partial(attend_kernel, width // HEAD_DIM, back),
        in_specs=[SMEM] + [VMEM] * (back + 4),
        out_specs=[VMEM] * 4,
        out_shape=[
            jax.ShapeDtypeStruct((rows, width), BF16),
            jax.ShapeDtypeStruct((rows, width), BF16),
            jax.ShapeDtypeStruct((rows, two), F32),
            jax.ShapeDtypeStruct((back * rows, two), BF16),
        ],
        compiler_params=pltpu.CompilerParams(vmem_limit_bytes=20 * 2**20),
        name="attend",
    )(docs, q, q_from, cot, *pairs)


def kept_rows(doc_row, flag_row, positions):
    ends = jnp.cumsum(doc_row)
    starts = ends - doc_row
    inside = (positions[:, None] >= starts[None, :]) & (positions[:, None] < ends[None, :])
    return jnp.sum(jnp.where(inside, flag_row[None, :], 0), axis=1)


def shards(inputs, weights, cotangent, doc_lengths, kept_flags):
    seq_count = lax.axis_size("seq")
    chips = lax.axis_size("dp") // CORES
    rest = seq_count // PAIR
    place = lax.axis_index("seq")
    tokens = inputs[0]
    local = tokens.shape[0]
    qwidth = cotangent.shape[2]
    shard_rows, cols = weights.shape
    width = shard_rows // seq_count
    back = -(-(local * seq_count // 2 - 1) // local)

    mine_own, mine_across, *sent, own = split_inputs(tokens, weights, chips, rest)
    tokens_mine = [mine_own, mine_across]
    tokens_other = [swap_x(part) for part in sent]

    blocks = weights.reshape(seq_count, width, cols)
    groups_own = [[lax.dynamic_index_in_dim(blocks, p, 0, keepdims=False) for p in own_places(rest)]]
    arrived = {}
    for k in sorted(range(1, chips), key=lambda k: (-abs(2 * k - chips), k)):
        first = shift_chip(own, k)
        if k == chips // 2:
            first, arrived = lax.optimization_barrier((first, arrived))
        arrived[k] = [first] + [shift_rest(first, j) for j in range(1, rest)]
    groups_own += [arrived[k] for k in range(1, chips)]
    groups_across = [[swap_core(piece) for piece in group] for group in groups_own]
    groups = groups_own + groups_across

    query_sent, pair_sent = project(tokens_other, groups, qwidth, BF16)
    pair_from, query_from = swap_x(pair_sent), swap_x(query_sent)
    query, pair = project(tokens_mine, groups, qwidth, F32)
    pair = (pair + pair_from.astype(F32)).astype(BF16)

    doc_row, flag_row = doc_lengths[0], kept_flags[0]
    positions = place * local + lax.iota(jnp.int32, local)
    kept = kept_rows(doc_row, flag_row, positions)
    cot = jnp.where(kept[:, None] > 0, cotangent[0], jnp.zeros_like(cotangent[0]))

    pairs = [shift_seq(pair, j) for j in range(back, 0, -1)] + [pair]
    attention, dquery, dpair, dback = attend(doc_row, query, query_from, cot, pairs)

    dquery_other = swap_x(dquery)
    for j in range(1, back + 1):
        sent = dback[(back - j) * local : (back - j + 1) * local]
        dpair = dpair + shift_seq(sent, -j).astype(F32)
    dpair = dpair.astype(BF16)
    dpair_other = swap_x(dpair)

    grad_sent, after = width_grad(dquery_other, dpair_other, groups)
    grad_from = swap_x(grad_sent)

    half = chips * rest * width
    across = [swap_core(part) for part in tokens_other]
    left = [(tokens_mine, 0), (tokens_other, 0), ([swap_core(mine_across)], 0), (across, half)]
    right = [[dquery, dpair], [dquery_other, dpair_other]]
    right += [[swap_core(g) for g in group] for group in right]
    order = sorted(range(chips), key=lambda k: (k == 0, -min(k, chips - k), k))
    parts = []
    for steps in (order[: chips // 2], order[chips // 2 :]):
        terms = weight_terms(steps, rest, width, left, right, after)
        after = terms[-1]
        for i, k in enumerate(steps):
            part, *sent = terms[i * rest : (i + 1) * rest]
            for j, piece in enumerate(sent, 1):
                part = part + shift_rest(piece, -j).astype(F32)
            if k:
                part = shift_chip(part.astype(BF16), -k).astype(F32)
            parts.append(part)
    weights_grad = functools.reduce(jnp.add, reversed(parts))

    inputs_grad = merge_halves(width_grad(dquery, dpair, groups)[0], grad_from, chips, rest, width)
    return (attention[None], inputs_grad[None], weights_grad)


def solution(mesh):
    in_specs = (
        P("dp", "seq", None),
        P("dp", None),
        P("dp", "seq", None),
        P("dp", None),
        P("dp", None),
    )
    out_specs = (P("dp", "seq", None), P("dp", "seq", None), P(("dp", "seq"), None))
    return jax.shard_map(shards, mesh=mesh, in_specs=in_specs, out_specs=out_specs, check_vma=False)
```

```python
import functools
import math

import jax
import jax.numpy as jnp
from jax import lax
from jax.experimental import pallas as pl
from jax.experimental.pallas import tpu as pltpu
from jax.sharding import PartitionSpec as P

HEAD_DIM = 128
PAIR = 2
CORES = 2
BF16 = jnp.bfloat16
F32 = jnp.float32
NT = (((1,), (1,)), ((), ()))
TN = (((0,), (0,)), ((), ()))
VMEM = pl.BlockSpec(memory_space=pltpu.VMEM)
SMEM = pl.BlockSpec(memory_space=pltpu.SMEM)


def dot(a, b, dims=(((1,), (0,)), ((), ()))):
    return lax.dot_general(a, b, dims, preferred_element_type=F32)


def swap_x(array):
    count = lax.axis_size("seq")
    return lax.ppermute(array, "seq", [(i, i ^ 1) for i in range(count)])


def shift_rest(array, step):
    count = lax.axis_size("seq")
    rest = count // PAIR
    pairs = [(i, PAIR * ((i // PAIR + step) % rest) + i % PAIR) for i in range(count)]
    return lax.ppermute(array, "seq", pairs)


def swap_core(array):
    count = lax.axis_size("dp")
    return lax.ppermute(array, "dp", [(i, i ^ 1) for i in range(count)])


def shift_chip(array, step):
    count = lax.axis_size("dp")
    chips = count // CORES
    pairs = [(i, CORES * ((i // CORES + step) % chips) + i % CORES) for i in range(count)]
    return lax.ppermute(array, "dp", pairs)


def shift_seq(array, step):
    count = lax.axis_size("seq")
    pairs = [(i, i + step) for i in range(count) if 0 <= i + step < count]
    return lax.ppermute(array, "seq", pairs)


def block_order(chips, rest, flip, steps):
    dp_index, place = lax.axis_index("dp"), lax.axis_index("seq")
    chip, core = dp_index // CORES, dp_index % CORES
    around, x = place // PAIR, (place + flip) % PAIR
    order = []
    for c in range(CORES):
        for k in steps:
            for j in range(rest):
                shard = CORES * ((chip - k + chips) % chips) + (core + c) % CORES
                order.append(shard * (PAIR * rest) + PAIR * ((around - j + rest) % rest) + x)
    return order


def whole_order(chips, rest):
    far = range(1, chips)
    return [block_order(chips, rest, flip, steps) for flip, steps in ((0, range(chips)), (1, far), (1, range(1)))]


def split_order(chips, rest):
    mine, *others = whole_order(chips, rest)
    half = len(mine) // CORES
    return [mine[:half], mine[half:], *others]


def lanes(index, width):
    return pl.ds(pl.multiple_of(index * width, width), width)


def split_kernel(chips, rest, width, tokens_ref, *out_refs):
    for ref, order in zip(out_refs, split_order(chips, rest)):
        for i, block in enumerate(order):
            ref[:, i * width : (i + 1) * width] = tokens_ref[:, lanes(block, width)]


def own_places(rest, flip):
    place = lax.axis_index("seq")
    return [PAIR * ((place // PAIR - j + rest) % rest) + (place + flip) % PAIR for j in range(rest)]


def split_tokens(tokens, chips, rest, width):
    rows, total = tokens.shape
    half = total // PAIR
    near = half // chips
    widths = [half // CORES] * CORES + [half - near, near]
    if width % 128:
        order = jnp.stack(sum(whole_order(chips, rest), []))
        taken = jnp.take(tokens.reshape(rows, total // width, width), order, axis=1).reshape(rows, total)
        return jnp.split(taken, [half // CORES, half, total - near], axis=1)
    tile = min(rows, 128)
    return pl.pallas_call(
        functools.partial(split_kernel, chips, rest, width),
        grid=(rows // tile,),
        in_specs=[pl.BlockSpec((tile, total), lambda i: (i, 0))],
        out_specs=[pl.BlockSpec((tile, w), lambda i: (i, 0)) for w in widths],
        out_shape=[jax.ShapeDtypeStruct((rows, w), tokens.dtype) for w in widths],
        name="split_tokens",
    )(tokens)


def merge_kernel(chips, rest, width, *refs):
    in_refs, out_ref, sems = refs[:-2], refs[-2], refs[-1]
    copies = []
    for ref, order in zip(in_refs, whole_order(chips, rest)):
        for i, block in enumerate(order):
            source = ref.at[:, pl.ds(i * width, width)]
            target = out_ref.at[:, lanes(block, width)]
            copies.append(pltpu.make_async_copy(source, target, sems.at[len(copies)]))
    for copy in copies:
        copy.start()
    for copy in copies:
        copy.wait()


def merge_parts(parts, chips, rest, width):
    rows = parts[0].shape[0]
    total = sum(part.shape[1] for part in parts)
    count = total // width
    if width % 128:
        order = jnp.stack(sum(whole_order(chips, rest), []))
        where = jnp.zeros_like(order).at[order].set(lax.iota(order.dtype, count))
        blocks = jnp.concatenate(parts, axis=1).reshape(rows, count, width)
        return jnp.take(blocks, where, axis=1).reshape(rows, total)
    return pl.pallas_call(
        functools.partial(merge_kernel, chips, rest, width),
        in_specs=[VMEM] * len(parts),
        out_specs=pl.BlockSpec(memory_space=pl.ANY),
        out_shape=jax.ShapeDtypeStruct((rows, total), BF16),
        scratch_shapes=[pltpu.SemaphoreType.DMA((count,))],
        compiler_params=pltpu.CompilerParams(vmem_limit_bytes=20 * 2**20),
        name="merge_parts",
    )(*parts)


def cut(parts, first, step):
    for part in parts:
        if first < part.shape[1]:
            return part[:, first : first + step]
        first -= part.shape[1]


def project_kernel(span, per, qwidth, count, *refs):
    tokens, pieces, (query_ref, pair_ref) = refs[:count], refs[count:-2], refs[-2:]
    total = None
    for g in range(len(pieces) // per):
        rows = jnp.concatenate([r[...] for r in pieces[g * per : (g + 1) * per]], axis=0)
        term = dot(cut(tokens, g * span, span), rows)
        total = term if total is None else total + term
    query_ref[...] = total[:, :qwidth].astype(query_ref.dtype)
    pair_ref[...] = total[:, qwidth:].astype(pair_ref.dtype)


def project(tokens, groups, qwidth, kind):
    rows = tokens[0].shape[0]
    cols = groups[0][0].shape[1]
    pieces = [piece for group in groups for piece in group]
    span = sum(piece.shape[0] for piece in groups[0])
    return pl.pallas_call(
        functools.partial(project_kernel, span, len(groups[0]), qwidth, len(tokens)),
        in_specs=[VMEM] * (len(tokens) + len(pieces)),
        out_specs=[VMEM] * 2,
        out_shape=[jax.ShapeDtypeStruct((rows, w), kind) for w in (qwidth, cols - qwidth)],
        compiler_params=pltpu.CompilerParams(vmem_limit_bytes=20 * 2**20),
        name="project",
    )(*tokens, *pieces)


def grad_kernel(span, counts, dquery_ref, dpair_ref, *refs):
    pieces, outs, mark_ref = refs[: -len(counts) - 1], refs[-len(counts) - 1 : -1], refs[-1]
    grads = jnp.concatenate([dquery_ref[...], dpair_ref[...]], axis=1)
    per = len(pieces) // sum(counts)
    for out_ref, count in zip(outs, counts):
        for i in range(count):
            rows = jnp.concatenate([r[...] for r in pieces[:per]], axis=0)
            pieces = pieces[per:]
            out_ref[:, i * span : (i + 1) * span] = dot(grads, rows, NT).astype(BF16)
    mark_ref[...] = grads[:16, :128]


def width_grad(dquery, dpair, parts):
    rows = dquery.shape[0]
    pieces = [piece for groups in parts for group in groups for piece in group]
    span = sum(piece.shape[0] for piece in parts[0][0])
    counts = [len(groups) for groups in parts]
    return pl.pallas_call(
        functools.partial(grad_kernel, span, counts),
        in_specs=[VMEM] * (2 + len(pieces)),
        out_specs=[VMEM] * (len(parts) + 1),
        out_shape=[jax.ShapeDtypeStruct((rows, span * count), BF16) for count in counts]
        + [jax.ShapeDtypeStruct((16, 128), BF16)],
        compiler_params=pltpu.CompilerParams(vmem_limit_bytes=20 * 2**20),
        name="width_grad",
    )(dquery, dpair, *pieces)


def weight_kernel(steps, rest, width, chips, sources, grads, *refs):
    tokens, refs = refs[: sum(sources)], refs[sum(sources) :]
    rights = [jnp.concatenate([r[...] for r in refs[i : i + grads]], axis=1) for i in range(0, grads * len(sources), grads)]
    right = jnp.concatenate(rights, axis=0)
    outs = refs[grads * len(sources) + 1 :]
    span = rest * width
    for i, k in enumerate(steps):
        left, at = [], 0
        for core, count in enumerate(sources):
            parts, at = tokens[at : at + count], at + count
            if count == 1:
                left.append(parts[0][:, k * span : (k + 1) * span])
            else:
                far, near = parts
                across = core // CORES
                first = across if k == 0 else across * (chips - 1) + k - 1
                left.append((far if k else near)[:, first * span : (first + 1) * span])
        total = dot(jnp.concatenate(left, axis=0).T, right)
        for j in range(rest):
            out = outs[i * rest + j]
            out[...] = total[j * width : (j + 1) * width].astype(out.dtype)


def weight_terms(steps, rest, width, chips, tokens, grads, after):
    cols = sum(g.shape[1] for g in grads[0])
    sources = [len(parts) for parts in tokens]
    parts = [part for group in tokens for part in group]
    given = [g for group in grads for g in group]
    return pl.pallas_call(
        functools.partial(weight_kernel, steps, rest, width, chips, sources, len(grads[0])),
        in_specs=[VMEM] * (len(parts) + len(given) + 1),
        out_specs=[VMEM] * (len(steps) * rest),
        out_shape=[jax.ShapeDtypeStruct((width, cols), BF16 if j else F32) for _ in steps for j in range(rest)],
        compiler_params=pltpu.CompilerParams(vmem_limit_bytes=20 * 2**20),
        name="weight_terms",
    )(*parts, *given, after)


def attend_kernel(
    heads, back, docs_ref, q_ref, q_from_ref, cot_ref, *refs
):
    pair_refs, (out_ref, dq_ref, dpair_ref, dback_ref) = refs[: back + 1], refs[back + 1 :]
    rows = q_ref.shape[0]
    hd = HEAD_DIM
    scale = 1.0 / math.sqrt(hd)
    first = lax.axis_index("seq") * rows
    base = first - back * rows
    total = (back + 1) * rows

    row_pos = first + lax.broadcasted_iota(jnp.int32, (1, rows), 1)
    start_of = jnp.zeros((1, rows), jnp.int32)
    start = jnp.int32(0)
    for d in range(docs_ref.shape[0]):
        end = start + docs_ref[d]
        start_of = jnp.where((row_pos >= start) & (row_pos < end), start, start_of)
        start = end
    key_pos = base + lax.broadcasted_iota(jnp.int32, (total, rows), 0)
    allowed = (key_pos >= start_of) & (key_pos <= row_pos)

    pairs = [r[...] for r in pair_refs]
    keys = jnp.concatenate([p[:, :hd] for p in pairs], axis=0)
    values = jnp.concatenate([p[:, hd:] for p in pairs], axis=0)
    keys_t, values_t = keys.T, values.T
    dk = jnp.zeros((total, hd), F32)
    dv = jnp.zeros((total, hd), F32)
    for h in range(heads):
        cols = slice(h * hd, (h + 1) * hd)
        q = (q_ref[:, cols] + q_from_ref[:, cols].astype(F32)).astype(BF16)
        cot = cot_ref[:, cols]
        logits = jnp.where(allowed, dot(keys, q, NT) * scale, -1e30)
        top = jnp.max(logits, axis=0, keepdims=True)
        raised = jnp.exp(logits - top)
        probs = raised * (1.0 / jnp.sum(raised, axis=0, keepdims=True))
        probs_half = probs.astype(BF16)
        out_t = dot(values_t, probs_half).astype(BF16)
        cot_t = cot.T
        delta = jnp.sum(cot_t.astype(F32) * out_t.astype(F32), axis=0, keepdims=True)
        dscores = (probs * (dot(values, cot, NT) - delta)).astype(BF16)
        out_ref[:, cols] = out_t.T
        dq_ref[:, cols] = (dot(keys_t, dscores) * scale).astype(BF16).T
        dk += dot(dscores, q)
        dv += dot(probs_half, cot)
    both = jnp.concatenate([dk * scale, dv], axis=1)
    dpair_ref[...] = both[back * rows :]
    dback_ref[...] = both[: back * rows].astype(BF16)


def attend(docs, q, q_from, cot, pairs):
    rows, width = q.shape
    back = len(pairs) - 1
    two = 2 * HEAD_DIM
    return pl.pallas_call(
        functools.partial(attend_kernel, width // HEAD_DIM, back),
        in_specs=[SMEM] + [VMEM] * (back + 4),
        out_specs=[VMEM] * 4,
        out_shape=[
            jax.ShapeDtypeStruct((rows, width), BF16),
            jax.ShapeDtypeStruct((rows, width), BF16),
            jax.ShapeDtypeStruct((rows, two), F32),
            jax.ShapeDtypeStruct((back * rows, two), BF16),
        ],
        compiler_params=pltpu.CompilerParams(vmem_limit_bytes=20 * 2**20),
        name="attend",
    )(docs, q, q_from, cot, *pairs)


def kept_rows(doc_row, flag_row, positions):
    ends = jnp.cumsum(doc_row)
    starts = ends - doc_row
    inside = (positions[:, None] >= starts[None, :]) & (positions[:, None] < ends[None, :])
    return jnp.sum(jnp.where(inside, flag_row[None, :], 0), axis=1)


def shards(inputs, weights, cotangent, doc_lengths, kept_flags):
    seq_count = lax.axis_size("seq")
    chips = lax.axis_size("dp") // CORES
    rest = seq_count // PAIR
    place = lax.axis_index("seq")
    tokens = inputs[0]
    local = tokens.shape[0]
    qwidth = cotangent.shape[2]
    shard_rows, cols = weights.shape
    width = shard_rows // seq_count
    back = -(-(local * seq_count // 2 - 1) // local)

    own = lax.dynamic_slice_in_dim(weights, place * width, width, 0)
    mine_own, mine_across, sent, near = split_tokens(tokens, chips, rest, width)

    blocks, near = lax.optimization_barrier((weights, near))
    blocks = blocks.reshape(seq_count, width, cols)
    groups_own, groups_near = [
        [[lax.dynamic_index_in_dim(blocks, p, 0, keepdims=False) for p in own_places(rest, flip)]] for flip in range(PAIR)
    ]
    arrived = {}
    for k in sorted(range(1, chips), key=lambda k: (-abs(2 * k - chips), k)):
        first = shift_chip(own, k)
        if not arrived:
            first, sent = lax.optimization_barrier((first, sent))
        if k == chips // 2:
            first, arrived = lax.optimization_barrier((first, arrived))
        arrived[k] = [first] + [shift_rest(first, j) for j in range(1, rest)]
    far_other = swap_x(sent)
    groups_own += [arrived[k] for k in range(1, chips)]
    last = groups_own[chips // 2]
    last[-1], far_other = lax.optimization_barrier((last[-1], far_other))
    groups_across = [[swap_core(piece) for piece in group] for group in groups_own]
    groups_near.append([swap_core(piece) for piece in groups_near[0]])
    groups = groups_own + groups_across
    groups_far = groups_own[1:] + groups_across[1:]

    query_sent, pair_sent = project([far_other], groups_far, qwidth, BF16)
    query_sent, near_other = lax.optimization_barrier((query_sent, swap_x(near)))
    pair_from, query_from = swap_x(pair_sent), swap_x(query_sent)
    query, pair = project([mine_own, mine_across, near], groups + groups_near, qwidth, F32)
    pair = (pair + pair_from.astype(F32)).astype(BF16)

    doc_row, flag_row = doc_lengths[0], kept_flags[0]
    positions = place * local + lax.iota(jnp.int32, local)
    kept = kept_rows(doc_row, flag_row, positions)
    cot = jnp.where(kept[:, None] > 0, cotangent[0], jnp.zeros_like(cotangent[0]))

    pairs = [shift_seq(pair, j) for j in range(back, 0, -1)] + [pair]
    attention, dquery, dpair, dback = attend(doc_row, query, query_from, cot, pairs)

    dquery_other = swap_x(dquery)
    for j in range(1, back + 1):
        sent = dback[(back - j) * local : (back - j + 1) * local]
        dpair = dpair + shift_seq(sent, -j).astype(F32)
    dpair = dpair.astype(BF16)
    dpair_other = swap_x(dpair)

    left = [[mine_own], [far_other, near_other]]
    left += [[swap_core(mine_across)], [swap_core(far_other), swap_core(near_other)]]
    right = [[dquery, dpair], [dquery_other, dpair_other]]
    right += [[swap_core(g) for g in group] for group in right]
    order = sorted(range(chips), key=lambda k: (k == 0, -min(k, chips - k), k))
    parts, after = [], dpair
    for steps in (order[: chips // 2], order[chips // 2 :]):
        terms = weight_terms(steps, rest, width, chips, left, right, after)
        if not parts:
            grad_sent, after = width_grad(dquery_other, dpair_other, [groups_far])
            grad_from = swap_x(grad_sent)
        for i, k in enumerate(steps):
            part, *sent = terms[i * rest : (i + 1) * rest]
            for j, piece in enumerate(sent, 1):
                part = part + shift_rest(piece, -j).astype(F32)
            if k:
                part = shift_chip(part.astype(BF16), -k).astype(F32)
            parts.append(part)
    weights_grad = functools.reduce(jnp.add, reversed(parts))

    grad_mine, grad_near, _ = width_grad(dquery, dpair, [groups, groups_near])
    inputs_grad = merge_parts([grad_mine, grad_from, grad_near], chips, rest, width)
    return (attention[None], inputs_grad[None], weights_grad)


def solution(mesh):
    in_specs = (
        P("dp", "seq", None),
        P("dp", None),
        P("dp", "seq", None),
        P("dp", None),
        P("dp", None),
    )
    out_specs = (P("dp", "seq", None), P("dp", "seq", None), P(("dp", "seq"), None))
    return jax.shard_map(shards, mesh=mesh, in_specs=in_specs, out_specs=out_specs, check_vma=False)
```

```python
import functools
import math

import jax
import jax.numpy as jnp
from jax import lax
from jax.experimental import pallas as pl
from jax.experimental.pallas import tpu as pltpu
from jax.sharding import PartitionSpec as P

HEAD_DIM = 128
PAIR = 2
CORES = 2
BF16 = jnp.bfloat16
F32 = jnp.float32
NT = (((1,), (1,)), ((), ()))
TN = (((0,), (0,)), ((), ()))
VMEM = pl.BlockSpec(memory_space=pltpu.VMEM)
SMEM = pl.BlockSpec(memory_space=pltpu.SMEM)


def dot(a, b, dims=(((1,), (0,)), ((), ()))):
    return lax.dot_general(a, b, dims, preferred_element_type=F32)


def swap_x(array):
    count = lax.axis_size("seq")
    return lax.ppermute(array, "seq", [(i, i ^ 1) for i in range(count)])


def shift_rest(array, step):
    count = lax.axis_size("seq")
    rest = count // PAIR
    pairs = [(i, PAIR * ((i // PAIR + step) % rest) + i % PAIR) for i in range(count)]
    return lax.ppermute(array, "seq", pairs)


def swap_core(array):
    count = lax.axis_size("dp")
    return lax.ppermute(array, "dp", [(i, i ^ 1) for i in range(count)])


def shift_chip(array, step):
    count = lax.axis_size("dp")
    chips = count // CORES
    pairs = [(i, CORES * ((i // CORES + step) % chips) + i % CORES) for i in range(count)]
    return lax.ppermute(array, "dp", pairs)


def shift_seq(array, step):
    count = lax.axis_size("seq")
    pairs = [(i, i + step) for i in range(count) if 0 <= i + step < count]
    return lax.ppermute(array, "seq", pairs)


def block_order(chips, rest, flip, steps):
    dp_index, place = lax.axis_index("dp"), lax.axis_index("seq")
    chip, core = dp_index // CORES, dp_index % CORES
    around, x = place // PAIR, (place + flip) % PAIR
    order = []
    for c in range(CORES):
        for k in steps:
            for j in range(rest):
                shard = CORES * ((chip - k + chips) % chips) + (core + c) % CORES
                order.append(shard * (PAIR * rest) + PAIR * ((around - j + rest) % rest) + x)
    return order


def whole_order(chips, rest):
    far = range(1, chips)
    return [block_order(chips, rest, flip, steps) for flip, steps in ((0, range(chips)), (1, far), (1, range(1)))]


def split_order(chips, rest):
    mine, *others = whole_order(chips, rest)
    half = len(mine) // CORES
    return [mine[:half], mine[half:], *others]


def lanes(index, width):
    return pl.ds(pl.multiple_of(index * width, width), width)


def split_kernel(chips, rest, width, tokens_ref, *out_refs):
    for ref, order in zip(out_refs, split_order(chips, rest)):
        for i, block in enumerate(order):
            ref[:, i * width : (i + 1) * width] = tokens_ref[:, lanes(block, width)]


def own_places(rest, flip):
    place = lax.axis_index("seq")
    return [PAIR * ((place // PAIR - j + rest) % rest) + (place + flip) % PAIR for j in range(rest)]


def split_tokens(tokens, chips, rest, width):
    rows, total = tokens.shape
    half = total // PAIR
    near = half // chips
    widths = [half // CORES] * CORES + [half - near, near]
    if width % 128:
        order = jnp.stack(sum(whole_order(chips, rest), []))
        taken = jnp.take(tokens.reshape(rows, total // width, width), order, axis=1).reshape(rows, total)
        return jnp.split(taken, [half // CORES, half, total - near], axis=1)
    tile = min(rows, 128)
    return pl.pallas_call(
        functools.partial(split_kernel, chips, rest, width),
        grid=(rows // tile,),
        in_specs=[pl.BlockSpec((tile, total), lambda i: (i, 0))],
        out_specs=[pl.BlockSpec((tile, w), lambda i: (i, 0)) for w in widths],
        out_shape=[jax.ShapeDtypeStruct((rows, w), tokens.dtype) for w in widths],
        name="split_tokens",
    )(tokens)


def merge_kernel(chips, rest, width, *refs):
    in_refs, out_ref, sems = refs[:-2], refs[-2], refs[-1]
    copies = []
    for ref, order in zip(in_refs, whole_order(chips, rest)):
        for i, block in enumerate(order):
            source = ref.at[:, pl.ds(i * width, width)]
            target = out_ref.at[:, lanes(block, width)]
            copies.append(pltpu.make_async_copy(source, target, sems.at[len(copies)]))
    for copy in copies:
        copy.start()
    for copy in copies:
        copy.wait()


def merge_parts(parts, chips, rest, width):
    rows = parts[0].shape[0]
    total = sum(part.shape[1] for part in parts)
    count = total // width
    if width % 128:
        order = jnp.stack(sum(whole_order(chips, rest), []))
        where = jnp.zeros_like(order).at[order].set(lax.iota(order.dtype, count))
        blocks = jnp.concatenate(parts, axis=1).reshape(rows, count, width)
        return jnp.take(blocks, where, axis=1).reshape(rows, total)
    return pl.pallas_call(
        functools.partial(merge_kernel, chips, rest, width),
        in_specs=[VMEM] * len(parts),
        out_specs=pl.BlockSpec(memory_space=pl.ANY),
        out_shape=jax.ShapeDtypeStruct((rows, total), BF16),
        scratch_shapes=[pltpu.SemaphoreType.DMA((count,))],
        compiler_params=pltpu.CompilerParams(vmem_limit_bytes=20 * 2**20),
        name="merge_parts",
    )(*parts)


def cut(parts, first, step):
    for part in parts:
        if first < part.shape[1]:
            return part[:, first : first + step]
        first -= part.shape[1]


def project_kernel(span, per, qwidth, count, *refs):
    tokens, pieces, (query_ref, pair_ref) = refs[:count], refs[count:-2], refs[-2:]
    total = None
    for g in range(len(pieces) // per):
        rows = jnp.concatenate([r[...] for r in pieces[g * per : (g + 1) * per]], axis=0)
        term = dot(cut(tokens, g * span, span), rows)
        total = term if total is None else total + term
    query_ref[...] = total[:, :qwidth].astype(query_ref.dtype)
    pair_ref[...] = total[:, qwidth:].astype(pair_ref.dtype)


def project(tokens, groups, qwidth, kind):
    rows = tokens[0].shape[0]
    cols = groups[0][0].shape[1]
    pieces = [piece for group in groups for piece in group]
    span = sum(piece.shape[0] for piece in groups[0])
    return pl.pallas_call(
        functools.partial(project_kernel, span, len(groups[0]), qwidth, len(tokens)),
        in_specs=[VMEM] * (len(tokens) + len(pieces)),
        out_specs=[VMEM] * 2,
        out_shape=[jax.ShapeDtypeStruct((rows, w), kind) for w in (qwidth, cols - qwidth)],
        compiler_params=pltpu.CompilerParams(vmem_limit_bytes=20 * 2**20),
        name="project",
    )(*tokens, *pieces)


def grad_kernel(span, counts, dquery_ref, dpair_ref, *refs):
    pieces, outs, mark_ref = refs[: -len(counts) - 1], refs[-len(counts) - 1 : -1], refs[-1]
    grads = jnp.concatenate([dquery_ref[...], dpair_ref[...]], axis=1)
    per = len(pieces) // sum(counts)
    for out_ref, count in zip(outs, counts):
        for i in range(count):
            rows = jnp.concatenate([r[...] for r in pieces[:per]], axis=0)
            pieces = pieces[per:]
            out_ref[:, i * span : (i + 1) * span] = dot(grads, rows, NT).astype(BF16)
    mark_ref[...] = grads[:16, :128]


def width_grad(dquery, dpair, parts):
    rows = dquery.shape[0]
    pieces = [piece for groups in parts for group in groups for piece in group]
    span = sum(piece.shape[0] for piece in parts[0][0])
    counts = [len(groups) for groups in parts]
    return pl.pallas_call(
        functools.partial(grad_kernel, span, counts),
        in_specs=[VMEM] * (2 + len(pieces)),
        out_specs=[VMEM] * (len(parts) + 1),
        out_shape=[jax.ShapeDtypeStruct((rows, span * count), BF16) for count in counts]
        + [jax.ShapeDtypeStruct((16, 128), BF16)],
        compiler_params=pltpu.CompilerParams(vmem_limit_bytes=20 * 2**20),
        name="width_grad",
    )(dquery, dpair, *pieces)


def weight_kernel(steps, rest, width, chips, sources, grads, *refs):
    tokens, refs = refs[: sum(sources)], refs[sum(sources) :]
    rights = [jnp.concatenate([r[...] for r in refs[i : i + grads]], axis=1) for i in range(0, grads * len(sources), grads)]
    right = jnp.concatenate(rights, axis=0)
    outs = refs[grads * len(sources) + 1 :]
    span = rest * width
    for i, k in enumerate(steps):
        left, at = [], 0
        for core, count in enumerate(sources):
            parts, at = tokens[at : at + count], at + count
            if count == 1:
                left.append(parts[0][:, k * span : (k + 1) * span])
            else:
                far, near = parts
                across = core // CORES
                first = across if k == 0 else across * (chips - 1) + k - 1
                left.append((far if k else near)[:, first * span : (first + 1) * span])
        total = dot(jnp.concatenate(left, axis=0).T, right)
        for j in range(rest):
            out = outs[i * rest + j]
            out[...] = total[j * width : (j + 1) * width].astype(out.dtype)


def weight_terms(steps, rest, width, chips, tokens, grads, after):
    cols = sum(g.shape[1] for g in grads[0])
    sources = [len(parts) for parts in tokens]
    parts = [part for group in tokens for part in group]
    given = [g for group in grads for g in group]
    return pl.pallas_call(
        functools.partial(weight_kernel, steps, rest, width, chips, sources, len(grads[0])),
        in_specs=[VMEM] * (len(parts) + len(given) + 1),
        out_specs=[VMEM] * (len(steps) * rest),
        out_shape=[jax.ShapeDtypeStruct((width, cols), BF16 if j else F32) for _ in steps for j in range(rest)],
        compiler_params=pltpu.CompilerParams(vmem_limit_bytes=20 * 2**20),
        name="weight_terms",
    )(*parts, *given, after)


def attend_kernel(heads, back, docs_ref, q_ref, q_from_ref, cot_ref, *refs):
    pair_refs, (out_ref, dq_ref, dpair_ref, dback_ref) = refs[: back + 1], refs[back + 1 :]
    rows = q_ref.shape[0]
    hd = HEAD_DIM
    scale = 1.0 / math.sqrt(hd)
    first = lax.axis_index("seq") * rows
    total = (back + 1) * rows

    row_pos = first + lax.broadcasted_iota(jnp.int32, (1, rows), 1)
    start_of = jnp.zeros((1, rows), jnp.int32)
    start = jnp.int32(0)
    for d in range(docs_ref.shape[0]):
        end = start + docs_ref[d]
        start_of = jnp.where((row_pos >= start) & (row_pos < end), start, start_of)
        start = end
    key_pos = first - back * rows + lax.broadcasted_iota(jnp.int32, (total, rows), 0)
    shut = jnp.where((key_pos >= start_of) & (key_pos <= row_pos), 0.0, -1e30)

    pairs = [r[...] for r in pair_refs]
    keys = jnp.concatenate([p[:, :hd] for p in pairs], axis=0)
    values = jnp.concatenate([p[:, hd:] for p in pairs], axis=0)
    keys_t, values_t = keys.T, values.T
    sums = [jnp.zeros((total, hd), F32), jnp.zeros((total, hd), F32)]
    cols = [slice(h * hd, (h + 1) * hd) for h in range(heads)]
    state = {}

    def products(h):
        q = (q_ref[:, cols[h]] + q_from_ref[:, cols[h]].astype(F32)).astype(BF16)
        cot = cot_ref[:, cols[h]]
        state[h] = [q, cot, dot(keys, q, NT), dot(values, cot, NT)]

    def softmax(h):
        logits = state[h][2] * (scale * math.log2(math.e)) + shut
        raised = jnp.exp2(logits - jnp.max(logits, axis=0, keepdims=True))
        probs = raised * (1.0 / jnp.sum(raised, axis=0, keepdims=True))
        state[h][2] = probs
        state[h].append(probs.astype(BF16))

    def outputs(h):
        _, cot, _, _, probs_half = state[h]
        out_t = dot(values_t, probs_half).astype(BF16)
        out_ref[:, cols[h]] = out_t.T
        state[h].append(jnp.sum(cot.T.astype(F32) * out_t.astype(F32), axis=0, keepdims=True))

    def score_grads(h):
        _, _, probs, dprobs, _, delta = state[h]
        state[h][3] = (probs * (dprobs - delta)).astype(BF16)

    def grads(h):
        q, cot, _, dscores, probs_half, _ = state.pop(h)
        dq_ref[:, cols[h]] = (dot(keys_t, dscores) * scale).astype(BF16).T
        sums[0] = sums[0] + dot(dscores, q)
        sums[1] = sums[1] + dot(probs_half, cot)

    products(0)
    for h in range(heads):
        softmax(h)
        if h + 1 < heads:
            products(h + 1)
        outputs(h)
        if h:
            grads(h - 1)
        score_grads(h)
    grads(heads - 1)
    both = jnp.concatenate([sums[0] * scale, sums[1]], axis=1)
    dpair_ref[...] = both[back * rows :]
    dback_ref[...] = both[: back * rows].astype(BF16)


def attend(docs, q, q_from, cot, pairs):
    rows, width = q.shape
    back = len(pairs) - 1
    two = 2 * HEAD_DIM
    return pl.pallas_call(
        functools.partial(attend_kernel, width // HEAD_DIM, back),
        in_specs=[SMEM] + [VMEM] * (back + 4),
        out_specs=[VMEM] * 4,
        out_shape=[
            jax.ShapeDtypeStruct((rows, width), BF16),
            jax.ShapeDtypeStruct((rows, width), BF16),
            jax.ShapeDtypeStruct((rows, two), F32),
            jax.ShapeDtypeStruct((back * rows, two), BF16),
        ],
        compiler_params=pltpu.CompilerParams(vmem_limit_bytes=20 * 2**20),
        name="attend",
    )(docs, q, q_from, cot, *pairs)


def kept_rows(doc_row, flag_row, positions):
    ends = jnp.cumsum(doc_row)
    starts = ends - doc_row
    inside = (positions[:, None] >= starts[None, :]) & (positions[:, None] < ends[None, :])
    return jnp.sum(jnp.where(inside, flag_row[None, :], 0), axis=1)


def shards(inputs, weights, cotangent, doc_lengths, kept_flags):
    seq_count = lax.axis_size("seq")
    chips = lax.axis_size("dp") // CORES
    rest = seq_count // PAIR
    place = lax.axis_index("seq")
    tokens = inputs[0]
    local = tokens.shape[0]
    qwidth = cotangent.shape[2]
    shard_rows, cols = weights.shape
    width = shard_rows // seq_count
    back = -(-(local * seq_count // 2 - 1) // local)

    own = lax.dynamic_slice_in_dim(weights, place * width, width, 0)
    mine_own, mine_across, sent, near = split_tokens(tokens, chips, rest, width)

    blocks, near = lax.optimization_barrier((weights, near))
    blocks = blocks.reshape(seq_count, width, cols)
    groups_own, groups_near = [
        [[lax.dynamic_index_in_dim(blocks, p, 0, keepdims=False) for p in own_places(rest, flip)]] for flip in range(PAIR)
    ]
    arrived = {}
    for k in sorted(range(1, chips), key=lambda k: (-abs(2 * k - chips), k)):
        first = shift_chip(own, k)
        if not arrived:
            first, sent = lax.optimization_barrier((first, sent))
        if k == chips // 2:
            first, arrived = lax.optimization_barrier((first, arrived))
        arrived[k] = [first] + [shift_rest(first, j) for j in range(1, rest)]
    far_other = swap_x(sent)
    groups_own += [arrived[k] for k in range(1, chips)]
    last = groups_own[chips // 2]
    last[-1], far_other = lax.optimization_barrier((last[-1], far_other))
    groups_across = [[swap_core(piece) for piece in group] for group in groups_own]
    groups_near.append([swap_core(piece) for piece in groups_near[0]])
    groups = groups_own + groups_across
    groups_far = groups_own[1:] + groups_across[1:]

    query_sent, pair_sent = project([far_other], groups_far, qwidth, BF16)
    query_sent, near_other = lax.optimization_barrier((query_sent, swap_x(near)))
    pair_from, query_from = swap_x(pair_sent), swap_x(query_sent)
    query, pair = project([mine_own, mine_across, near], groups + groups_near, qwidth, F32)
    pair = (pair + pair_from.astype(F32)).astype(BF16)

    doc_row, flag_row = doc_lengths[0], kept_flags[0]
    positions = place * local + lax.iota(jnp.int32, local)
    kept = kept_rows(doc_row, flag_row, positions)
    cot = jnp.where(kept[:, None] > 0, cotangent[0], jnp.zeros_like(cotangent[0]))

    pairs = [shift_seq(pair, j) for j in range(back, 0, -1)] + [pair]
    attention, dquery, dpair, dback = attend(doc_row, query, query_from, cot, pairs)

    dquery_other = swap_x(dquery)
    for j in range(1, back + 1):
        sent = dback[(back - j) * local : (back - j + 1) * local]
        dpair = dpair + shift_seq(sent, -j).astype(F32)
    dpair = dpair.astype(BF16)
    dpair_other = swap_x(dpair)

    left = [[mine_own], [far_other, near_other]]
    left += [[swap_core(mine_across)], [swap_core(far_other), swap_core(near_other)]]
    right = [[dquery, dpair], [dquery_other, dpair_other]]
    right += [[swap_core(g) for g in group] for group in right]
    order = sorted(range(chips), key=lambda k: (k == 0, -min(k, chips - k), k))
    parts, after = [], dpair
    for steps in (order[: chips // 2], order[chips // 2 :]):
        terms = weight_terms(steps, rest, width, chips, left, right, after)
        if not parts:
            grad_sent, after = width_grad(dquery_other, dpair_other, [groups_far])
            grad_from = swap_x(grad_sent)
        for i, k in enumerate(steps):
            part, *sent = terms[i * rest : (i + 1) * rest]
            for j, piece in enumerate(sent, 1):
                part = part + shift_rest(piece, -j).astype(F32)
            if k:
                part = shift_chip(part.astype(BF16), -k).astype(F32)
            parts.append(part)
    weights_grad = functools.reduce(jnp.add, reversed(parts))

    grad_mine, grad_near, _ = width_grad(dquery, dpair, [groups, groups_near])
    inputs_grad = merge_parts([grad_mine, grad_from, grad_near], chips, rest, width)
    return (attention[None], inputs_grad[None], weights_grad)


def solution(mesh):
    in_specs = (
        P("dp", "seq", None),
        P("dp", None),
        P("dp", "seq", None),
        P("dp", None),
        P("dp", None),
    )
    out_specs = (P("dp", "seq", None), P("dp", "seq", None), P(("dp", "seq"), None))
    return jax.shard_map(shards, mesh=mesh, in_specs=in_specs, out_specs=out_specs, check_vma=False)
```

```python
import functools
import math

import jax
import jax.numpy as jnp
from jax import lax
from jax.experimental import pallas as pl
from jax.experimental.pallas import tpu as pltpu
from jax.sharding import PartitionSpec as P

HEAD_DIM = 128
PAIR = 2
CORES = 2
BF16 = jnp.bfloat16
F32 = jnp.float32
NT = (((1,), (1,)), ((), ()))
TN = (((0,), (0,)), ((), ()))
VMEM = pl.BlockSpec(memory_space=pltpu.VMEM)
SMEM = pl.BlockSpec(memory_space=pltpu.SMEM)


def dot(a, b, dims=(((1,), (0,)), ((), ()))):
    return lax.dot_general(a, b, dims, preferred_element_type=F32)


def swap_x(array):
    count = lax.axis_size("seq")
    return lax.ppermute(array, "seq", [(i, i ^ 1) for i in range(count)])


def shift_rest(array, step):
    count = lax.axis_size("seq")
    rest = count // PAIR
    pairs = [(i, PAIR * ((i // PAIR + step) % rest) + i % PAIR) for i in range(count)]
    return lax.ppermute(array, "seq", pairs)


def swap_core(array):
    count = lax.axis_size("dp")
    return lax.ppermute(array, "dp", [(i, i ^ 1) for i in range(count)])


def shift_chip(array, step):
    count = lax.axis_size("dp")
    chips = count // CORES
    pairs = [(i, CORES * ((i // CORES + step) % chips) + i % CORES) for i in range(count)]
    return lax.ppermute(array, "dp", pairs)


def shift_seq(array, step):
    count = lax.axis_size("seq")
    pairs = [(i, i + step) for i in range(count) if 0 <= i + step < count]
    return lax.ppermute(array, "seq", pairs)


def block_order(chips, rest, flip, steps):
    dp_index, place = lax.axis_index("dp"), lax.axis_index("seq")
    chip, core = dp_index // CORES, dp_index % CORES
    around, x = place // PAIR, (place + flip) % PAIR
    order = []
    for c in range(CORES):
        for k in steps:
            for j in range(rest):
                shard = CORES * ((chip - k + chips) % chips) + (core + c) % CORES
                order.append(shard * (PAIR * rest) + PAIR * ((around - j + rest) % rest) + x)
    return order


def whole_order(chips, rest):
    far = range(1, chips)
    return [block_order(chips, rest, flip, steps) for flip, steps in ((0, range(chips)), (1, far), (1, range(1)))]


def split_order(chips, rest):
    mine, *others = whole_order(chips, rest)
    half = len(mine) // CORES
    return [mine[:half], mine[half:], *others]


def lanes(index, width):
    return pl.ds(pl.multiple_of(index * width, width), width)


def split_kernel(chips, rest, width, tokens_ref, *out_refs):
    for ref, order in zip(out_refs, split_order(chips, rest)):
        for i, block in enumerate(order):
            ref[:, i * width : (i + 1) * width] = tokens_ref[:, lanes(block, width)]


def own_places(rest, flip):
    place = lax.axis_index("seq")
    return [PAIR * ((place // PAIR - j + rest) % rest) + (place + flip) % PAIR for j in range(rest)]


def split_tokens(tokens, chips, rest, width):
    rows, total = tokens.shape
    half = total // PAIR
    near = half // chips
    widths = [half // CORES] * CORES + [half - near, near]
    if width % 128:
        order = jnp.stack(sum(whole_order(chips, rest), []))
        taken = jnp.take(tokens.reshape(rows, total // width, width), order, axis=1).reshape(rows, total)
        return jnp.split(taken, [half // CORES, half, total - near], axis=1)
    tile = min(rows, 128)
    return pl.pallas_call(
        functools.partial(split_kernel, chips, rest, width),
        grid=(rows // tile,),
        in_specs=[pl.BlockSpec((tile, total), lambda i: (i, 0))],
        out_specs=[pl.BlockSpec((tile, w), lambda i: (i, 0)) for w in widths],
        out_shape=[jax.ShapeDtypeStruct((rows, w), tokens.dtype) for w in widths],
        name="split_tokens",
    )(tokens)


def finish_kernel(chips, rest, width, *refs):
    part_refs, term_refs, (out_ref, sum_ref, total_ref, sems) = refs[:3], refs[3:-4], refs[-4:]
    copies = []
    for ref, order in zip(part_refs, whole_order(chips, rest)):
        for i, block in enumerate(order):
            source = ref.at[:, pl.ds(i * width, width)]
            target = out_ref.at[:, lanes(block, width)]
            copies.append(pltpu.make_async_copy(source, target, sems.at[len(copies)]))
    for copy in copies:
        copy.start()
    total = term_refs[0][...].astype(F32)
    for ref in term_refs[1:]:
        total = total + ref[...].astype(F32)
    total_ref[...] = total
    copies.append(pltpu.make_async_copy(total_ref, sum_ref, sems.at[len(copies)]))
    copies[-1].start()
    for copy in copies:
        copy.wait()


def finish(parts, terms, chips, rest, width):
    rows = parts[0].shape[0]
    total = sum(part.shape[1] for part in parts)
    count = total // width
    if width % 128:
        order = jnp.stack(sum(whole_order(chips, rest), []))
        where = jnp.zeros_like(order).at[order].set(lax.iota(order.dtype, count))
        blocks = jnp.concatenate(parts, axis=1).reshape(rows, count, width)
        summed = functools.reduce(jnp.add, [term.astype(F32) for term in terms])
        return jnp.take(blocks, where, axis=1).reshape(rows, total), summed
    return pl.pallas_call(
        functools.partial(finish_kernel, chips, rest, width),
        in_specs=[VMEM] * (len(parts) + len(terms)),
        out_specs=[pl.BlockSpec(memory_space=pl.ANY)] * 2,
        out_shape=[
            jax.ShapeDtypeStruct((rows, total), BF16),
            jax.ShapeDtypeStruct(terms[0].shape, F32),
        ],
        scratch_shapes=[pltpu.VMEM(terms[0].shape, F32), pltpu.SemaphoreType.DMA((count + 1,))],
        compiler_params=pltpu.CompilerParams(vmem_limit_bytes=20 * 2**20),
        name="finish",
    )(*parts, *terms)


def cut(parts, first, step):
    for part in parts:
        if first < part.shape[1]:
            return part[:, first : first + step]
        first -= part.shape[1]


def project_kernel(span, per, qwidth, count, *refs):
    tokens, pieces, (query_ref, pair_ref) = refs[:count], refs[count:-2], refs[-2:]
    total = None
    for g in range(len(pieces) // per):
        rows = jnp.concatenate([r[...] for r in pieces[g * per : (g + 1) * per]], axis=0)
        term = dot(cut(tokens, g * span, span), rows)
        total = term if total is None else total + term
    query_ref[...] = total[:, :qwidth].astype(query_ref.dtype)
    pair_ref[...] = total[:, qwidth:].astype(pair_ref.dtype)


def project(tokens, groups, qwidth, kind):
    rows = tokens[0].shape[0]
    cols = groups[0][0].shape[1]
    pieces = [piece for group in groups for piece in group]
    span = sum(piece.shape[0] for piece in groups[0])
    return pl.pallas_call(
        functools.partial(project_kernel, span, len(groups[0]), qwidth, len(tokens)),
        in_specs=[VMEM] * (len(tokens) + len(pieces)),
        out_specs=[VMEM] * 2,
        out_shape=[jax.ShapeDtypeStruct((rows, w), kind) for w in (qwidth, cols - qwidth)],
        compiler_params=pltpu.CompilerParams(vmem_limit_bytes=20 * 2**20),
        name="project",
    )(*tokens, *pieces)


def grad_kernel(span, counts, dquery_ref, dpair_ref, *refs):
    pieces, outs, mark_ref = refs[: -len(counts) - 1], refs[-len(counts) - 1 : -1], refs[-1]
    grads = jnp.concatenate([dquery_ref[...], dpair_ref[...]], axis=1)
    per = len(pieces) // sum(counts)
    for out_ref, count in zip(outs, counts):
        for i in range(count):
            rows = jnp.concatenate([r[...] for r in pieces[:per]], axis=0)
            pieces = pieces[per:]
            out_ref[:, i * span : (i + 1) * span] = dot(grads, rows, NT).astype(BF16)
    mark_ref[...] = grads[:16, :128]


def width_grad(dquery, dpair, parts):
    rows = dquery.shape[0]
    pieces = [piece for groups in parts for group in groups for piece in group]
    span = sum(piece.shape[0] for piece in parts[0][0])
    counts = [len(groups) for groups in parts]
    return pl.pallas_call(
        functools.partial(grad_kernel, span, counts),
        in_specs=[VMEM] * (2 + len(pieces)),
        out_specs=[VMEM] * (len(parts) + 1),
        out_shape=[jax.ShapeDtypeStruct((rows, span * count), BF16) for count in counts]
        + [jax.ShapeDtypeStruct((16, 128), BF16)],
        compiler_params=pltpu.CompilerParams(vmem_limit_bytes=20 * 2**20),
        name="width_grad",
    )(dquery, dpair, *pieces)


def weight_kernel(steps, rest, width, chips, sources, grads, *refs):
    tokens, refs = refs[: sum(sources)], refs[sum(sources) :]
    rights = [jnp.concatenate([r[...] for r in refs[i : i + grads]], axis=1) for i in range(0, grads * len(sources), grads)]
    right = jnp.concatenate(rights, axis=0)
    outs = refs[grads * len(sources) + 1 :]
    span = rest * width
    for i, k in enumerate(steps):
        left, at = [], 0
        for core, count in enumerate(sources):
            parts, at = tokens[at : at + count], at + count
            if count == 1:
                left.append(parts[0][:, k * span : (k + 1) * span])
            else:
                far, near = parts
                across = core // CORES
                first = across if k == 0 else across * (chips - 1) + k - 1
                left.append((far if k else near)[:, first * span : (first + 1) * span])
        total = dot(jnp.concatenate(left, axis=0).T, right)
        for j in range(rest):
            out = outs[i * rest + j]
            out[...] = total[j * width : (j + 1) * width].astype(out.dtype)


def weight_terms(steps, rest, width, chips, tokens, grads, after):
    cols = sum(g.shape[1] for g in grads[0])
    sources = [len(parts) for parts in tokens]
    parts = [part for group in tokens for part in group]
    given = [g for group in grads for g in group]
    return pl.pallas_call(
        functools.partial(weight_kernel, steps, rest, width, chips, sources, len(grads[0])),
        in_specs=[VMEM] * (len(parts) + len(given) + 1),
        out_specs=[VMEM] * (len(steps) * rest),
        out_shape=[jax.ShapeDtypeStruct((width, cols), BF16 if j else F32) for _ in steps for j in range(rest)],
        compiler_params=pltpu.CompilerParams(vmem_limit_bytes=20 * 2**20),
        name="weight_terms",
    )(*parts, *given, after)


def attend_kernel(heads, back, docs_ref, q_ref, q_from_ref, cot_ref, *refs):
    pair_refs, (out_ref, dq_ref, dpair_ref, dback_ref) = refs[: back + 1], refs[back + 1 :]
    rows = q_ref.shape[0]
    hd = HEAD_DIM
    scale = 1.0 / math.sqrt(hd)
    first = lax.axis_index("seq") * rows
    total = (back + 1) * rows

    row_pos = first + lax.broadcasted_iota(jnp.int32, (1, rows), 1)
    start_of = jnp.zeros((1, rows), jnp.int32)
    start = jnp.int32(0)
    for d in range(docs_ref.shape[0]):
        end = start + docs_ref[d]
        start_of = jnp.where((row_pos >= start) & (row_pos < end), start, start_of)
        start = end
    key_pos = first - back * rows + lax.broadcasted_iota(jnp.int32, (total, rows), 0)
    shut = jnp.where((key_pos >= start_of) & (key_pos <= row_pos), 0.0, -1e30)

    pairs = [r[...] for r in pair_refs]
    keys = jnp.concatenate([p[:, :hd] for p in pairs], axis=0)
    values = jnp.concatenate([p[:, hd:] for p in pairs], axis=0)
    keys_t, values_t = keys.T, values.T
    sums = [jnp.zeros((total, hd), F32), jnp.zeros((total, hd), F32)]
    cols = [slice(h * hd, (h + 1) * hd) for h in range(heads)]
    state = {}

    def products(h):
        q = (q_ref[:, cols[h]] + q_from_ref[:, cols[h]].astype(F32)).astype(BF16)
        cot = cot_ref[:, cols[h]]
        state[h] = [q, cot, dot(keys, q, NT), dot(values, cot, NT)]

    def softmax(h):
        logits = state[h][2] * (scale * math.log2(math.e)) + shut
        raised = jnp.exp2(logits - jnp.max(logits, axis=0, keepdims=True))
        probs = raised * (1.0 / jnp.sum(raised, axis=0, keepdims=True))
        state[h][2] = probs
        state[h].append(probs.astype(BF16))

    def outputs(h):
        _, cot, _, _, probs_half = state[h]
        out_t = dot(values_t, probs_half).astype(BF16)
        out_ref[:, cols[h]] = out_t.T
        state[h].append(jnp.sum(cot.T.astype(F32) * out_t.astype(F32), axis=0, keepdims=True))

    def score_grads(h):
        _, _, probs, dprobs, _, delta = state[h]
        state[h][3] = (probs * (dprobs - delta)).astype(BF16)

    def grads(h):
        q, cot, _, dscores, probs_half, _ = state.pop(h)
        dq_ref[:, cols[h]] = (dot(keys_t, dscores) * scale).astype(BF16).T
        sums[0] = sums[0] + dot(dscores, q)
        sums[1] = sums[1] + dot(probs_half, cot)

    products(0)
    for h in range(heads):
        softmax(h)
        if h + 1 < heads:
            products(h + 1)
        outputs(h)
        if h:
            grads(h - 1)
        score_grads(h)
    grads(heads - 1)
    both = jnp.concatenate([sums[0] * scale, sums[1]], axis=1)
    dpair_ref[...] = both[back * rows :]
    dback_ref[...] = both[: back * rows].astype(BF16)


def attend(docs, q, q_from, cot, pairs):
    rows, width = q.shape
    back = len(pairs) - 1
    two = 2 * HEAD_DIM
    return pl.pallas_call(
        functools.partial(attend_kernel, width // HEAD_DIM, back),
        in_specs=[SMEM] + [VMEM] * (back + 4),
        out_specs=[VMEM] * 4,
        out_shape=[
            jax.ShapeDtypeStruct((rows, width), BF16),
            jax.ShapeDtypeStruct((rows, width), BF16),
            jax.ShapeDtypeStruct((rows, two), F32),
            jax.ShapeDtypeStruct((back * rows, two), BF16),
        ],
        compiler_params=pltpu.CompilerParams(vmem_limit_bytes=20 * 2**20),
        name="attend",
    )(docs, q, q_from, cot, *pairs)


def kept_rows(doc_row, flag_row, positions):
    ends = jnp.cumsum(doc_row)
    starts = ends - doc_row
    inside = (positions[:, None] >= starts[None, :]) & (positions[:, None] < ends[None, :])
    return jnp.sum(jnp.where(inside, flag_row[None, :], 0), axis=1)


def shards(inputs, weights, cotangent, doc_lengths, kept_flags):
    seq_count = lax.axis_size("seq")
    chips = lax.axis_size("dp") // CORES
    rest = seq_count // PAIR
    place = lax.axis_index("seq")
    tokens = inputs[0]
    local = tokens.shape[0]
    qwidth = cotangent.shape[2]
    shard_rows, cols = weights.shape
    width = shard_rows // seq_count
    back = -(-(local * seq_count // 2 - 1) // local)

    own = lax.dynamic_slice_in_dim(weights, place * width, width, 0)
    mine_own, mine_across, sent, near = split_tokens(tokens, chips, rest, width)

    blocks, near = lax.optimization_barrier((weights, near))
    blocks = blocks.reshape(seq_count, width, cols)
    groups_own, groups_near = [
        [[lax.dynamic_index_in_dim(blocks, p, 0, keepdims=False) for p in own_places(rest, flip)]] for flip in range(PAIR)
    ]
    arrived = {}
    for k in sorted(range(1, chips), key=lambda k: (-abs(2 * k - chips), k)):
        first = shift_chip(own, k)
        if not arrived:
            first, sent = lax.optimization_barrier((first, sent))
        if k == chips // 2:
            first, arrived = lax.optimization_barrier((first, arrived))
        arrived[k] = [first] + [shift_rest(first, j) for j in range(1, rest)]
    far_other = swap_x(sent)
    groups_own += [arrived[k] for k in range(1, chips)]
    last = groups_own[chips // 2]
    last[-1], far_other = lax.optimization_barrier((last[-1], far_other))
    groups_across = [[swap_core(piece) for piece in group] for group in groups_own]
    groups_near.append([swap_core(piece) for piece in groups_near[0]])
    groups = groups_own + groups_across
    groups_far = groups_own[1:] + groups_across[1:]

    query_sent, pair_sent = project([far_other], groups_far, qwidth, BF16)
    query_sent, near_other = lax.optimization_barrier((query_sent, swap_x(near)))
    pair_from, query_from = swap_x(pair_sent), swap_x(query_sent)
    query, pair = project([mine_own, mine_across, near], groups + groups_near, qwidth, F32)
    pair = (pair + pair_from.astype(F32)).astype(BF16)

    doc_row, flag_row = doc_lengths[0], kept_flags[0]
    positions = place * local + lax.iota(jnp.int32, local)
    kept = kept_rows(doc_row, flag_row, positions)
    cot = jnp.where(kept[:, None] > 0, cotangent[0], jnp.zeros_like(cotangent[0]))

    pairs = [shift_seq(pair, j) for j in range(back, 0, -1)] + [pair]
    attention, dquery, dpair, dback = attend(doc_row, query, query_from, cot, pairs)

    dquery_other = swap_x(dquery)
    for j in range(1, back + 1):
        sent = dback[(back - j) * local : (back - j + 1) * local]
        dpair = dpair + shift_seq(sent, -j).astype(F32)
    dpair = dpair.astype(BF16)
    dpair_other = swap_x(dpair)

    left = [[mine_own], [far_other, near_other]]
    left += [[swap_core(mine_across)], [swap_core(far_other), swap_core(near_other)]]
    right = [[dquery, dpair], [dquery_other, dpair_other]]
    right += [[swap_core(g) for g in group] for group in right]
    order = sorted(range(chips), key=lambda k: (k == 0, -min(k, chips - k), k))
    parts, after = [], dpair
    for steps in (order[: chips // 2], order[chips // 2 :]):
        terms = weight_terms(steps, rest, width, chips, left, right, after)
        if not parts:
            grad_sent, after = width_grad(dquery_other, dpair_other, [groups_far])
            grad_from = swap_x(grad_sent)
        for i, k in enumerate(steps):
            part, *sent = terms[i * rest : (i + 1) * rest]
            received = [shift_rest(piece, -j) for j, piece in enumerate(sent, 1)]
            if k:
                part = functools.reduce(jnp.add, [term.astype(F32) for term in received], part)
                parts.append(shift_chip(part.astype(BF16), -k))
            else:
                parts += [part, *received]

    grad_mine, grad_near, _ = width_grad(dquery, dpair, [groups, groups_near])
    inputs_grad, weights_grad = finish([grad_mine, grad_from, grad_near], parts, chips, rest, width)
    return (attention[None], inputs_grad[None], weights_grad)


def solution(mesh):
    in_specs = (
        P("dp", "seq", None),
        P("dp", None),
        P("dp", "seq", None),
        P("dp", None),
        P("dp", None),
    )
    out_specs = (P("dp", "seq", None), P("dp", "seq", None), P(("dp", "seq"), None))
    return jax.shard_map(shards, mesh=mesh, in_specs=in_specs, out_specs=out_specs, check_vma=False)
```

```python
import functools
import math

import jax
import jax.numpy as jnp
from jax import lax
from jax.experimental import pallas as pl
from jax.experimental.pallas import tpu as pltpu
from jax.sharding import PartitionSpec as P

HEAD_DIM = 128
PAIR = 2
CORES = 2
BF16 = jnp.bfloat16
F32 = jnp.float32
NT = (((1,), (1,)), ((), ()))
TN = (((0,), (0,)), ((), ()))
VMEM = pl.BlockSpec(memory_space=pltpu.VMEM)
SMEM = pl.BlockSpec(memory_space=pltpu.SMEM)


def dot(a, b, dims=(((1,), (0,)), ((), ()))):
    return lax.dot_general(a, b, dims, preferred_element_type=F32)


def swap_x(array):
    count = lax.axis_size("seq")
    return lax.ppermute(array, "seq", [(i, i ^ 1) for i in range(count)])


def shift_rest(array, step):
    count = lax.axis_size("seq")
    rest = count // PAIR
    pairs = [(i, PAIR * ((i // PAIR + step) % rest) + i % PAIR) for i in range(count)]
    return lax.ppermute(array, "seq", pairs)


def swap_core(array):
    count = lax.axis_size("dp")
    return lax.ppermute(array, "dp", [(i, i ^ 1) for i in range(count)])


def shift_chip(array, step):
    count = lax.axis_size("dp")
    chips = count // CORES
    pairs = [(i, CORES * ((i // CORES + step) % chips) + i % CORES) for i in range(count)]
    return lax.ppermute(array, "dp", pairs)


def shift_seq(array, step):
    count = lax.axis_size("seq")
    pairs = [(i, i + step) for i in range(count) if 0 <= i + step < count]
    return lax.ppermute(array, "seq", pairs)


def block_order(chips, rest, flip, steps):
    dp_index, place = lax.axis_index("dp"), lax.axis_index("seq")
    chip, core = dp_index // CORES, dp_index % CORES
    around, x = place // PAIR, (place + flip) % PAIR
    order = []
    for c in range(CORES):
        for k in steps:
            for j in range(rest):
                shard = CORES * ((chip - k + chips) % chips) + (core + c) % CORES
                order.append(shard * (PAIR * rest) + PAIR * ((around - j + rest) % rest) + x)
    return order


def whole_order(chips, rest):
    far = range(1, chips)
    return [block_order(chips, rest, flip, steps) for flip, steps in ((0, range(chips)), (1, far), (1, range(1)))]


def split_order(chips, rest):
    mine, *others = whole_order(chips, rest)
    half = len(mine) // CORES
    return [mine[:half], mine[half:], *others]


def lanes(index, width):
    return pl.ds(pl.multiple_of(index * width, width), width)


def split_kernel(chips, rest, width, tokens_ref, *out_refs):
    for ref, order in zip(out_refs, split_order(chips, rest)):
        for i, block in enumerate(order):
            ref[:, i * width : (i + 1) * width] = tokens_ref[:, lanes(block, width)]


def own_places(rest, flip):
    place = lax.axis_index("seq")
    return [PAIR * ((place // PAIR - j + rest) % rest) + (place + flip) % PAIR for j in range(rest)]


def split_tokens(tokens, chips, rest, width):
    rows, total = tokens.shape
    half = total // PAIR
    near = half // chips
    widths = [half // CORES] * CORES + [half - near, near]
    if width % 128:
        order = jnp.stack(sum(whole_order(chips, rest), []))
        taken = jnp.take(tokens.reshape(rows, total // width, width), order, axis=1).reshape(rows, total)
        return jnp.split(taken, [half // CORES, half, total - near], axis=1)
    tile = min(rows, 128)
    return pl.pallas_call(
        functools.partial(split_kernel, chips, rest, width),
        grid=(rows // tile,),
        in_specs=[pl.BlockSpec((tile, total), lambda i: (i, 0))],
        out_specs=[pl.BlockSpec((tile, w), lambda i: (i, 0)) for w in widths],
        out_shape=[jax.ShapeDtypeStruct((rows, w), tokens.dtype) for w in widths],
        name="split_tokens",
    )(tokens)


def finish_kernel(chips, rest, width, *refs):
    part_refs, term_refs, (out_ref, sum_ref, total_ref, sems) = refs[:3], refs[3:-4], refs[-4:]
    copies = []
    for ref, order in zip(part_refs, whole_order(chips, rest)):
        for i, block in enumerate(order):
            source = ref.at[:, pl.ds(i * width, width)]
            target = out_ref.at[:, lanes(block, width)]
            copies.append(pltpu.make_async_copy(source, target, sems.at[len(copies)]))
    for copy in copies:
        copy.start()
    total = term_refs[0][...].astype(F32)
    for ref in term_refs[1:]:
        total = total + ref[...].astype(F32)
    total_ref[...] = total
    copies.append(pltpu.make_async_copy(total_ref, sum_ref, sems.at[len(copies)]))
    copies[-1].start()
    for copy in copies:
        copy.wait()


def finish(parts, terms, chips, rest, width):
    rows = parts[0].shape[0]
    total = sum(part.shape[1] for part in parts)
    count = total // width
    if width % 128:
        order = jnp.stack(sum(whole_order(chips, rest), []))
        where = jnp.zeros_like(order).at[order].set(lax.iota(order.dtype, count))
        blocks = jnp.concatenate(parts, axis=1).reshape(rows, count, width)
        summed = functools.reduce(jnp.add, [term.astype(F32) for term in terms])
        return jnp.take(blocks, where, axis=1).reshape(rows, total), summed
    return pl.pallas_call(
        functools.partial(finish_kernel, chips, rest, width),
        in_specs=[VMEM] * (len(parts) + len(terms)),
        out_specs=[pl.BlockSpec(memory_space=pl.ANY)] * 2,
        out_shape=[
            jax.ShapeDtypeStruct((rows, total), BF16),
            jax.ShapeDtypeStruct(terms[0].shape, F32),
        ],
        scratch_shapes=[pltpu.VMEM(terms[0].shape, F32), pltpu.SemaphoreType.DMA((count + 1,))],
        compiler_params=pltpu.CompilerParams(vmem_limit_bytes=20 * 2**20),
        name="finish",
    )(*parts, *terms)


def cut(parts, first, step):
    for part in parts:
        if first < part.shape[1]:
            return part[:, first : first + step]
        first -= part.shape[1]


def project_kernel(span, per, qwidth, count, *refs):
    tokens, pieces, (query_ref, pair_ref) = refs[:count], refs[count:-2], refs[-2:]
    total = None
    for g in range(len(pieces) // per):
        rows = jnp.concatenate([r[...] for r in pieces[g * per : (g + 1) * per]], axis=0)
        term = dot(cut(tokens, g * span, span), rows)
        total = term if total is None else total + term
    query_ref[...] = total[:, :qwidth].astype(query_ref.dtype)
    pair_ref[...] = total[:, qwidth:].astype(pair_ref.dtype)


def project(tokens, groups, qwidth, kind):
    rows = tokens[0].shape[0]
    cols = groups[0][0].shape[1]
    pieces = [piece for group in groups for piece in group]
    span = sum(piece.shape[0] for piece in groups[0])
    return pl.pallas_call(
        functools.partial(project_kernel, span, len(groups[0]), qwidth, len(tokens)),
        in_specs=[VMEM] * (len(tokens) + len(pieces)),
        out_specs=[VMEM] * 2,
        out_shape=[jax.ShapeDtypeStruct((rows, w), kind) for w in (qwidth, cols - qwidth)],
        compiler_params=pltpu.CompilerParams(vmem_limit_bytes=20 * 2**20),
        name="project",
    )(*tokens, *pieces)


def grad_kernel(span, counts, dquery_ref, dpair_ref, *refs):
    pieces, outs, mark_ref = refs[: -len(counts) - 1], refs[-len(counts) - 1 : -1], refs[-1]
    grads = jnp.concatenate([dquery_ref[...], dpair_ref[...]], axis=1)
    per = len(pieces) // sum(counts)
    for out_ref, count in zip(outs, counts):
        for i in range(count):
            rows = jnp.concatenate([r[...] for r in pieces[:per]], axis=0)
            pieces = pieces[per:]
            out_ref[:, i * span : (i + 1) * span] = dot(grads, rows, NT).astype(BF16)
    mark_ref[...] = grads[:16, :128]


def width_grad(dquery, dpair, parts):
    rows = dquery.shape[0]
    pieces = [piece for groups in parts for group in groups for piece in group]
    span = sum(piece.shape[0] for piece in parts[0][0])
    counts = [len(groups) for groups in parts]
    return pl.pallas_call(
        functools.partial(grad_kernel, span, counts),
        in_specs=[VMEM] * (2 + len(pieces)),
        out_specs=[VMEM] * (len(parts) + 1),
        out_shape=[jax.ShapeDtypeStruct((rows, span * count), BF16) for count in counts]
        + [jax.ShapeDtypeStruct((16, 128), BF16)],
        compiler_params=pltpu.CompilerParams(vmem_limit_bytes=20 * 2**20),
        name="width_grad",
    )(dquery, dpair, *pieces)


def weight_kernel(steps, rest, width, chips, sources, grads, *refs):
    tokens, refs = refs[: sum(sources)], refs[sum(sources) :]
    rights = [jnp.concatenate([r[...] for r in refs[i : i + grads]], axis=1) for i in range(0, grads * len(sources), grads)]
    right = jnp.concatenate(rights, axis=0)
    outs = refs[grads * len(sources) + 1 :]
    span = rest * width
    for i, k in enumerate(steps):
        left, at = [], 0
        for core, count in enumerate(sources):
            parts, at = tokens[at : at + count], at + count
            if count == 1:
                left.append(parts[0][:, k * span : (k + 1) * span])
            else:
                far, near = parts
                across = core // CORES
                first = across if k == 0 else across * (chips - 1) + k - 1
                left.append((far if k else near)[:, first * span : (first + 1) * span])
        total = dot(jnp.concatenate(left, axis=0).T, right)
        for j in range(rest):
            out = outs[i * rest + j]
            out[...] = total[j * width : (j + 1) * width].astype(out.dtype)


def weight_terms(steps, rest, width, chips, tokens, grads, after):
    cols = sum(g.shape[1] for g in grads[0])
    sources = [len(parts) for parts in tokens]
    parts = [part for group in tokens for part in group]
    given = [g for group in grads for g in group]
    return pl.pallas_call(
        functools.partial(weight_kernel, steps, rest, width, chips, sources, len(grads[0])),
        in_specs=[VMEM] * (len(parts) + len(given) + 1),
        out_specs=[VMEM] * (len(steps) * rest),
        out_shape=[jax.ShapeDtypeStruct((width, cols), BF16 if j else F32) for _ in steps for j in range(rest)],
        compiler_params=pltpu.CompilerParams(vmem_limit_bytes=20 * 2**20),
        name="weight_terms",
    )(*parts, *given, after)


def attend_kernel(heads, back, docs_ref, q_ref, q_from_ref, cot_ref, *refs):
    pair_refs, (out_ref, dq_ref, dpair_ref, dback_ref) = refs[: back + 1], refs[back + 1 :]
    rows = q_ref.shape[0]
    hd = HEAD_DIM
    scale = 1.0 / math.sqrt(hd)
    first = lax.axis_index("seq") * rows
    total = (back + 1) * rows

    row_pos = first + lax.broadcasted_iota(jnp.int32, (1, rows), 1)
    start_of = jnp.zeros((1, rows), jnp.int32)
    start = jnp.int32(0)
    for d in range(docs_ref.shape[0]):
        end = start + docs_ref[d]
        start_of = jnp.where((row_pos >= start) & (row_pos < end), start, start_of)
        start = end
    key_pos = first - back * rows + lax.broadcasted_iota(jnp.int32, (total, rows), 0)
    shut = jnp.where((key_pos >= start_of) & (key_pos <= row_pos), 0.0, -1e30)

    pairs = [r[...] for r in pair_refs]
    keys = jnp.concatenate([p[:, :hd] for p in pairs], axis=0)
    values = jnp.concatenate([p[:, hd:] for p in pairs], axis=0)
    keys_t, values_t = keys.T, values.T
    sums = [jnp.zeros((total, hd), F32), jnp.zeros((total, hd), F32)]
    cols = [slice(h * hd, (h + 1) * hd) for h in range(heads)]
    state = {}

    def products(h):
        q = (q_ref[:, cols[h]] + q_from_ref[:, cols[h]].astype(F32)).astype(BF16)
        cot = cot_ref[:, cols[h]]
        state[h] = [q, cot, dot(keys, q, NT), dot(values, cot, NT)]

    def softmax(h):
        logits = state[h][2] * (scale * math.log2(math.e)) + shut
        raised = jnp.exp2(logits - jnp.max(logits, axis=0, keepdims=True))
        probs = raised * (1.0 / jnp.sum(raised, axis=0, keepdims=True))
        state[h][2] = probs
        state[h].append(probs.astype(BF16))

    def outputs(h):
        _, cot, _, _, probs_half = state[h]
        out_t = dot(values_t, probs_half).astype(BF16)
        out_ref[:, cols[h]] = out_t.T
        state[h].append(jnp.sum(cot.T.astype(F32) * out_t.astype(F32), axis=0, keepdims=True))

    def score_grads(h):
        _, _, probs, dprobs, _, delta = state[h]
        state[h][3] = (probs * (dprobs - delta)).astype(BF16)

    def grads(h):
        q, cot, _, dscores, probs_half, _ = state.pop(h)
        dq_ref[:, cols[h]] = (dot(keys_t, dscores) * scale).astype(BF16).T
        sums[0] = sums[0] + dot(dscores, q)
        sums[1] = sums[1] + dot(probs_half, cot)

    products(0)
    for h in range(heads):
        softmax(h)
        if h + 1 < heads:
            products(h + 1)
        outputs(h)
        if h:
            grads(h - 1)
        score_grads(h)
    grads(heads - 1)
    both = jnp.concatenate([sums[0] * scale, sums[1]], axis=1)
    dpair_ref[...] = both[back * rows :]
    dback_ref[...] = both[: back * rows].astype(BF16)


def attend(docs, q, q_from, cot, pairs):
    rows, width = q.shape
    back = len(pairs) - 1
    two = 2 * HEAD_DIM
    return pl.pallas_call(
        functools.partial(attend_kernel, width // HEAD_DIM, back),
        in_specs=[SMEM] + [VMEM] * (back + 4),
        out_specs=[VMEM] * 4,
        out_shape=[
            jax.ShapeDtypeStruct((rows, width), BF16),
            jax.ShapeDtypeStruct((rows, width), BF16),
            jax.ShapeDtypeStruct((rows, two), F32),
            jax.ShapeDtypeStruct((back * rows, two), BF16),
        ],
        compiler_params=pltpu.CompilerParams(vmem_limit_bytes=20 * 2**20),
        name="attend",
    )(docs, q, q_from, cot, *pairs)


def kept_rows(doc_row, flag_row, positions):
    ends = jnp.cumsum(doc_row)
    starts = ends - doc_row
    inside = (positions[:, None] >= starts[None, :]) & (positions[:, None] < ends[None, :])
    return jnp.sum(jnp.where(inside, flag_row[None, :], 0), axis=1)


def shards(inputs, weights, cotangent, doc_lengths, kept_flags):
    seq_count = lax.axis_size("seq")
    chips = lax.axis_size("dp") // CORES
    rest = seq_count // PAIR
    place = lax.axis_index("seq")
    tokens = inputs[0]
    local = tokens.shape[0]
    qwidth = cotangent.shape[2]
    shard_rows, cols = weights.shape
    width = shard_rows // seq_count
    back = -(-(local * seq_count // 2 - 1) // local)

    own = lax.dynamic_slice_in_dim(weights, place * width, width, 0)
    mine_own, mine_across, sent, near = split_tokens(tokens, chips, rest, width)

    blocks, near = lax.optimization_barrier((weights, near))
    blocks = blocks.reshape(seq_count, width, cols)
    groups_own, groups_near = [
        [[lax.dynamic_index_in_dim(blocks, p, 0, keepdims=False) for p in own_places(rest, flip)]] for flip in range(PAIR)
    ]
    arrived = {}
    for k in sorted(range(1, chips), key=lambda k: (-abs(2 * k - chips), k)):
        first = shift_chip(own, k)
        if not arrived:
            first, sent = lax.optimization_barrier((first, sent))
        if k == chips // 2:
            first, arrived = lax.optimization_barrier((first, arrived))
        arrived[k] = [first] + [shift_rest(first, j) for j in range(1, rest)]
    far_other = swap_x(sent)
    groups_own += [arrived[k] for k in range(1, chips)]
    last = groups_own[chips // 2]
    last[-1], far_other = lax.optimization_barrier((last[-1], far_other))
    groups_across = [[swap_core(piece) for piece in group] for group in groups_own]
    groups_near.append([swap_core(piece) for piece in groups_near[0]])
    groups = groups_own + groups_across
    groups_far = groups_own[1:] + groups_across[1:]

    query_sent, pair_sent = project([far_other], groups_far, qwidth, BF16)
    pair_from, query_from = swap_x(pair_sent), swap_x(query_sent)
    query, pair = project([mine_own, mine_across, near], groups + groups_near, qwidth, F32)
    pair = (pair + pair_from.astype(F32)).astype(BF16)

    doc_row, flag_row = doc_lengths[0], kept_flags[0]
    positions = place * local + lax.iota(jnp.int32, local)
    kept = kept_rows(doc_row, flag_row, positions)
    cot = jnp.where(kept[:, None] > 0, cotangent[0], jnp.zeros_like(cotangent[0]))

    near, _ = lax.optimization_barrier((near, pair))
    near_other = swap_x(near)
    pairs = [shift_seq(pair, j) for j in range(back, 0, -1)] + [pair]
    attention, dquery, dpair, dback = attend(doc_row, query, query_from, cot, pairs)

    dquery_sent, near_other = lax.optimization_barrier((dquery, near_other))
    dquery_other = swap_x(dquery_sent)
    for j in range(1, back + 1):
        sent = dback[(back - j) * local : (back - j + 1) * local]
        dpair = dpair + shift_seq(sent, -j).astype(F32)
    dpair = dpair.astype(BF16)
    dpair_other = swap_x(dpair)

    left = [[mine_own], [far_other, near_other]]
    left += [[swap_core(mine_across)], [swap_core(far_other), swap_core(near_other)]]
    right = [[dquery, dpair], [dquery_other, dpair_other]]
    right += [[swap_core(g) for g in group] for group in right]
    order = sorted(range(chips), key=lambda k: (k == 0, -min(k, chips - k), k))
    parts, after = [], dpair
    for steps in (order[: chips // 2], order[chips // 2 :]):
        terms = weight_terms(steps, rest, width, chips, left, right, after)
        if not parts:
            grad_sent, after = width_grad(dquery_other, dpair_other, [groups_far])
            grad_from = swap_x(grad_sent)
        for i, k in enumerate(steps):
            part, *sent = terms[i * rest : (i + 1) * rest]
            received = [shift_rest(piece, -j) for j, piece in enumerate(sent, 1)]
            if k:
                part = functools.reduce(jnp.add, [term.astype(F32) for term in received], part)
                parts.append(shift_chip(part.astype(BF16), -k))
            else:
                parts += [part, *received]

    grad_mine, grad_near, _ = width_grad(dquery, dpair, [groups, groups_near])
    inputs_grad, weights_grad = finish([grad_mine, grad_from, grad_near], parts, chips, rest, width)
    return (attention[None], inputs_grad[None], weights_grad)


def solution(mesh):
    in_specs = (
        P("dp", "seq", None),
        P("dp", None),
        P("dp", "seq", None),
        P("dp", None),
        P("dp", None),
    )
    out_specs = (P("dp", "seq", None), P("dp", "seq", None), P(("dp", "seq"), None))
    return jax.shard_map(shards, mesh=mesh, in_specs=in_specs, out_specs=out_specs, check_vma=False)
```

```python
import functools
import math

import jax
import jax.numpy as jnp
from jax import lax
from jax.experimental import pallas as pl
from jax.experimental.pallas import tpu as pltpu
from jax.sharding import PartitionSpec as P

HEAD_DIM = 128
PAIR = 2
CORES = 2
BF16 = jnp.bfloat16
F32 = jnp.float32
NT = (((1,), (1,)), ((), ()))
TN = (((0,), (0,)), ((), ()))
VMEM = pl.BlockSpec(memory_space=pltpu.VMEM)
SMEM = pl.BlockSpec(memory_space=pltpu.SMEM)


def dot(a, b, dims=(((1,), (0,)), ((), ()))):
    return lax.dot_general(a, b, dims, preferred_element_type=F32)


def swap_x(array):
    count = lax.axis_size("seq")
    return lax.ppermute(array, "seq", [(i, i ^ 1) for i in range(count)])


def shift_rest(array, step):
    count = lax.axis_size("seq")
    rest = count // PAIR
    pairs = [(i, PAIR * ((i // PAIR + step) % rest) + i % PAIR) for i in range(count)]
    return lax.ppermute(array, "seq", pairs)


def swap_core(array):
    count = lax.axis_size("dp")
    return lax.ppermute(array, "dp", [(i, i ^ 1) for i in range(count)])


def shift_chip(array, step):
    count = lax.axis_size("dp")
    chips = count // CORES
    pairs = [(i, CORES * ((i // CORES + step) % chips) + i % CORES) for i in range(count)]
    return lax.ppermute(array, "dp", pairs)


def shift_seq(array, step):
    count = lax.axis_size("seq")
    pairs = [(i, i + step) for i in range(count) if 0 <= i + step < count]
    return lax.ppermute(array, "seq", pairs)


def block_order(chips, rest, flip, steps):
    dp_index, place = lax.axis_index("dp"), lax.axis_index("seq")
    chip, core = dp_index // CORES, dp_index % CORES
    around, x = place // PAIR, (place + flip) % PAIR
    order = []
    for c in range(CORES):
        for k in steps:
            for j in range(rest):
                shard = CORES * ((chip - k + chips) % chips) + (core + c) % CORES
                order.append(shard * (PAIR * rest) + PAIR * ((around - j + rest) % rest) + x)
    return order


def whole_order(chips, rest):
    far = range(1, chips)
    return [block_order(chips, rest, flip, steps) for flip, steps in ((0, range(chips)), (1, far), (1, range(1)))]


def split_order(chips, rest):
    mine, *others = whole_order(chips, rest)
    half = len(mine) // CORES
    return [mine[:half], mine[half:], *others]


def lanes(index, width):
    return pl.ds(pl.multiple_of(index * width, width), width)


def split_kernel(chips, rest, width, tokens_ref, *out_refs):
    for ref, order in zip(out_refs, split_order(chips, rest)):
        for i, block in enumerate(order):
            ref[:, i * width : (i + 1) * width] = tokens_ref[:, lanes(block, width)]


def own_places(rest, flip):
    place = lax.axis_index("seq")
    return [PAIR * ((place // PAIR - j + rest) % rest) + (place + flip) % PAIR for j in range(rest)]


def split_tokens(tokens, chips, rest, width):
    rows, total = tokens.shape
    half = total // PAIR
    near = half // chips
    widths = [half // CORES] * CORES + [half - near, near]
    if width % 128:
        order = jnp.stack(sum(whole_order(chips, rest), []))
        taken = jnp.take(tokens.reshape(rows, total // width, width), order, axis=1).reshape(rows, total)
        return jnp.split(taken, [half // CORES, half, total - near], axis=1)
    tile = min(rows, 128)
    return pl.pallas_call(
        functools.partial(split_kernel, chips, rest, width),
        grid=(rows // tile,),
        in_specs=[pl.BlockSpec((tile, total), lambda i: (i, 0))],
        out_specs=[pl.BlockSpec((tile, w), lambda i: (i, 0)) for w in widths],
        out_shape=[jax.ShapeDtypeStruct((rows, w), tokens.dtype) for w in widths],
        name="split_tokens",
    )(tokens)


def finish_kernel(chips, rest, width, *refs):
    part_refs, term_refs, (out_ref, sum_ref, total_ref, sems) = refs[:3], refs[3:-4], refs[-4:]
    copies = []
    for ref, order in zip(part_refs, whole_order(chips, rest)):
        for i, block in enumerate(order):
            source = ref.at[:, pl.ds(i * width, width)]
            target = out_ref.at[:, lanes(block, width)]
            copies.append(pltpu.make_async_copy(source, target, sems.at[len(copies)]))
    for copy in copies:
        copy.start()
    total = term_refs[0][...].astype(F32)
    for ref in term_refs[1:]:
        total = total + ref[...].astype(F32)
    total_ref[...] = total
    copies.append(pltpu.make_async_copy(total_ref, sum_ref, sems.at[len(copies)]))
    copies[-1].start()
    for copy in copies:
        copy.wait()


def finish(parts, terms, chips, rest, width):
    rows = parts[0].shape[0]
    total = sum(part.shape[1] for part in parts)
    count = total // width
    if width % 128:
        order = jnp.stack(sum(whole_order(chips, rest), []))
        where = jnp.zeros_like(order).at[order].set(lax.iota(order.dtype, count))
        blocks = jnp.concatenate(parts, axis=1).reshape(rows, count, width)
        summed = functools.reduce(jnp.add, [term.astype(F32) for term in terms])
        return jnp.take(blocks, where, axis=1).reshape(rows, total), summed
    return pl.pallas_call(
        functools.partial(finish_kernel, chips, rest, width),
        in_specs=[VMEM] * (len(parts) + len(terms)),
        out_specs=[pl.BlockSpec(memory_space=pl.ANY)] * 2,
        out_shape=[
            jax.ShapeDtypeStruct((rows, total), BF16),
            jax.ShapeDtypeStruct(terms[0].shape, F32),
        ],
        scratch_shapes=[pltpu.VMEM(terms[0].shape, F32), pltpu.SemaphoreType.DMA((count + 1,))],
        compiler_params=pltpu.CompilerParams(vmem_limit_bytes=20 * 2**20),
        name="finish",
    )(*parts, *terms)


def cut(parts, first, step):
    for part in parts:
        if first < part.shape[1]:
            return part[:, first : first + step]
        first -= part.shape[1]


def project_kernel(span, per, cuts, count, *refs):
    tokens, pieces, out_refs = refs[:count], refs[count : -len(cuts)], refs[-len(cuts) :]
    low, high = cuts[0][0], cuts[-1][1]
    total = None
    for g in range(len(pieces) // per):
        rows = jnp.concatenate([r[:, low:high] for r in pieces[g * per : (g + 1) * per]], axis=0)
        term = dot(cut(tokens, g * span, span), rows)
        total = term if total is None else total + term
    for (first, end), ref in zip(cuts, out_refs):
        ref[...] = total[:, first - low : end - low].astype(ref.dtype)


def project(tokens, groups, cuts, kind):
    rows = tokens[0].shape[0]
    pieces = [piece for group in groups for piece in group]
    span = sum(piece.shape[0] for piece in groups[0])
    return pl.pallas_call(
        functools.partial(project_kernel, span, len(groups[0]), cuts, len(tokens)),
        in_specs=[VMEM] * (len(tokens) + len(pieces)),
        out_specs=[VMEM] * len(cuts),
        out_shape=[jax.ShapeDtypeStruct((rows, end - first), kind) for first, end in cuts],
        compiler_params=pltpu.CompilerParams(vmem_limit_bytes=20 * 2**20),
        name="project",
    )(*tokens, *pieces)


def grad_kernel(span, counts, dquery_ref, dpair_ref, *refs):
    pieces, outs, mark_ref = refs[: -len(counts) - 1], refs[-len(counts) - 1 : -1], refs[-1]
    grads = jnp.concatenate([dquery_ref[...], dpair_ref[...]], axis=1)
    per = len(pieces) // sum(counts)
    for out_ref, count in zip(outs, counts):
        for i in range(count):
            rows = jnp.concatenate([r[...] for r in pieces[:per]], axis=0)
            pieces = pieces[per:]
            out_ref[:, i * span : (i + 1) * span] = dot(grads, rows, NT).astype(BF16)
    mark_ref[...] = grads[:16, :128]


def width_grad(dquery, dpair, parts):
    rows = dquery.shape[0]
    pieces = [piece for groups in parts for group in groups for piece in group]
    span = sum(piece.shape[0] for piece in parts[0][0])
    counts = [len(groups) for groups in parts]
    return pl.pallas_call(
        functools.partial(grad_kernel, span, counts),
        in_specs=[VMEM] * (2 + len(pieces)),
        out_specs=[VMEM] * (len(parts) + 1),
        out_shape=[jax.ShapeDtypeStruct((rows, span * count), BF16) for count in counts]
        + [jax.ShapeDtypeStruct((16, 128), BF16)],
        compiler_params=pltpu.CompilerParams(vmem_limit_bytes=20 * 2**20),
        name="width_grad",
    )(dquery, dpair, *pieces)


def weight_kernel(steps, rest, width, chips, sources, grads, *refs):
    tokens, refs = refs[: sum(sources)], refs[sum(sources) :]
    rights = [jnp.concatenate([r[...] for r in refs[i : i + grads]], axis=1) for i in range(0, grads * len(sources), grads)]
    right = jnp.concatenate(rights, axis=0)
    outs = refs[grads * len(sources) + 1 :]
    span = rest * width
    for i, k in enumerate(steps):
        left, at = [], 0
        for core, count in enumerate(sources):
            parts, at = tokens[at : at + count], at + count
            if count == 1:
                left.append(parts[0][:, k * span : (k + 1) * span])
            else:
                far, near = parts
                across = core // CORES
                first = across if k == 0 else across * (chips - 1) + k - 1
                left.append((far if k else near)[:, first * span : (first + 1) * span])
        total = dot(jnp.concatenate(left, axis=0).T, right)
        for j in range(rest):
            out = outs[i * rest + j]
            out[...] = total[j * width : (j + 1) * width].astype(out.dtype)


def weight_terms(steps, rest, width, chips, tokens, grads, after):
    cols = sum(g.shape[1] for g in grads[0])
    sources = [len(parts) for parts in tokens]
    parts = [part for group in tokens for part in group]
    given = [g for group in grads for g in group]
    return pl.pallas_call(
        functools.partial(weight_kernel, steps, rest, width, chips, sources, len(grads[0])),
        in_specs=[VMEM] * (len(parts) + len(given) + 1),
        out_specs=[VMEM] * (len(steps) * rest),
        out_shape=[jax.ShapeDtypeStruct((width, cols), BF16 if j else F32) for _ in steps for j in range(rest)],
        compiler_params=pltpu.CompilerParams(vmem_limit_bytes=20 * 2**20),
        name="weight_terms",
    )(*parts, *given, after)


def attend_kernel(heads, back, docs_ref, q_ref, q_from_ref, cot_ref, *refs):
    pair_refs, (out_ref, dq_ref, dpair_ref, dback_ref) = refs[: back + 1], refs[back + 1 :]
    rows = q_ref.shape[0]
    hd = HEAD_DIM
    scale = 1.0 / math.sqrt(hd)
    first = lax.axis_index("seq") * rows
    total = (back + 1) * rows

    row_pos = first + lax.broadcasted_iota(jnp.int32, (1, rows), 1)
    start_of = jnp.zeros((1, rows), jnp.int32)
    start = jnp.int32(0)
    for d in range(docs_ref.shape[0]):
        end = start + docs_ref[d]
        start_of = jnp.where((row_pos >= start) & (row_pos < end), start, start_of)
        start = end
    key_pos = first - back * rows + lax.broadcasted_iota(jnp.int32, (total, rows), 0)
    shut = jnp.where((key_pos >= start_of) & (key_pos <= row_pos), 0.0, -1e30)

    pairs = [r[...] for r in pair_refs]
    keys = jnp.concatenate([p[:, :hd] for p in pairs], axis=0)
    values = jnp.concatenate([p[:, hd:] for p in pairs], axis=0)
    keys_t, values_t = keys.T, values.T
    sums = [jnp.zeros((total, hd), F32), jnp.zeros((total, hd), F32)]
    cols = [slice(h * hd, (h + 1) * hd) for h in range(heads)]
    state = {}

    def products(h):
        q = (q_ref[:, cols[h]] + q_from_ref[:, cols[h]].astype(F32)).astype(BF16)
        cot = cot_ref[:, cols[h]]
        state[h] = [q, cot, dot(keys, q, NT), dot(values, cot, NT)]

    def softmax(h):
        logits = state[h][2] * (scale * math.log2(math.e)) + shut
        raised = jnp.exp2(logits - jnp.max(logits, axis=0, keepdims=True))
        probs = raised * (1.0 / jnp.sum(raised, axis=0, keepdims=True))
        state[h][2] = probs
        state[h].append(probs.astype(BF16))

    def outputs(h):
        _, cot, _, _, probs_half = state[h]
        out_t = dot(values_t, probs_half).astype(BF16)
        out_ref[:, cols[h]] = out_t.T
        state[h].append(jnp.sum(cot.T.astype(F32) * out_t.astype(F32), axis=0, keepdims=True))

    def score_grads(h):
        _, _, probs, dprobs, _, delta = state[h]
        state[h][3] = (probs * (dprobs - delta)).astype(BF16)

    def grads(h):
        q, cot, _, dscores, probs_half, _ = state.pop(h)
        dq_ref[:, cols[h]] = (dot(keys_t, dscores) * scale).astype(BF16).T
        sums[0] = sums[0] + dot(dscores, q)
        sums[1] = sums[1] + dot(probs_half, cot)

    products(0)
    for h in range(heads):
        softmax(h)
        if h + 1 < heads:
            products(h + 1)
        outputs(h)
        if h:
            grads(h - 1)
        score_grads(h)
    grads(heads - 1)
    both = jnp.concatenate([sums[0] * scale, sums[1]], axis=1)
    dpair_ref[...] = both[back * rows :]
    dback_ref[...] = both[: back * rows].astype(BF16)


def attend(docs, q, q_from, cot, pairs):
    rows, width = q.shape
    back = len(pairs) - 1
    two = 2 * HEAD_DIM
    return pl.pallas_call(
        functools.partial(attend_kernel, width // HEAD_DIM, back),
        in_specs=[SMEM] + [VMEM] * (back + 4),
        out_specs=[VMEM] * 4,
        out_shape=[
            jax.ShapeDtypeStruct((rows, width), BF16),
            jax.ShapeDtypeStruct((rows, width), BF16),
            jax.ShapeDtypeStruct((rows, two), F32),
            jax.ShapeDtypeStruct((back * rows, two), BF16),
        ],
        compiler_params=pltpu.CompilerParams(vmem_limit_bytes=20 * 2**20),
        name="attend",
    )(docs, q, q_from, cot, *pairs)


def kept_rows(doc_row, flag_row, positions):
    ends = jnp.cumsum(doc_row)
    starts = ends - doc_row
    inside = (positions[:, None] >= starts[None, :]) & (positions[:, None] < ends[None, :])
    return jnp.sum(jnp.where(inside, flag_row[None, :], 0), axis=1)


def shards(inputs, weights, cotangent, doc_lengths, kept_flags):
    seq_count = lax.axis_size("seq")
    chips = lax.axis_size("dp") // CORES
    rest = seq_count // PAIR
    place = lax.axis_index("seq")
    tokens = inputs[0]
    local = tokens.shape[0]
    qwidth = cotangent.shape[2]
    shard_rows, cols = weights.shape
    width = shard_rows // seq_count
    back = -(-(local * seq_count // 2 - 1) // local)

    own = lax.dynamic_slice_in_dim(weights, place * width, width, 0)
    mine_own, mine_across, sent, near = split_tokens(tokens, chips, rest, width)

    blocks, near = lax.optimization_barrier((weights, near))
    blocks = blocks.reshape(seq_count, width, cols)
    groups_own, groups_near = [
        [[lax.dynamic_index_in_dim(blocks, p, 0, keepdims=False) for p in own_places(rest, flip)]] for flip in range(PAIR)
    ]
    arrived = {}
    for k in sorted(range(1, chips), key=lambda k: (-abs(2 * k - chips), k)):
        first = shift_chip(own, k)
        if not arrived:
            first, sent = lax.optimization_barrier((first, sent))
        if k == chips // 2:
            first, arrived = lax.optimization_barrier((first, arrived))
        arrived[k] = [first] + [shift_rest(first, j) for j in range(1, rest)]
    far_other = swap_x(sent)
    groups_own += [arrived[k] for k in range(1, chips)]
    last = groups_own[chips // 2]
    last[-1], far_other = lax.optimization_barrier((last[-1], far_other))
    groups_across = [[swap_core(piece) for piece in group] for group in groups_own]
    groups_near.append([swap_core(piece) for piece in groups_near[0]])
    groups = groups_own + groups_across
    groups_far = groups_own[1:] + groups_across[1:]

    query_cut, pair_cut = (0, qwidth), (qwidth, cols)
    (pair_sent,) = project([far_other], groups_far, [pair_cut], BF16)
    (query_sent,) = project([far_other], groups_far, [query_cut], BF16)
    pair_from, query_from = swap_x(pair_sent), swap_x(query_sent)
    query, pair = project([mine_own, mine_across, near], groups + groups_near, [query_cut, pair_cut], F32)
    pair = (pair + pair_from.astype(F32)).astype(BF16)

    doc_row, flag_row = doc_lengths[0], kept_flags[0]
    positions = place * local + lax.iota(jnp.int32, local)
    kept = kept_rows(doc_row, flag_row, positions)
    cot = jnp.where(kept[:, None] > 0, cotangent[0], jnp.zeros_like(cotangent[0]))

    near, _ = lax.optimization_barrier((near, pair))
    near_other = swap_x(near)
    pairs = [shift_seq(pair, j) for j in range(back, 0, -1)] + [pair]
    attention, dquery, dpair, dback = attend(doc_row, query, query_from, cot, pairs)

    dquery_sent, near_other = lax.optimization_barrier((dquery, near_other))
    dquery_other = swap_x(dquery_sent)
    for j in range(1, back + 1):
        sent = dback[(back - j) * local : (back - j + 1) * local]
        dpair = dpair + shift_seq(sent, -j).astype(F32)
    dpair = dpair.astype(BF16)
    dpair_other = swap_x(dpair)

    left = [[mine_own], [far_other, near_other]]
    left += [[swap_core(mine_across)], [swap_core(far_other), swap_core(near_other)]]
    right = [[dquery, dpair], [dquery_other, dpair_other]]
    right += [[swap_core(g) for g in group] for group in right]
    order = sorted(range(chips), key=lambda k: (k == 0, -min(k, chips - k), k))
    parts, after = [], dpair
    for steps in (order[:1], order[1:]):
        terms = weight_terms(steps, rest, width, chips, left, right, after)
        if not parts:
            grad_sent, after = width_grad(dquery_other, dpair_other, [groups_far])
            grad_from = swap_x(grad_sent)
        for i, k in enumerate(steps):
            part, *sent = terms[i * rest : (i + 1) * rest]
            received = [shift_rest(piece, -j) for j, piece in enumerate(sent, 1)]
            if k:
                part = functools.reduce(jnp.add, [term.astype(F32) for term in received], part)
                parts.append(shift_chip(part.astype(BF16), -k))
            else:
                parts += [part, *received]

    grad_mine, grad_near, _ = width_grad(dquery, dpair, [groups, groups_near])
    inputs_grad, weights_grad = finish([grad_mine, grad_from, grad_near], parts, chips, rest, width)
    return (attention[None], inputs_grad[None], weights_grad)


def solution(mesh):
    in_specs = (
        P("dp", "seq", None),
        P("dp", None),
        P("dp", "seq", None),
        P("dp", None),
        P("dp", None),
    )
    out_specs = (P("dp", "seq", None), P("dp", "seq", None), P(("dp", "seq"), None))
    return jax.shard_map(shards, mesh=mesh, in_specs=in_specs, out_specs=out_specs, check_vma=False)
```

```python
import functools
import math

import jax
import jax.numpy as jnp
from jax import lax
from jax.experimental import pallas as pl
from jax.experimental.pallas import tpu as pltpu
from jax.sharding import PartitionSpec as P

HEAD_DIM = 128
PAIR = 2
CORES = 2
BF16 = jnp.bfloat16
F32 = jnp.float32
NT = (((1,), (1,)), ((), ()))
TN = (((0,), (0,)), ((), ()))
VMEM = pl.BlockSpec(memory_space=pltpu.VMEM)
SMEM = pl.BlockSpec(memory_space=pltpu.SMEM)


def dot(a, b, dims=(((1,), (0,)), ((), ()))):
    return lax.dot_general(a, b, dims, preferred_element_type=F32)


def swap_x(array):
    count = lax.axis_size("seq")
    return lax.ppermute(array, "seq", [(i, i ^ 1) for i in range(count)])


def shift_rest(array, step):
    count = lax.axis_size("seq")
    rest = count // PAIR
    pairs = [(i, PAIR * ((i // PAIR + step) % rest) + i % PAIR) for i in range(count)]
    return lax.ppermute(array, "seq", pairs)


def swap_core(array):
    count = lax.axis_size("dp")
    return lax.ppermute(array, "dp", [(i, i ^ 1) for i in range(count)])


def shift_chip(array, step):
    count = lax.axis_size("dp")
    chips = count // CORES
    pairs = [(i, CORES * ((i // CORES + step) % chips) + i % CORES) for i in range(count)]
    return lax.ppermute(array, "dp", pairs)


def shift_seq(array, step):
    count = lax.axis_size("seq")
    pairs = [(i, i + step) for i in range(count) if 0 <= i + step < count]
    return lax.ppermute(array, "seq", pairs)


def block_order(chips, rest, flip, steps):
    dp_index, place = lax.axis_index("dp"), lax.axis_index("seq")
    chip, core = dp_index // CORES, dp_index % CORES
    around, x = place // PAIR, (place + flip) % PAIR
    order = []
    for c in range(CORES):
        for k in steps:
            for j in range(rest):
                shard = CORES * ((chip - k + chips) % chips) + (core + c) % CORES
                order.append(shard * (PAIR * rest) + PAIR * ((around - j + rest) % rest) + x)
    return order


def whole_order(chips, rest):
    far = range(1, chips)
    return [block_order(chips, rest, flip, steps) for flip, steps in ((0, range(chips)), (1, far), (1, range(1)))]


def split_order(chips, rest):
    mine, *others = whole_order(chips, rest)
    half = len(mine) // CORES
    return [mine[:half], mine[half:], *others]


def lanes(index, width):
    return pl.ds(pl.multiple_of(index * width, width), width)


def split_kernel(chips, rest, width, tokens_ref, *out_refs):
    for ref, order in zip(out_refs, split_order(chips, rest)):
        for i, block in enumerate(order):
            ref[:, i * width : (i + 1) * width] = tokens_ref[:, lanes(block, width)]


def own_places(rest, flip):
    place = lax.axis_index("seq")
    return [PAIR * ((place // PAIR - j + rest) % rest) + (place + flip) % PAIR for j in range(rest)]


def split_tokens(tokens, chips, rest, width):
    rows, total = tokens.shape
    half = total // PAIR
    near = half // chips
    widths = [half // CORES] * CORES + [half - near, near]
    if width % 128:
        order = jnp.stack(sum(whole_order(chips, rest), []))
        taken = jnp.take(tokens.reshape(rows, total // width, width), order, axis=1).reshape(rows, total)
        return jnp.split(taken, [half // CORES, half, total - near], axis=1)
    tile = min(rows, 128)
    return pl.pallas_call(
        functools.partial(split_kernel, chips, rest, width),
        grid=(rows // tile,),
        in_specs=[pl.BlockSpec((tile, total), lambda i: (i, 0))],
        out_specs=[pl.BlockSpec((tile, w), lambda i: (i, 0)) for w in widths],
        out_shape=[jax.ShapeDtypeStruct((rows, w), tokens.dtype) for w in widths],
        name="split_tokens",
    )(tokens)


def finish_kernel(chips, rest, width, *refs):
    part_refs, term_refs, (out_ref, sum_ref, total_ref, sems) = refs[:3], refs[3:-4], refs[-4:]
    copies = []
    for ref, order in zip(part_refs, whole_order(chips, rest)):
        for i, block in enumerate(order):
            source = ref.at[:, pl.ds(i * width, width)]
            target = out_ref.at[:, lanes(block, width)]
            copies.append(pltpu.make_async_copy(source, target, sems.at[len(copies)]))
    for copy in copies:
        copy.start()
    total = term_refs[0][...].astype(F32)
    for ref in term_refs[1:]:
        total = total + ref[...].astype(F32)
    total_ref[...] = total
    copies.append(pltpu.make_async_copy(total_ref, sum_ref, sems.at[len(copies)]))
    copies[-1].start()
    for copy in copies:
        copy.wait()


def finish(parts, terms, chips, rest, width):
    rows = parts[0].shape[0]
    total = sum(part.shape[1] for part in parts)
    count = total // width
    if width % 128:
        order = jnp.stack(sum(whole_order(chips, rest), []))
        where = jnp.zeros_like(order).at[order].set(lax.iota(order.dtype, count))
        blocks = jnp.concatenate(parts, axis=1).reshape(rows, count, width)
        summed = functools.reduce(jnp.add, [term.astype(F32) for term in terms])
        return jnp.take(blocks, where, axis=1).reshape(rows, total), summed
    return pl.pallas_call(
        functools.partial(finish_kernel, chips, rest, width),
        in_specs=[VMEM] * (len(parts) + len(terms)),
        out_specs=[pl.BlockSpec(memory_space=pl.ANY)] * 2,
        out_shape=[
            jax.ShapeDtypeStruct((rows, total), BF16),
            jax.ShapeDtypeStruct(terms[0].shape, F32),
        ],
        scratch_shapes=[pltpu.VMEM(terms[0].shape, F32), pltpu.SemaphoreType.DMA((count + 1,))],
        compiler_params=pltpu.CompilerParams(vmem_limit_bytes=20 * 2**20),
        name="finish",
    )(*parts, *terms)


def cut(parts, first, step):
    for part in parts:
        if first < part.shape[1]:
            return part[:, first : first + step]
        first -= part.shape[1]


def project_kernel(span, per, cuts, count, *refs):
    tokens, pieces, out_refs = refs[:count], refs[count : -len(cuts)], refs[-len(cuts) :]
    low, high = cuts[0][0], cuts[-1][1]
    total = None
    for g in range(len(pieces) // per):
        rows = jnp.concatenate([r[:, low:high] for r in pieces[g * per : (g + 1) * per]], axis=0)
        term = dot(cut(tokens, g * span, span), rows)
        total = term if total is None else total + term
    for (first, end), ref in zip(cuts, out_refs):
        ref[...] = total[:, first - low : end - low].astype(ref.dtype)


def project(tokens, groups, cuts, kind):
    rows = tokens[0].shape[0]
    pieces = [piece for group in groups for piece in group]
    span = sum(piece.shape[0] for piece in groups[0])
    return pl.pallas_call(
        functools.partial(project_kernel, span, len(groups[0]), cuts, len(tokens)),
        in_specs=[VMEM] * (len(tokens) + len(pieces)),
        out_specs=[VMEM] * len(cuts),
        out_shape=[jax.ShapeDtypeStruct((rows, end - first), kind) for first, end in cuts],
        compiler_params=pltpu.CompilerParams(vmem_limit_bytes=20 * 2**20),
        name="project",
    )(*tokens, *pieces)


def grad_kernel(span, counts, dquery_ref, dpair_ref, *refs):
    pieces, outs, mark_ref = refs[: -len(counts) - 1], refs[-len(counts) - 1 : -1], refs[-1]
    grads = jnp.concatenate([dquery_ref[...], dpair_ref[...]], axis=1)
    per = len(pieces) // sum(counts)
    for out_ref, count in zip(outs, counts):
        for i in range(count):
            rows = jnp.concatenate([r[...] for r in pieces[:per]], axis=0)
            pieces = pieces[per:]
            out_ref[:, i * span : (i + 1) * span] = dot(grads, rows, NT).astype(BF16)
    mark_ref[...] = grads[:16, :128]


def width_grad(dquery, dpair, parts):
    rows = dquery.shape[0]
    pieces = [piece for groups in parts for group in groups for piece in group]
    span = sum(piece.shape[0] for piece in parts[0][0])
    counts = [len(groups) for groups in parts]
    return pl.pallas_call(
        functools.partial(grad_kernel, span, counts),
        in_specs=[VMEM] * (2 + len(pieces)),
        out_specs=[VMEM] * (len(parts) + 1),
        out_shape=[jax.ShapeDtypeStruct((rows, span * count), BF16) for count in counts]
        + [jax.ShapeDtypeStruct((16, 128), BF16)],
        compiler_params=pltpu.CompilerParams(vmem_limit_bytes=20 * 2**20),
        name="width_grad",
    )(dquery, dpair, *pieces)


def weight_kernel(steps, whole, rest, width, chips, sources, grads, *refs):
    tokens, refs = refs[: sum(sources)], refs[sum(sources) :]
    rights = [jnp.concatenate([r[...] for r in refs[i : i + grads]], axis=1) for i in range(0, grads * len(sources), grads)]
    right = jnp.concatenate(rights, axis=0)
    outs = refs[grads * len(sources) + 1 :]
    span = rest * width
    for i, k in enumerate(steps):
        left, at = [], 0
        for core, count in enumerate(sources):
            parts, at = tokens[at : at + count], at + count
            if count == 1:
                left.append(parts[0][:, k * span : (k + 1) * span])
            else:
                far, near = parts
                across = core // CORES
                first = across if k == 0 else across * (chips - 1) + k - 1
                left.append((far if k else near)[:, first * span : (first + 1) * span])
        total = dot(jnp.concatenate(left, axis=0).T, right)
        here = 1 if k == whole else rest
        rows = total.shape[0] // here
        for j in range(here):
            outs[j][...] = total[j * rows : (j + 1) * rows].astype(outs[j].dtype)
        outs = outs[here:]


def weight_terms(steps, whole, rest, width, chips, tokens, grads, after):
    cols = sum(g.shape[1] for g in grads[0])
    sources = [len(parts) for parts in tokens]
    parts = [part for group in tokens for part in group]
    given = [g for group in grads for g in group]
    shapes = []
    for k in steps:
        if k == whole:
            shapes.append(jax.ShapeDtypeStruct((rest * width, cols), BF16))
        else:
            shapes += [jax.ShapeDtypeStruct((width, cols), BF16 if j else F32) for j in range(rest)]
    return pl.pallas_call(
        functools.partial(weight_kernel, steps, whole, rest, width, chips, sources, len(grads[0])),
        in_specs=[VMEM] * (len(parts) + len(given) + 1),
        out_specs=[VMEM] * len(shapes),
        out_shape=shapes,
        compiler_params=pltpu.CompilerParams(vmem_limit_bytes=20 * 2**20),
        name="weight_terms",
    )(*parts, *given, after)


def attend_kernel(heads, back, docs_ref, q_ref, q_from_ref, cot_ref, *refs):
    pair_refs, (out_ref, dq_ref, dpair_ref, dback_ref) = refs[: back + 1], refs[back + 1 :]
    rows = q_ref.shape[0]
    hd = HEAD_DIM
    scale = 1.0 / math.sqrt(hd)
    first = lax.axis_index("seq") * rows
    total = (back + 1) * rows

    row_pos = first + lax.broadcasted_iota(jnp.int32, (1, rows), 1)
    start_of = jnp.zeros((1, rows), jnp.int32)
    start = jnp.int32(0)
    for d in range(docs_ref.shape[0]):
        end = start + docs_ref[d]
        start_of = jnp.where((row_pos >= start) & (row_pos < end), start, start_of)
        start = end
    key_pos = first - back * rows + lax.broadcasted_iota(jnp.int32, (total, rows), 0)
    shut = jnp.where((key_pos >= start_of) & (key_pos <= row_pos), 0.0, -1e30)

    pairs = [r[...] for r in pair_refs]
    keys = jnp.concatenate([p[:, :hd] for p in pairs], axis=0)
    values = jnp.concatenate([p[:, hd:] for p in pairs], axis=0)
    keys_t, values_t = keys.T, values.T
    sums = [jnp.zeros((total, hd), F32), jnp.zeros((total, hd), F32)]
    cols = [slice(h * hd, (h + 1) * hd) for h in range(heads)]
    state = {}

    def products(h):
        q = (q_ref[:, cols[h]] + q_from_ref[:, cols[h]].astype(F32)).astype(BF16)
        cot = cot_ref[:, cols[h]]
        state[h] = [q, cot, dot(keys, q, NT), dot(values, cot, NT)]

    def softmax(h):
        logits = state[h][2] * (scale * math.log2(math.e)) + shut
        raised = jnp.exp2(logits - jnp.max(logits, axis=0, keepdims=True))
        probs = raised * (1.0 / jnp.sum(raised, axis=0, keepdims=True))
        state[h][2] = probs
        state[h].append(probs.astype(BF16))

    def outputs(h):
        _, cot, _, _, probs_half = state[h]
        out_t = dot(values_t, probs_half).astype(BF16)
        out_ref[:, cols[h]] = out_t.T
        state[h].append(jnp.sum(cot.T.astype(F32) * out_t.astype(F32), axis=0, keepdims=True))

    def score_grads(h):
        _, _, probs, dprobs, _, delta = state[h]
        state[h][3] = (probs * (dprobs - delta)).astype(BF16)

    def grads(h):
        q, cot, _, dscores, probs_half, _ = state.pop(h)
        dq_ref[:, cols[h]] = (dot(keys_t, dscores) * scale).astype(BF16).T
        sums[0] = sums[0] + dot(dscores, q)
        sums[1] = sums[1] + dot(probs_half, cot)

    products(0)
    for h in range(heads):
        softmax(h)
        if h + 1 < heads:
            products(h + 1)
        outputs(h)
        score_grads(h)
        if h:
            grads(h - 1)
    grads(heads - 1)
    both = jnp.concatenate([sums[0] * scale, sums[1]], axis=1)
    dpair_ref[...] = both[back * rows :]
    dback_ref[...] = both[: back * rows].astype(BF16)


def attend(docs, q, q_from, cot, pairs):
    rows, width = q.shape
    back = len(pairs) - 1
    two = 2 * HEAD_DIM
    return pl.pallas_call(
        functools.partial(attend_kernel, width // HEAD_DIM, back),
        in_specs=[SMEM] + [VMEM] * (back + 4),
        out_specs=[VMEM] * 4,
        out_shape=[
            jax.ShapeDtypeStruct((rows, width), BF16),
            jax.ShapeDtypeStruct((rows, width), BF16),
            jax.ShapeDtypeStruct((rows, two), F32),
            jax.ShapeDtypeStruct((back * rows, two), BF16),
        ],
        compiler_params=pltpu.CompilerParams(vmem_limit_bytes=20 * 2**20),
        name="attend",
    )(docs, q, q_from, cot, *pairs)


def kept_rows(doc_row, flag_row, positions):
    ends = jnp.cumsum(doc_row)
    starts = ends - doc_row
    inside = (positions[:, None] >= starts[None, :]) & (positions[:, None] < ends[None, :])
    return jnp.sum(jnp.where(inside, flag_row[None, :], 0), axis=1)


def shards(inputs, weights, cotangent, doc_lengths, kept_flags):
    seq_count = lax.axis_size("seq")
    chips = lax.axis_size("dp") // CORES
    rest = seq_count // PAIR
    place = lax.axis_index("seq")
    tokens = inputs[0]
    local = tokens.shape[0]
    qwidth = cotangent.shape[2]
    shard_rows, cols = weights.shape
    width = shard_rows // seq_count
    back = -(-(local * seq_count // 2 - 1) // local)

    own = lax.dynamic_slice_in_dim(weights, place * width, width, 0)
    mine_own, mine_across, sent, near = split_tokens(tokens, chips, rest, width)

    blocks, near = lax.optimization_barrier((weights, near))
    blocks = blocks.reshape(seq_count, width, cols)
    groups_own, groups_near = [
        [[lax.dynamic_index_in_dim(blocks, p, 0, keepdims=False) for p in own_places(rest, flip)]] for flip in range(PAIR)
    ]
    arrived = {}
    for k in sorted(range(1, chips), key=lambda k: (-abs(2 * k - chips), k)):
        first = shift_chip(own, k)
        if not arrived:
            first, sent = lax.optimization_barrier((first, sent))
        if k == chips // 2:
            first, arrived = lax.optimization_barrier((first, arrived))
        arrived[k] = [first] + [shift_rest(first, j) for j in range(1, rest)]
    far_other = swap_x(sent)
    groups_own += [arrived[k] for k in range(1, chips)]
    last = groups_own[chips // 2]
    last[-1], far_other = lax.optimization_barrier((last[-1], far_other))
    groups_across = [[swap_core(piece) for piece in group] for group in groups_own]
    groups_near.append([swap_core(piece) for piece in groups_near[0]])
    groups = groups_own + groups_across
    groups_far = groups_own[1:] + groups_across[1:]

    query_cut, pair_cut = (0, qwidth), (qwidth, cols)
    (pair_sent,) = project([far_other], groups_far, [pair_cut], BF16)
    (query_sent,) = project([far_other], groups_far, [query_cut], BF16)
    pair_from, query_from = swap_x(pair_sent), swap_x(query_sent)
    query, pair = project([mine_own, mine_across, near], groups + groups_near, [query_cut, pair_cut], F32)
    pair = (pair + pair_from.astype(F32)).astype(BF16)

    doc_row, flag_row = doc_lengths[0], kept_flags[0]
    positions = place * local + lax.iota(jnp.int32, local)
    kept = kept_rows(doc_row, flag_row, positions)
    cot = jnp.where(kept[:, None] > 0, cotangent[0], jnp.zeros_like(cotangent[0]))

    near, _ = lax.optimization_barrier((near, pair_from))
    near_other = swap_x(near)
    pairs = [shift_seq(pair, j) for j in range(back, 0, -1)] + [pair]
    attention, dquery, dpair, dback = attend(doc_row, query, query_from, cot, pairs)

    dquery_sent, near_other = lax.optimization_barrier((dquery, near_other))
    dquery_other = swap_x(dquery_sent)
    for j in range(1, back + 1):
        sent = dback[(back - j) * local : (back - j + 1) * local]
        dpair = dpair + shift_seq(sent, -j).astype(F32)
    dpair = dpair.astype(BF16)
    dpair_other = swap_x(dpair)

    left = [[mine_own], [far_other, near_other]]
    left += [[swap_core(mine_across)], [swap_core(far_other), swap_core(near_other)]]
    right = [[dquery, dpair], [dquery_other, dpair_other]]
    right += [[swap_core(g) for g in group] for group in right]
    order = sorted(range(chips), key=lambda k: (k == 0, -min(k, chips - k), k))
    whole = chips - 1
    steps_left = [k for k in order if k != whole]
    parts, after, joined = [], dpair, None
    for steps in ([whole, steps_left[0]], steps_left[1:]):
        terms = weight_terms(steps, whole, rest, width, chips, left, right, after)
        if joined is None:
            joined, terms = shift_chip(terms[0], -whole), terms[1:]
            steps = steps[1:]
            grad_sent, after = width_grad(dquery_other, dpair_other, [groups_far])
            grad_from = swap_x(grad_sent)
        for i, k in enumerate(steps):
            part, *sent = terms[i * rest : (i + 1) * rest]
            if k == 0:
                extra = [joined[j * width : (j + 1) * width].astype(F32) for j in range(rest)]
                part = part + extra[0]
                sent = [(piece.astype(F32) + more).astype(BF16) for piece, more in zip(sent, extra[1:])]
            received = [shift_rest(piece, -j) for j, piece in enumerate(sent, 1)]
            if k:
                part = functools.reduce(jnp.add, [term.astype(F32) for term in received], part)
                parts.append(shift_chip(part.astype(BF16), -k))
            else:
                parts = [*received, part, *parts]

    grad_mine, grad_near, _ = width_grad(dquery, dpair, [groups, groups_near])
    inputs_grad, weights_grad = finish([grad_mine, grad_from, grad_near], parts, chips, rest, width)
    return (attention[None], inputs_grad[None], weights_grad)


def solution(mesh):
    in_specs = (
        P("dp", "seq", None),
        P("dp", None),
        P("dp", "seq", None),
        P("dp", None),
        P("dp", None),
    )
    out_specs = (P("dp", "seq", None), P("dp", "seq", None), P(("dp", "seq"), None))
    return jax.shard_map(shards, mesh=mesh, in_specs=in_specs, out_specs=out_specs, check_vma=False)
```

```python
import functools
import math

import jax
import jax.numpy as jnp
from jax import lax
from jax.experimental import pallas as pl
from jax.experimental.pallas import tpu as pltpu
from jax.sharding import PartitionSpec as P

HEAD_DIM = 128
PAIR = 2
CORES = 2
BF16 = jnp.bfloat16
F32 = jnp.float32
NT = (((1,), (1,)), ((), ()))
TN = (((0,), (0,)), ((), ()))
VMEM = pl.BlockSpec(memory_space=pltpu.VMEM)
SMEM = pl.BlockSpec(memory_space=pltpu.SMEM)


def dot(a, b, dims=(((1,), (0,)), ((), ()))):
    return lax.dot_general(a, b, dims, preferred_element_type=F32)


def swap_x(array):
    count = lax.axis_size("seq")
    return lax.ppermute(array, "seq", [(i, i ^ 1) for i in range(count)])


def shift_rest(array, step):
    count = lax.axis_size("seq")
    rest = count // PAIR
    pairs = [(i, PAIR * ((i // PAIR + step) % rest) + i % PAIR) for i in range(count)]
    return lax.ppermute(array, "seq", pairs)


def swap_core(array):
    count = lax.axis_size("dp")
    return lax.ppermute(array, "dp", [(i, i ^ 1) for i in range(count)])


def shift_chip(array, step):
    count = lax.axis_size("dp")
    chips = count // CORES
    pairs = [(i, CORES * ((i // CORES + step) % chips) + i % CORES) for i in range(count)]
    return lax.ppermute(array, "dp", pairs)


def shift_seq(array, step):
    count = lax.axis_size("seq")
    pairs = [(i, i + step) for i in range(count) if 0 <= i + step < count]
    return lax.ppermute(array, "seq", pairs)


def block_order(chips, rest, flip, steps):
    dp_index, place = lax.axis_index("dp"), lax.axis_index("seq")
    chip, core = dp_index // CORES, dp_index % CORES
    around, x = place // PAIR, (place + flip) % PAIR
    order = []
    for c in range(CORES):
        for k in steps:
            for j in range(rest):
                shard = CORES * ((chip - k + chips) % chips) + (core + c) % CORES
                order.append(shard * (PAIR * rest) + PAIR * ((around - j + rest) % rest) + x)
    return order


def whole_order(chips, rest):
    far = range(1, chips)
    return [block_order(chips, rest, flip, steps) for flip, steps in ((0, range(chips)), (1, far), (1, range(1)))]


def split_order(chips, rest):
    mine, *others = whole_order(chips, rest)
    half = len(mine) // CORES
    return [mine[:half], mine[half:], *others]


def lanes(index, width):
    return pl.ds(pl.multiple_of(index * width, width), width)


def split_kernel(chips, rest, width, tokens_ref, *out_refs):
    for ref, order in zip(out_refs, split_order(chips, rest)):
        for i, block in enumerate(order):
            ref[:, i * width : (i + 1) * width] = tokens_ref[:, lanes(block, width)]


def own_places(rest, flip):
    place = lax.axis_index("seq")
    return [PAIR * ((place // PAIR - j + rest) % rest) + (place + flip) % PAIR for j in range(rest)]


def split_tokens(tokens, chips, rest, width):
    rows, total = tokens.shape
    half = total // PAIR
    near = half // chips
    widths = [half // CORES] * CORES + [half - near, near]
    if width % 128:
        order = jnp.stack(sum(whole_order(chips, rest), []))
        taken = jnp.take(tokens.reshape(rows, total // width, width), order, axis=1).reshape(rows, total)
        return jnp.split(taken, [half // CORES, half, total - near], axis=1)
    tile = min(rows, 128)
    return pl.pallas_call(
        functools.partial(split_kernel, chips, rest, width),
        grid=(rows // tile,),
        in_specs=[pl.BlockSpec((tile, total), lambda i: (i, 0))],
        out_specs=[pl.BlockSpec((tile, w), lambda i: (i, 0)) for w in widths],
        out_shape=[jax.ShapeDtypeStruct((rows, w), tokens.dtype) for w in widths],
        name="split_tokens",
    )(tokens)


def finish_kernel(chips, rest, width, *refs):
    part_refs, term_refs, (out_ref, sum_ref, total_ref, sems) = refs[:3], refs[3:-4], refs[-4:]
    copies = []
    for ref, order in zip(part_refs, whole_order(chips, rest)):
        for i, block in enumerate(order):
            source = ref.at[:, pl.ds(i * width, width)]
            target = out_ref.at[:, lanes(block, width)]
            copies.append(pltpu.make_async_copy(source, target, sems.at[len(copies)]))
    for copy in copies:
        copy.start()
    total = term_refs[0][...].astype(F32)
    for ref in term_refs[1:]:
        total = total + ref[...].astype(F32)
    total_ref[...] = total
    copies.append(pltpu.make_async_copy(total_ref, sum_ref, sems.at[len(copies)]))
    copies[-1].start()
    for copy in copies:
        copy.wait()


def finish(parts, terms, chips, rest, width):
    rows = parts[0].shape[0]
    total = sum(part.shape[1] for part in parts)
    count = total // width
    if width % 128:
        order = jnp.stack(sum(whole_order(chips, rest), []))
        where = jnp.zeros_like(order).at[order].set(lax.iota(order.dtype, count))
        blocks = jnp.concatenate(parts, axis=1).reshape(rows, count, width)
        summed = functools.reduce(jnp.add, [term.astype(F32) for term in terms])
        return jnp.take(blocks, where, axis=1).reshape(rows, total), summed
    return pl.pallas_call(
        functools.partial(finish_kernel, chips, rest, width),
        in_specs=[VMEM] * (len(parts) + len(terms)),
        out_specs=[pl.BlockSpec(memory_space=pl.ANY)] * 2,
        out_shape=[
            jax.ShapeDtypeStruct((rows, total), BF16),
            jax.ShapeDtypeStruct(terms[0].shape, F32),
        ],
        scratch_shapes=[pltpu.VMEM(terms[0].shape, F32), pltpu.SemaphoreType.DMA((count + 1,))],
        compiler_params=pltpu.CompilerParams(vmem_limit_bytes=20 * 2**20),
        name="finish",
    )(*parts, *terms)


def cut(parts, first, step):
    for part in parts:
        if first < part.shape[1]:
            return part[:, first : first + step]
        first -= part.shape[1]


def project_kernel(span, per, cuts, count, *refs):
    tokens, pieces, out_refs = refs[:count], refs[count : -len(cuts)], refs[-len(cuts) :]
    low, high = cuts[0][0], cuts[-1][1]
    total = None
    for g in range(len(pieces) // per):
        rows = jnp.concatenate([r[:, low:high] for r in pieces[g * per : (g + 1) * per]], axis=0)
        term = dot(cut(tokens, g * span, span), rows)
        total = term if total is None else total + term
    for (first, end), ref in zip(cuts, out_refs):
        ref[...] = total[:, first - low : end - low].astype(ref.dtype)


def project(tokens, groups, cuts, kind):
    rows = tokens[0].shape[0]
    pieces = [piece for group in groups for piece in group]
    span = sum(piece.shape[0] for piece in groups[0])
    return pl.pallas_call(
        functools.partial(project_kernel, span, len(groups[0]), cuts, len(tokens)),
        in_specs=[VMEM] * (len(tokens) + len(pieces)),
        out_specs=[VMEM] * len(cuts),
        out_shape=[jax.ShapeDtypeStruct((rows, end - first), kind) for first, end in cuts],
        compiler_params=pltpu.CompilerParams(vmem_limit_bytes=20 * 2**20),
        name="project",
    )(*tokens, *pieces)


def grad_kernel(span, counts, dquery_ref, dpair_ref, *refs):
    pieces, outs, mark_ref = refs[: -len(counts) - 1], refs[-len(counts) - 1 : -1], refs[-1]
    grads = jnp.concatenate([dquery_ref[...], dpair_ref[...]], axis=1)
    per = len(pieces) // sum(counts)
    for out_ref, count in zip(outs, counts):
        for i in range(count):
            rows = jnp.concatenate([r[...] for r in pieces[:per]], axis=0)
            pieces = pieces[per:]
            out_ref[:, i * span : (i + 1) * span] = dot(grads, rows, NT).astype(BF16)
    mark_ref[...] = grads[:16, :128]


def width_grad(dquery, dpair, parts):
    rows = dquery.shape[0]
    pieces = [piece for groups in parts for group in groups for piece in group]
    span = sum(piece.shape[0] for piece in parts[0][0])
    counts = [len(groups) for groups in parts]
    return pl.pallas_call(
        functools.partial(grad_kernel, span, counts),
        in_specs=[VMEM] * (2 + len(pieces)),
        out_specs=[VMEM] * (len(parts) + 1),
        out_shape=[jax.ShapeDtypeStruct((rows, span * count), BF16) for count in counts]
        + [jax.ShapeDtypeStruct((16, 128), BF16)],
        compiler_params=pltpu.CompilerParams(vmem_limit_bytes=20 * 2**20),
        name="width_grad",
    )(dquery, dpair, *pieces)


def weight_kernel(steps, rest, width, chips, sources, grads, *refs):
    tokens, refs = refs[: sum(sources)], refs[sum(sources) :]
    rights = [jnp.concatenate([r[...] for r in refs[i : i + grads]], axis=1) for i in range(0, grads * len(sources), grads)]
    right = jnp.concatenate(rights, axis=0)
    outs = refs[grads * len(sources) + 1 :]
    span = rest * width
    for i, k in enumerate(steps):
        left, at = [], 0
        for core, count in enumerate(sources):
            parts, at = tokens[at : at + count], at + count
            if count == 1:
                left.append(parts[0][:, k * span : (k + 1) * span])
            else:
                far, near = parts
                across = core // CORES
                first = across if k == 0 else across * (chips - 1) + k - 1
                left.append((far if k else near)[:, first * span : (first + 1) * span])
        total = dot(jnp.concatenate(left, axis=0).T, right)
        for j in range(rest):
            out = outs[i * rest + j]
            out[...] = total[j * width : (j + 1) * width].astype(out.dtype)


def weight_terms(steps, rest, width, chips, tokens, grads, after):
    cols = sum(g.shape[1] for g in grads[0])
    sources = [len(parts) for parts in tokens]
    parts = [part for group in tokens for part in group]
    given = [g for group in grads for g in group]
    return pl.pallas_call(
        functools.partial(weight_kernel, steps, rest, width, chips, sources, len(grads[0])),
        in_specs=[VMEM] * (len(parts) + len(given) + 1),
        out_specs=[VMEM] * (len(steps) * rest),
        out_shape=[jax.ShapeDtypeStruct((width, cols), BF16 if j else F32) for _ in steps for j in range(rest)],
        compiler_params=pltpu.CompilerParams(vmem_limit_bytes=20 * 2**20),
        name="weight_terms",
    )(*parts, *given, after)


def attend_kernel(heads, back, docs_ref, q_ref, q_from_ref, cot_ref, *refs):
    pair_refs, (out_ref, dq_ref, dpair_ref, dback_ref) = refs[: back + 1], refs[back + 1 :]
    rows = q_ref.shape[0]
    hd = HEAD_DIM
    scale = 1.0 / math.sqrt(hd)
    first = lax.axis_index("seq") * rows
    total = (back + 1) * rows

    row_pos = first + lax.broadcasted_iota(jnp.int32, (1, rows), 1)
    start_of = jnp.zeros((1, rows), jnp.int32)
    start = jnp.int32(0)
    for d in range(docs_ref.shape[0]):
        end = start + docs_ref[d]
        start_of = jnp.where((row_pos >= start) & (row_pos < end), start, start_of)
        start = end
    key_pos = first - back * rows + lax.broadcasted_iota(jnp.int32, (total, rows), 0)
    shut = jnp.where((key_pos >= start_of) & (key_pos <= row_pos), 0.0, -1e30)

    pairs = [r[...] for r in pair_refs]
    keys = jnp.concatenate([p[:, :hd] for p in pairs], axis=0)
    values = jnp.concatenate([p[:, hd:] for p in pairs], axis=0)
    keys_t, values_t = keys.T, values.T
    sums = [jnp.zeros((total, hd), F32), jnp.zeros((total, hd), F32)]
    cols = [slice(h * hd, (h + 1) * hd) for h in range(heads)]
    state = {}

    def products(h):
        q = (q_ref[:, cols[h]] + q_from_ref[:, cols[h]].astype(F32)).astype(BF16)
        cot = cot_ref[:, cols[h]]
        state[h] = [q, cot, dot(keys, q, NT), dot(values, cot, NT)]

    def softmax(h):
        logits = state[h][2] * (scale * math.log2(math.e)) + shut
        raised = jnp.exp2(logits - jnp.max(logits, axis=0, keepdims=True))
        probs = raised * (1.0 / jnp.sum(raised, axis=0, keepdims=True))
        state[h][2] = probs
        state[h].append(probs.astype(BF16))

    def outputs(h):
        _, cot, _, _, probs_half = state[h]
        out_t = dot(values_t, probs_half).astype(BF16)
        out_ref[:, cols[h]] = out_t.T
        state[h].append(jnp.sum(cot.T.astype(F32) * out_t.astype(F32), axis=0, keepdims=True))

    def score_grads(h):
        _, _, probs, dprobs, _, delta = state[h]
        state[h][3] = (probs * (dprobs - delta)).astype(BF16)

    def grads(h):
        q, cot, _, dscores, probs_half, _ = state.pop(h)
        dq_ref[:, cols[h]] = (dot(keys_t, dscores) * scale).astype(BF16).T
        sums[0] = sums[0] + dot(dscores, q)
        sums[1] = sums[1] + dot(probs_half, cot)

    products(0)
    for h in range(heads):
        softmax(h)
        if h + 1 < heads:
            products(h + 1)
        outputs(h)
        score_grads(h)
        if h:
            grads(h - 1)
    grads(heads - 1)
    both = jnp.concatenate([sums[0] * scale, sums[1]], axis=1)
    dpair_ref[...] = both[back * rows :]
    dback_ref[...] = both[: back * rows].astype(BF16)


def attend(docs, q, q_from, cot, pairs):
    rows, width = q.shape
    back = len(pairs) - 1
    two = 2 * HEAD_DIM
    return pl.pallas_call(
        functools.partial(attend_kernel, width // HEAD_DIM, back),
        in_specs=[SMEM] + [VMEM] * (back + 4),
        out_specs=[VMEM] * 4,
        out_shape=[
            jax.ShapeDtypeStruct((rows, width), BF16),
            jax.ShapeDtypeStruct((rows, width), BF16),
            jax.ShapeDtypeStruct((rows, two), F32),
            jax.ShapeDtypeStruct((back * rows, two), BF16),
        ],
        compiler_params=pltpu.CompilerParams(vmem_limit_bytes=20 * 2**20),
        name="attend",
    )(docs, q, q_from, cot, *pairs)


def kept_rows(doc_row, flag_row, positions):
    ends = jnp.cumsum(doc_row)
    starts = ends - doc_row
    inside = (positions[:, None] >= starts[None, :]) & (positions[:, None] < ends[None, :])
    return jnp.sum(jnp.where(inside, flag_row[None, :], 0), axis=1)


def shards(inputs, weights, cotangent, doc_lengths, kept_flags):
    seq_count = lax.axis_size("seq")
    chips = lax.axis_size("dp") // CORES
    rest = seq_count // PAIR
    place = lax.axis_index("seq")
    tokens = inputs[0]
    local = tokens.shape[0]
    qwidth = cotangent.shape[2]
    shard_rows, cols = weights.shape
    width = shard_rows // seq_count
    back = -(-(local * seq_count // 2 - 1) // local)

    own = lax.dynamic_slice_in_dim(weights, place * width, width, 0)
    mine_own, mine_across, sent, near = split_tokens(tokens, chips, rest, width)

    blocks, near = lax.optimization_barrier((weights, near))
    blocks = blocks.reshape(seq_count, width, cols)
    groups_own, groups_near = [
        [[lax.dynamic_index_in_dim(blocks, p, 0, keepdims=False) for p in own_places(rest, flip)]] for flip in range(PAIR)
    ]
    arrived = {}
    for k in sorted(range(1, chips), key=lambda k: (-abs(2 * k - chips), k)):
        first = shift_chip(own, k)
        if not arrived:
            first, sent = lax.optimization_barrier((first, sent))
        if k == chips // 2:
            first, arrived = lax.optimization_barrier((first, arrived))
        arrived[k] = [first] + [shift_rest(first, j) for j in range(1, rest)]
    far_other = swap_x(sent)
    groups_own += [arrived[k] for k in range(1, chips)]
    last = groups_own[chips // 2]
    last[-1], far_other = lax.optimization_barrier((last[-1], far_other))
    groups_across = [[swap_core(piece) for piece in group] for group in groups_own]
    groups_near.append([swap_core(piece) for piece in groups_near[0]])
    groups = groups_own + groups_across
    groups_far = groups_own[1:] + groups_across[1:]

    query_cut, pair_cut = (0, qwidth), (qwidth, cols)
    (pair_sent,) = project([far_other], groups_far, [pair_cut], BF16)
    (query_sent,) = project([far_other], groups_far, [query_cut], BF16)
    pair_from, query_from = swap_x(pair_sent), swap_x(query_sent)
    query, pair = project([mine_own, mine_across, near], groups + groups_near, [query_cut, pair_cut], F32)
    pair = (pair + pair_from.astype(F32)).astype(BF16)

    doc_row, flag_row = doc_lengths[0], kept_flags[0]
    positions = place * local + lax.iota(jnp.int32, local)
    kept = kept_rows(doc_row, flag_row, positions)
    cot = jnp.where(kept[:, None] > 0, cotangent[0], jnp.zeros_like(cotangent[0]))

    near, _ = lax.optimization_barrier((near, pair_from))
    near_other = swap_x(near)
    pairs = [shift_seq(pair, j) for j in range(back, 0, -1)] + [pair]
    attention, dquery, dpair, dback = attend(doc_row, query, query_from, cot, pairs)

    dquery_sent, near_other = lax.optimization_barrier((dquery, near_other))
    dquery_other = swap_x(dquery_sent)
    for j in range(1, back + 1):
        sent = dback[(back - j) * local : (back - j + 1) * local]
        dpair = dpair + shift_seq(sent, -j).astype(F32)
    dpair = dpair.astype(BF16)
    dpair_other = swap_x(dpair)

    left = [[mine_own], [far_other, near_other]]
    left += [[swap_core(mine_across)], [swap_core(far_other), swap_core(near_other)]]
    right = [[dquery, dpair], [dquery_other, dpair_other]]
    right += [[swap_core(g) for g in group] for group in right]
    order = sorted(range(chips), key=lambda k: (k == 0, -min(k, chips - k), k))
    parts, after = [], dpair
    for steps in (order[:1], order[1:]):
        terms = weight_terms(steps, rest, width, chips, left, right, after)
        if not parts:
            grad_sent, after = width_grad(dquery_other, dpair_other, [groups_far])
            grad_from = swap_x(grad_sent)
        for i, k in enumerate(steps):
            part, *sent = terms[i * rest : (i + 1) * rest]
            received = [shift_rest(piece, -j) for j, piece in enumerate(sent, 1)]
            if k:
                part = functools.reduce(jnp.add, [term.astype(F32) for term in received], part)
                parts.append(shift_chip(part.astype(BF16), -k))
            else:
                parts += [part, *received]

    grad_mine, grad_near, _ = width_grad(dquery, dpair, [groups, groups_near])
    inputs_grad, weights_grad = finish([grad_mine, grad_from, grad_near], parts, chips, rest, width)
    return (attention[None], inputs_grad[None], weights_grad)


def solution(mesh):
    in_specs = (
        P("dp", "seq", None),
        P("dp", None),
        P("dp", "seq", None),
        P("dp", None),
        P("dp", None),
    )
    out_specs = (P("dp", "seq", None), P("dp", "seq", None), P(("dp", "seq"), None))
    return jax.shard_map(shards, mesh=mesh, in_specs=in_specs, out_specs=out_specs, check_vma=False)
```
